32 devices in a mesh: ctx: 4 (over y, x), exp: 4 (over z), tp: 2 (over core).
Axes of the slice: x: 2, y: 2, z: 4, core: 2. Of those that a mesh axis runs over, the one named last changes fastest.
Arguments:
- hidden: bfloat16 [2048, 4, 1408], P(('ctx', 'exp'), None, 'tp'), may hold values from -6 to 6
- expert_ids: int32 [2048, 4], P(('ctx', 'exp')), may hold values from 0 to 7, all different within a row; in each aligned block of 128 rows (0 to 127, 128 to 255, ...) at most 72 rows name the same one
- gate_fix: int32 [2048, 4], P(('ctx', 'exp')), may hold values from 1024 to 65535
- grad_out: bfloat16 [2048, 2048], P(('ctx', 'exp'), 'tp'), may hold values from -6 to 6
- w_down: bfloat16 [8, 1408, 2048], P('ctx', 'tp'), may hold values from -0.15625 to 0.15625
Outputs:
- mixed: bfloat16 [2048, 2048], P(('ctx', 'exp'), 'tp')
- grad_hidden: bfloat16 [2048, 4, 1408], P(('ctx', 'exp'), None, 'tp')
The draws below stay inside these ranges and needn't reach their ends.
Inputs may be any that keep to these rules, and one draw needn't show every extreme that they name: `expert_ids`: each row names 4 different experts. Within the 128 rows of one index of ctx and exp, no expert is named by more than 72 rows, a bound that some block reaches.
All inputs are finite; a program needn't handle non-finite values.
Results may differ from the reference program's by a relative error of at most 0.013.
Values may be sent and summed in bfloat16 or wider, within the bound.
No kernel may reach another device: no remote copies, remote signals or barrier semaphores. Data moves between devices by JAX's collectives and lax.ppermute only.
A program may use at most 64 MiB of HBM per device.

```python
import math
import jax
import jax.numpy as jnp
import numpy as np
from jax import lax

D = 2048
FF = 1408
TOPK = 4
TOK_DEV = 128
EXPERTS = 8
CAP = 72
TOKENS = 2048
N_CTX = 4
N_EXP = 4
N_TP = 2


def plant(drawn, stream_key, smallest, largest):
    shape = drawn.shape
    spot = [jax.random.randint(jax.random.fold_in(stream_key, axis), (), 0, shape[axis]) for axis in range(len(shape))]
    drawn = drawn.at[tuple(spot)].set(smallest)
    longest = shape.index(max(shape))
    spot[longest] = (spot[longest] + 1) % shape[longest]
    return drawn.at[tuple(spot)].set(largest)


def block_scale(rng, shape, pieces, least, high):
    def one(axis_at, shards_of):
        draws = jax.random.uniform(jax.random.fold_in(jax.random.fold_in(rng, 6), axis_at), (shards_of,), jnp.float32, least / len(pieces), high / len(pieces))
        return jnp.repeat(jnp.exp(draws), shape[axis_at] // shards_of).reshape((-1,) + (1,) * (len(shape) - axis_at - 1))

    factor_of = one(*pieces[0])
    for cut in pieces[1:]:
        factor_of = factor_of * one(*cut)
    return factor_of


def shared_out(rng, own, number, rows, count, top, reach, skew):
    order = jax.random.permutation(rng, count)
    packed, common = load_shares(count, rows * top, reach, skew, True), load_shares(count, rows * top, reach, skew, False)
    places = jnp.arange(count)

    def named(tallies, turn):
        used = int((tallies > 0).sum())
        fixed = max(1, used // 4)
        shifted = fixed + (places - fixed + turn * (used - fixed)) % max(1, count - fixed)
        return jnp.zeros((count,), jnp.int32).at[order[jnp.where(places < fixed, places, shifted)]].set(jnp.asarray(tallies, jnp.int32))

    tallies = jnp.where(number % 4 == 0, named(packed, number // 4), named(common, number - number // 4 - 1))
    mixed = jax.random.permutation(jax.random.fold_in(own, 3), count)
    donor, sink = mixed[0:count // 2 * 2:2], mixed[1:count // 2 * 2:2]
    margin = jnp.minimum(tallies[donor] - 1, reach - tallies[sink]) // 2
    margin = jnp.where((donor == order[0]) | (sink == order[0]) | (tallies[sink] == 0), 0, jnp.maximum(margin, 0))
    shifted = jax.random.randint(jax.random.fold_in(own, 4), (count // 2,), 0, 1 << 20) % (margin + 1)
    tallies = tallies.at[donor].add(-shifted).at[sink].add(shifted)
    labels = jnp.searchsorted(jnp.cumsum(tallies), jnp.arange(rows * top), side="right").astype(jnp.int32)
    grid = labels.reshape(top, rows).T
    grid = grid[jax.random.permutation(jax.random.fold_in(own, 1), rows)]
    turn = jax.random.randint(jax.random.fold_in(own, 2), (rows, 1), 0, top)
    return jnp.take_along_axis(grid, (jnp.arange(top)[None, :] + turn) % top, axis=1)


def load_shares(amount, total, bound, lean, full):
    portions = [(1 << 20) // math.isqrt(grade ** lean) + 1 for grade in range(1, amount + 1)]
    largest = bound if full else min(bound, max(-(-total // amount), total * portions[0] // sum(portions)))
    least = 1 if total - largest >= amount - 1 else 0
    holding, spare = [largest] + [least] * (amount - 1), total - largest - least * (amount - 1)
    while spare > 0:
        movable = [i for i in range(1, amount) if holding[i] < largest] or [i for i in range(1, amount) if holding[i] < bound]
        whole, left = sum([portions[i] for i in movable]), spare
        for i in movable:
            addition = min(bound - holding[i], max(1, left * portions[i] // whole), spare)
            holding[i] = holding[i] + addition
            spare = spare - addition
    return np.array(holding)


def normal_values(stream_key, shape, scale, reach, shards=(), held_as=jnp.bfloat16):
    entries = scale * jax.random.normal(stream_key, shape, jnp.float32)
    if shards:
        entries = entries * block_scale(stream_key, shape, shards, -0.22, 0.18)
    return jnp.clip(entries, -reach, reach).astype(held_as)


def setup_inputs(seed: int = 0) -> dict:
    key_list = jax.random.split(jax.random.key(seed), 6)
    hidden = normal_values(key_list[0], (TOKENS, TOPK, FF), 1.0, 6.0, ((0, 16), (2, 2)))
    expert_ids_keys = jax.random.split(jax.random.fold_in(key_list[1], 1), TOKENS // TOK_DEV)
    expert_ids_turns = jax.random.permutation(jax.random.fold_in(key_list[1], 3), TOKENS // TOK_DEV)
    expert_ids = jax.vmap(lambda own, number: shared_out(jax.random.fold_in(key_list[1], 2), own, number, TOK_DEV, EXPERTS, TOPK, CAP, 2))(expert_ids_keys, expert_ids_turns).reshape((TOKENS, TOPK))
    gate_fix = plant(jax.random.randint(key_list[2], (TOKENS, TOPK), 1024, 65536), jax.random.fold_in(key_list[2], 1), 1024, 65535).astype(jnp.int32)
    grad_out = normal_values(key_list[3], (TOKENS, D), 1.0, 6.0, ((0, 16), (1, 2)))
    w_down = normal_values(key_list[4], (EXPERTS, FF, D), FF ** -0.5, 0.15625, ((0, 4), (1, 2)))
    return {"hidden": hidden, "expert_ids": expert_ids, "gate_fix": gate_fix, "grad_out": grad_out, "w_down": w_down}


def rounded_sum(partials):
    rounded = lax.optimization_barrier(partials.astype(jnp.bfloat16))
    return jnp.sum(rounded.astype(jnp.float32), axis=0)


def reference(hidden, expert_ids, gate_fix, grad_out, w_down):
    blocks = N_CTX * N_EXP
    per_block = TOK_DEV * TOPK
    block_width = FF // N_TP
    flat_ids = expert_ids.reshape(blocks, per_block)
    onehot = (flat_ids[:, :, None] == jnp.arange(EXPERTS, dtype=jnp.int32)[None, None, :]).astype(jnp.int32)
    before = jnp.cumsum(onehot, axis=1) - onehot
    position = jnp.sum(before * onehot, axis=2)
    target = (flat_ids * CAP + position).astype(jnp.int32)
    assign_index = jnp.arange(blocks * per_block, dtype=jnp.int32).reshape(blocks, per_block)
    block_index = jnp.arange(blocks, dtype=jnp.int32)[:, None]
    source = jnp.full((blocks, EXPERTS * CAP), blocks * per_block, jnp.int32).at[block_index, target].set(assign_index)
    source_by_expert = source.reshape(blocks, EXPERTS, CAP).transpose(1, 0, 2)
    gate_val = gate_fix.astype(jnp.float32) * (1.0 / 65536.0)
    gate_flat = gate_val.reshape(TOKENS * TOPK)
    hidden_flat = hidden.reshape(TOKENS * TOPK, FF)
    scaled = (gate_val[:, :, None] * grad_out[:, None, :].astype(jnp.float32)).astype(jnp.bfloat16)
    scaled = scaled.reshape(TOKENS * TOPK, D)

    def expert_step(carry, operands):
        mixed_sum, grad_rows = carry
        src, down_w = operands
        flat_src = src.reshape(blocks * CAP).astype(jnp.int32)
        h_rows = jnp.take(hidden_flat, flat_src, axis=0, mode="fill", fill_value=0)
        dy_rows = jnp.take(scaled, flat_src, axis=0, mode="fill", fill_value=0)
        gate_rows = jnp.take(gate_flat, flat_src, axis=0, mode="fill", fill_value=0)
        hid_blocks = h_rows.astype(jnp.float32).reshape(-1, N_TP, block_width)
        down_blocks = down_w.astype(jnp.float32).reshape(N_TP, block_width, D)
        part_y = jnp.einsum("rth,thd->trd", hid_blocks, down_blocks)
        y_rows = rounded_sum(part_y).astype(jnp.bfloat16)
        d_rows = jnp.dot(dy_rows, down_w.T, preferred_element_type=jnp.float32).astype(jnp.bfloat16)
        token_index = (flat_src // TOPK).astype(jnp.int32)
        mixed_sum = mixed_sum.at[token_index].add(gate_rows[:, None] * y_rows.astype(jnp.float32), mode="drop")
        grad_rows = grad_rows.at[flat_src].set(d_rows, mode="drop")
        return (mixed_sum, grad_rows), None

    start = (jnp.zeros((TOKENS, D), jnp.float32), jnp.zeros((TOKENS * TOPK, FF), jnp.bfloat16))
    (mixed_sum, grad_rows), unused = lax.scan(expert_step, start, (source_by_expert, w_down))
    return mixed_sum.astype(jnp.bfloat16), grad_rows.reshape(TOKENS, TOPK, FF)
```

```python
import functools

import jax
import jax.numpy as jnp
from jax import lax
from jax.experimental import pallas as pl
from jax.experimental.pallas import tpu as pltpu
from jax.sharding import PartitionSpec as P

BF16 = jnp.bfloat16
F32 = jnp.float32
NN = (((1,), (0,)), ((), ()))
NT = (((1,), (1,)), ((), ()))
TN = (((0,), (0,)), ((), ()))
GRANT = 40 * 1024 * 1024


def dot(a, b, dims):
    return lax.dot_general(a, b, dims, preferred_element_type=F32)


def iota(shape, axis):
    return lax.broadcasted_iota(jnp.int32, shape, axis)


def ones_where(mask):
    return mask.astype(F32).astype(BF16)


def earlier(tokens):
    return ones_where(iota((tokens, tokens), 0) < iota((tokens, tokens), 1))


def token_slots(ids, me, experts, local, cap, width):
    top, tokens = ids.shape
    row = iota((experts, tokens), 0)
    hits = [ids[k : k + 1, :] == row for k in range(top)]
    named = functools.reduce(jnp.logical_or, hits)
    before = dot(ones_where(named), earlier(tokens), NN)
    base = jnp.bitwise_xor(row // local, me) * width + lax.rem(row, local) * cap
    slot = before + base.astype(F32)
    return [
        jnp.sum(jnp.where(hit, slot, 0.0), axis=0, keepdims=True).astype(jnp.int32)
        for hit in hits
    ]


def named_here(ids, me, local):
    top, tokens = ids.shape
    row = iota((8, tokens), 0) + me * local
    return functools.reduce(
        jnp.logical_or, [ids[k : k + 1, :] == row for k in range(top)]
    )


def slots_by_lane(ids, me, local, cap, width):
    tokens = ids.shape[1]
    named = named_here(ids, me, local)
    before = dot(ones_where(named), earlier(tokens), NN)
    slot = before.astype(jnp.int32) + iota((8, tokens), 0) * cap
    slot = jnp.where(named, slot, -1)
    rows = iota((width, tokens), 0)
    return [ones_where(rows == slot[l : l + 1, :]) for l in range(local)]


def slots_by_row(ids, me, local, cap, width):
    tokens = ids.shape[1]
    named = ones_where(named_here(ids, me, local))
    later = ones_where(iota((tokens, tokens), 1) < iota((tokens, tokens), 0))
    same = ones_where(iota((tokens, tokens), 1) == iota((tokens, tokens), 0))
    before = dot(later, named, NT)
    present = dot(same, named, NT)
    slot = before + (iota((tokens, 8), 1) * cap).astype(F32)
    slot = jnp.where(present > 0.5, slot, -1.0).astype(jnp.int32)
    lanes = iota((tokens, width), 1)
    return [ones_where(lanes == slot[:, l : l + 1]) for l in range(local)]


def dispatch_kernel(dims, place, ids_ref, gate_ref, hid_ref, *outs):
    experts, local, cap, width = dims
    top = ids_ref.shape[0]
    slots = token_slots(ids_ref[...], place[0], experts, local, cap, width)
    gate = gate_ref[...].astype(F32) * (1.0 / 65536.0)
    scaled = [
        (hid_ref[k].astype(F32) * gate[k : k + 1, :]).astype(BF16) for k in range(top)
    ]
    rows = iota((len(outs) * width, ids_ref.shape[1]), 0)
    picks = [ones_where(rows == slots[k]) for k in range(top)]
    sent = dot(jnp.concatenate(picks, axis=1), jnp.concatenate(scaled, axis=1), NT)
    for s, out in enumerate(outs):
        out[...] = sent[s * width : (s + 1) * width].astype(BF16)


def grad_kernel(dims, count, place, *refs):
    experts, local, cap, width = dims
    ids = refs[:count]
    own = refs[count : 2 * count]
    other = refs[2 * count : 3 * count]
    w_hbm = refs[3 * count]
    outs = refs[3 * count + 1 : 4 * count + 1]
    w_ref, dy_ref, grad_ref, sems = refs[4 * count + 1 :]
    pieces = sems.shape[1]
    step = w_ref.shape[1] // pieces
    half = own[0].shape[1]
    tokens = own[0].shape[0]

    def piece(l, i):
        at = pl.ds(i * step, step)
        return pltpu.make_async_copy(w_hbm.at[l, at], w_ref.at[l, at], sems.at[l, i])

    for l in range(local):
        for i in range(pieces):
            piece(l, i).start()
    mine = pl.ds(pl.multiple_of(place[1] * half, half), half)
    sibling = pl.ds(pl.multiple_of((1 - place[1]) * half, half), half)
    for s in range(count):
        at = pl.ds(s * tokens, tokens)
        dy_ref[at, mine] = own[s][...]
        dy_ref[at, sibling] = other[s][...]
    for l in range(local):
        for i in range(pieces):
            piece(l, i).wait()
            at = pl.ds(i * step, step)
            grad_ref[l, at, :] = dot(w_ref[l, at, :], dy_ref[...], NT).astype(BF16)
    for s in range(count):
        held = slots_by_lane(ids[s][...], place[0], local, cap, width)
        at = pl.ds(s * tokens, tokens)
        grads = [grad_ref[l, :, at] for l in range(local)]
        outs[s][...] = dot(
            jnp.concatenate(held, axis=1), jnp.concatenate(grads, axis=1), NT
        ).astype(BF16)


def mix_kernel(dims, count, add, sibling, place, *refs):
    experts, local, cap, width = dims
    ids = refs[:count]
    hid = refs[count : 2 * count]
    at = 2 * count
    arrived = ()
    if add:
        arrived = refs[at : at + count]
        at += count
    w_hbm = refs[at]
    outs = refs[at + 1 : at + 1 + count]
    w_ref, x_ref, sems = refs[at + 1 + count :]
    pieces = sems.shape[0]
    half = outs[0].shape[1]
    step = half // pieces
    tokens = outs[0].shape[0]
    ff = w_ref.shape[1]
    side = 1 - place[1] if sibling else place[1]

    def piece(i):
        source = pl.ds(pl.multiple_of(side * half + i * step, step), step)
        return pltpu.make_async_copy(
            w_hbm.at[:, :, source], w_ref.at[:, :, pl.ds(i * step, step)], sems.at[i]
        )

    for i in range(pieces):
        piece(i).start()
    for s in range(count):
        held = slots_by_row(ids[s][...], place[0], local, cap, width)
        for l in range(local):
            x_ref[l, pl.ds(s * tokens, tokens), :] = dot(held[l], hid[s][...], NN).astype(BF16)
    for i in range(pieces):
        piece(i).wait()
        columns = pl.ds(i * step, step)
        total = dot(x_ref[0], w_ref[0, :, columns], NN)
        for l in range(1, local):
            total += dot(x_ref[l], w_ref[l, :, columns], NN)
        for s in range(count):
            part = total[s * tokens : (s + 1) * tokens]
            if add:
                part = part + arrived[s][:, columns].astype(F32)
            outs[s][:, columns] = part.astype(BF16)


def restore_kernel(dims, count, place, ids_ref, gate_ref, *refs):
    experts, local, cap, width = dims
    slots_refs, out = refs[:count], refs[count]
    top, tokens = ids_ref.shape
    slots = token_slots(ids_ref[...], place[0], experts, local, cap, width)
    gate = gate_ref[...].astype(F32) * (1.0 / 65536.0)
    rows = iota((count * width, tokens), 0)
    picks = jnp.concatenate([ones_where(rows == slots[k]) for k in range(top)], axis=1)
    back = jnp.concatenate([ref[...] for ref in slots_refs], axis=0)
    grads = dot(back, picks, TN)
    for k in range(top):
        out[k] = (grads[:, k * tokens : (k + 1) * tokens] * gate[k : k + 1, :]).astype(BF16)


def call(kernel, outs, args, anywhere=(), scratch=(), flops=0, name=None):
    specs = [pl.BlockSpec(memory_space=pltpu.SMEM)]
    for i in range(1, len(args)):
        specs.append(pl.BlockSpec(memory_space=pl.ANY if i in anywhere else pltpu.VMEM))
    moved = sum(a.size * a.dtype.itemsize for a in list(args) + list(outs))
    return pl.pallas_call(
        kernel,
        out_shape=outs,
        in_specs=specs,
        out_specs=[pl.BlockSpec(memory_space=pltpu.VMEM)] * len(outs),
        scratch_shapes=scratch,
        compiler_params=pltpu.CompilerParams(vmem_limit_bytes=GRANT),
        cost_estimate=pl.CostEstimate(flops=flops, bytes_accessed=moved, transcendentals=0),
        name=name,
    )(*args)


def body(hidden, expert_ids, gate_fix, grad_out, w_down):
    tokens, top, ff = hidden.shape
    half = grad_out.shape[1]
    local, _, full = w_down.shape
    n = lax.axis_size("ctx")
    experts = n * local
    assigned = tokens * top
    cap = min(tokens, assigned // experts + max(1, assigned // (8 * experts)))
    width = -(-local * cap // 16) * 16
    dims = (experts, local, cap, width)
    group = min(n, 4)
    place = jnp.stack([lax.axis_index("ctx"), lax.axis_index("tp")]).astype(jnp.int32)

    def send(x, s):
        return lax.ppermute(x, "ctx", [(i, i ^ s) for i in range(n)]) if s else x

    def swap(x):
        return lax.ppermute(x, "tp", [(0, 1), (1, 0)])

    ids = expert_ids.T
    gate = gate_fix.T
    hid_t = hidden.transpose(1, 2, 0)
    ids_from = [send(ids, s) for s in range(n)]
    own = [send(grad_out, s) for s in range(n)]
    slot = jax.ShapeDtypeStruct((width, ff), BF16)
    hid_sent = call(
        functools.partial(dispatch_kernel, dims), [slot] * n, [place, ids, gate, hid_t],
        flops=2 * n * width * assigned * ff, name="dispatch",
    )
    hid_from = [send(hid_sent[s], s) for s in range(n)]
    other = [swap(x) for x in own]

    grad_from = []
    for g in range(0, n, group):
        them = slice(g, g + group)
        sent = call(
            functools.partial(grad_kernel, dims, group), [slot] * group,
            [place, *ids_from[them], *own[them], *other[them], w_down],
            anywhere=(3 * group + 1,),
            scratch=[
                pltpu.VMEM(w_down.shape, BF16),
                pltpu.VMEM((group * tokens, full), BF16),
                pltpu.VMEM((local, ff, group * tokens), BF16),
                pltpu.SemaphoreType.DMA((local, 4)),
            ],
            flops=2 * group * tokens * local * ff * full, name="grad",
        )
        grad_from += [send(sent[s], g + s) for s in range(group)]

    block = jax.ShapeDtypeStruct((tokens, half), BF16)
    out_from = []
    for g in range(0, n, group):
        them = slice(g, g + group)
        scratch = [
            pltpu.VMEM((local, ff, half), BF16),
            pltpu.VMEM((local, group * tokens, ff), BF16),
            pltpu.SemaphoreType.DMA((4,)),
        ]
        flops = 2 * group * tokens * local * ff * half
        theirs = call(
            functools.partial(mix_kernel, dims, group, False, True), [block] * group,
            [place, *ids_from[them], *hid_from[them], w_down],
            anywhere=(2 * group + 1,), scratch=scratch, flops=flops, name="mix_sibling",
        )
        arrived = [swap(x) for x in theirs]
        mine = call(
            functools.partial(mix_kernel, dims, group, True, False), [block] * group,
            [place, *ids_from[them], *hid_from[them], *arrived, w_down],
            anywhere=(3 * group + 1,), scratch=scratch, flops=flops, name="mix_own",
        )
        out_from += [send(mine[s], g + s) for s in range(group)]

    (grad_t,) = call(
        functools.partial(restore_kernel, dims, n),
        [jax.ShapeDtypeStruct((top, ff, tokens), BF16)],
        [place, ids, gate, *grad_from],
        flops=2 * n * width * assigned * ff, name="restore",
    )
    mixed = sum(x.astype(F32) for x in out_from).astype(BF16)
    return mixed, grad_t.transpose(2, 0, 1)


def solution(mesh):
    placed = (
        P(("ctx", "exp"), None, "tp"),
        P(("ctx", "exp"), None),
        P(("ctx", "exp"), None),
        P(("ctx", "exp"), "tp"),
        P("ctx", "tp", None),
    )
    return jax.shard_map(
        body,
        mesh=mesh,
        in_specs=placed,
        out_specs=(P(("ctx", "exp"), "tp"), P(("ctx", "exp"), None, "tp")),
        check_vma=False,
    )
```

```python
import functools

import jax
import jax.numpy as jnp
from jax import lax
from jax.experimental import pallas as pl
from jax.experimental.pallas import tpu as pltpu
from jax.sharding import PartitionSpec as P

BF16 = jnp.bfloat16
F32 = jnp.float32
NN = (((1,), (0,)), ((), ()))
NT = (((1,), (1,)), ((), ()))
TN = (((0,), (0,)), ((), ()))
GRANT = 24 * 1024 * 1024


def dot(a, b, dims):
    return lax.dot_general(a, b, dims, preferred_element_type=F32)


def iota(shape, axis):
    return lax.broadcasted_iota(jnp.int32, shape, axis)


def ones_where(mask):
    return mask.astype(F32).astype(BF16)


def earlier(tokens):
    return ones_where(iota((tokens, tokens), 0) < iota((tokens, tokens), 1))


def token_slots(ids, me, experts, local, cap, width):
    top, tokens = ids.shape
    row = iota((experts, tokens), 0)
    hits = [ids[k : k + 1, :] == row for k in range(top)]
    named = functools.reduce(jnp.logical_or, hits)
    before = dot(ones_where(named), earlier(tokens), NN)
    base = jnp.bitwise_xor(row // local, me) * width + lax.rem(row, local) * cap
    slot = before + base.astype(F32)
    return [
        jnp.sum(jnp.where(hit, slot, 0.0), axis=0, keepdims=True).astype(jnp.int32)
        for hit in hits
    ]


def named_here(ids, me, local):
    top, tokens = ids.shape
    row = iota((8, tokens), 0) + me * local
    return functools.reduce(
        jnp.logical_or, [ids[k : k + 1, :] == row for k in range(top)]
    )


def slots_by_lane(ids, me, local, cap, width):
    tokens = ids.shape[1]
    named = named_here(ids, me, local)
    before = dot(ones_where(named), earlier(tokens), NN)
    slot = before.astype(jnp.int32) + iota((8, tokens), 0) * cap
    slot = jnp.where(named, slot, -1)
    rows = iota((cap, tokens), 0)
    return [ones_where(rows + l * cap == slot[l : l + 1, :]) for l in range(local)]


def slots_by_row(ids, me, local, cap, width):
    tokens = ids.shape[1]
    named = ones_where(named_here(ids, me, local))
    later = ones_where(iota((tokens, tokens), 1) < iota((tokens, tokens), 0))
    same = ones_where(iota((tokens, tokens), 1) == iota((tokens, tokens), 0))
    before = dot(later, named, NT)
    present = dot(same, named, NT)
    slot = before + (iota((tokens, 8), 1) * cap).astype(F32)
    slot = jnp.where(present > 0.5, slot, -1.0).astype(jnp.int32)
    lanes = iota((tokens, width), 1)
    return [ones_where(lanes == slot[:, l : l + 1]) for l in range(local)]


def pack_kernel(ids_ref, dy_ref, out):
    tokens, half = dy_ref.shape
    top = ids_ref.shape[0]
    out[:tokens, :] = dy_ref[...]
    rows = jnp.concatenate(
        [ids_ref[...].astype(F32), jnp.zeros((8 - top, tokens), F32)], axis=0
    )
    rest = jnp.zeros((8, half - tokens), F32)
    out[tokens:, :] = jnp.concatenate([rows, rest], axis=1).astype(BF16)


def dispatch_kernel(dims, place, ids_ref, gate_ref, hid_ref, *outs):
    experts, local, cap, width = dims
    top = ids_ref.shape[0]
    slots = token_slots(ids_ref[...], place[0], experts, local, cap, width)
    gate = gate_ref[...].astype(F32) * (1.0 / 65536.0)
    scaled = [
        (hid_ref[k].astype(F32) * gate[k : k + 1, :]).astype(BF16) for k in range(top)
    ]
    rows = iota((len(outs) * width, ids_ref.shape[1]), 0)
    picks = [ones_where(rows == slots[k]) for k in range(top)]
    sent = dot(jnp.concatenate(picks, axis=1), jnp.concatenate(scaled, axis=1), NT)
    for s, out in enumerate(outs):
        out[...] = sent[s * width : (s + 1) * width].astype(BF16)


def by_expert(rows, local, cap):
    return [
        jnp.concatenate([r[l * cap : (l + 1) * cap] for r in rows], axis=0)
        for l in range(local)
    ]


def by_source(rows, count, cap):
    return [
        jnp.concatenate([r[s * cap : (s + 1) * cap] for r in rows], axis=0)
        for s in range(count)
    ]


def grad_kernel(dims, top, count, place, *refs):
    experts, local, cap, width = dims
    own = refs[:count]
    other = refs[count : 2 * count]
    w_ref = refs[2 * count]
    outs = refs[2 * count + 1 : 3 * count + 1]
    held_ref, x_ref = refs[3 * count + 1 :]
    half = own[0].shape[1]
    tokens = held_ref.shape[0] // count
    chunk = min(half, 512)
    held = []
    for s in range(count):
        ids = own[s][tokens:, :tokens].astype(F32).astype(jnp.int32)[:top]
        held.append(
            jnp.concatenate(slots_by_lane(ids, place[0], local, cap, width), axis=0)
        )
        held_ref[pl.ds(s * tokens, tokens), :] = sum(
            slots_by_row(ids, place[0], local, cap, width)
        )
    for side, halves in ((place[1], own), (1 - place[1], other)):
        for c in range(0, half, chunk):
            rows = [
                dot(held[s], halves[s][:tokens, c : c + chunk], NN) for s in range(count)
            ]
            at = pl.ds(pl.multiple_of(side * half + c, chunk), chunk)
            for l, x in enumerate(by_expert(rows, local, cap)):
                x_ref[l, :, at] = x.astype(BF16)
    grads = [dot(x_ref[l], w_ref[l], NT) for l in range(local)]
    for s, rows in enumerate(by_source(grads, count, cap)):
        outs[s][...] = rows.astype(BF16)


def mix_kernel(dims, count, sibling, place, *refs):
    experts, local, cap, width = dims
    hid = refs[:count]
    held_ref, w_ref, out = refs[count:]
    half = out.shape[1]
    tokens = out.shape[0] // count
    chunk = min(half, 256)
    side = 1 - place[1] if sibling else place[1]
    x = [r.astype(BF16) for r in by_expert([h[...].astype(F32) for h in hid], local, cap)]
    for c in range(0, half, chunk):
        at = pl.ds(pl.multiple_of(side * half + c, chunk), chunk)
        products = [dot(x[l], w_ref[l, :, at], NN) for l in range(local)]
        for s, rows in enumerate(by_source(products, count, cap)):
            tok = pl.ds(s * tokens, tokens)
            part = dot(held_ref[tok, :], rows.astype(BF16), NN)
            out[tok, c : c + chunk] = part.astype(out.dtype)


def add_kernel(own, arrived, *outs):
    tokens = outs[0].shape[0]
    for s, out in enumerate(outs):
        at = pl.ds(s * tokens, tokens)
        out[...] = (own[at, :] + arrived[at, :].astype(F32)).astype(BF16)


def restore_kernel(dims, count, place, ids_ref, gate_ref, *refs):
    experts, local, cap, width = dims
    slots_refs, out = refs[:count], refs[count]
    top, tokens = ids_ref.shape
    slots = token_slots(ids_ref[...], place[0], experts, local, cap, width)
    gate = gate_ref[...].astype(F32) * (1.0 / 65536.0)
    rows = iota((count * width, tokens), 0)
    picks = jnp.concatenate([ones_where(rows == slots[k]) for k in range(top)], axis=1)
    back = jnp.concatenate([ref[...] for ref in slots_refs], axis=0)
    grads = dot(back, picks, TN)
    for k in range(top):
        out[k] = (grads[:, k * tokens : (k + 1) * tokens] * gate[k : k + 1, :]).astype(BF16)


def call(kernel, outs, args, where=(), scratch=(), name=None):
    where = dict(where)
    return pl.pallas_call(
        kernel,
        out_shape=outs,
        in_specs=[
            pl.BlockSpec(memory_space=where.get(i, pltpu.VMEM)) for i in range(len(args))
        ],
        out_specs=[pl.BlockSpec(memory_space=pltpu.VMEM)] * len(outs),
        scratch_shapes=scratch,
        compiler_params=pltpu.CompilerParams(vmem_limit_bytes=GRANT),
        cost_estimate=pl.CostEstimate(flops=1, bytes_accessed=1, transcendentals=0),
        name=name,
    )(*args)


def body(hidden, expert_ids, gate_fix, grad_out, w_down):
    tokens, top, ff = hidden.shape
    half = grad_out.shape[1]
    local, _, full = w_down.shape
    n = lax.axis_size("ctx")
    experts = n * local
    assigned = tokens * top
    cap = min(tokens, assigned // experts + max(1, assigned // (8 * experts)))
    unit = 8 if local % 2 == 0 else 16
    cap = -(-cap // unit) * unit
    width = local * cap
    dims = (experts, local, cap, width)
    group = min(n, 4)
    place = jnp.stack([lax.axis_index("ctx"), lax.axis_index("tp")]).astype(jnp.int32)
    placed = {0: pltpu.SMEM}

    def send(x, s):
        return lax.ppermute(x, "ctx", [(i, i ^ s) for i in range(n)]) if s else x

    def swap(x):
        return lax.ppermute(x, "tp", [(0, 1), (1, 0)])

    ids = expert_ids.T
    gate = gate_fix.T
    hid_t = hidden.transpose(1, 2, 0)
    (packed,) = call(
        pack_kernel, [jax.ShapeDtypeStruct((tokens + 8, half), BF16)], [ids, grad_out],
        name="pack",
    )
    own = [send(packed, s) for s in range(n)]
    swapped = swap(packed)
    ids, swapped = lax.optimization_barrier((ids, swapped))
    slot = jax.ShapeDtypeStruct((width, ff), BF16)
    hid_sent = call(
        functools.partial(dispatch_kernel, dims), [slot] * n, [place, ids, gate, hid_t],
        where=placed, name="dispatch",
    )
    hid_from = [send(hid_sent[s], s) for s in range(n)]
    for s in range(1, n):
        own[s], hid_from[0] = lax.optimization_barrier((own[s], hid_from[0]))
    other = [swapped] + [swap(x) for x in own[1:]]

    grad_from, held = [], []
    for g in range(0, n, group):
        them = slice(g, g + group)
        *sent, rows = call(
            functools.partial(grad_kernel, dims, top, group),
            [slot] * group + [jax.ShapeDtypeStruct((group * tokens, width), BF16)],
            [place, *own[them], *other[them], w_down], where=placed,
            scratch=[pltpu.VMEM((local, group * cap, full), BF16)],
            name="grad",
        )
        held.append(rows)
        grad_from += [send(sent[s], g + s) for s in range(group)]

    out_from = []
    for g in range(0, n, group):
        rows = held[g // group]
        hid = hid_from[g : g + group]
        (theirs,) = call(
            functools.partial(mix_kernel, dims, group, True),
            [jax.ShapeDtypeStruct((group * tokens, half), BF16)],
            [place, *hid, rows, w_down], where=placed, name="mix_sibling",
        )
        arrived = swap(theirs)
        (mine,) = call(
            functools.partial(mix_kernel, dims, group, False),
            [jax.ShapeDtypeStruct((group * tokens, half), F32)],
            [place, *hid, rows, w_down], where=placed, name="mix_own",
        )
        sums = call(
            add_kernel, [jax.ShapeDtypeStruct((tokens, half), BF16)] * group,
            [mine, arrived], name="add",
        )
        out_from += [send(sums[s], g + s) for s in range(group)]

    (grad_t,) = call(
        functools.partial(restore_kernel, dims, n),
        [jax.ShapeDtypeStruct((top, ff, tokens), BF16)],
        [place, ids, gate, *grad_from], where=placed,
        name="restore",
    )
    mixed = sum(x.astype(F32) for x in out_from).astype(BF16)
    return mixed, grad_t.transpose(2, 0, 1)


def solution(mesh):
    placed = (
        P(("ctx", "exp"), None, "tp"),
        P(("ctx", "exp"), None),
        P(("ctx", "exp"), None),
        P(("ctx", "exp"), "tp"),
        P("ctx", "tp", None),
    )
    return jax.shard_map(
        body,
        mesh=mesh,
        in_specs=placed,
        out_specs=(P(("ctx", "exp"), "tp"), P(("ctx", "exp"), None, "tp")),
        check_vma=False,
    )
```

```python
import functools

import jax
import jax.numpy as jnp
from jax import lax
from jax.experimental import pallas as pl
from jax.experimental.pallas import tpu as pltpu
from jax.sharding import PartitionSpec as P

BF16 = jnp.bfloat16
F32 = jnp.float32
NN = (((1,), (0,)), ((), ()))
NT = (((1,), (1,)), ((), ()))
TN = (((0,), (0,)), ((), ()))


def dot(a, b, dims):
    return lax.dot_general(a, b, dims, preferred_element_type=F32)


def iota(shape, axis):
    return lax.broadcasted_iota(jnp.int32, shape, axis)


def ones_where(mask):
    return mask.astype(F32).astype(BF16)


def earlier(tokens):
    return ones_where(iota((tokens, tokens), 0) < iota((tokens, tokens), 1))


def token_slots(ids, experts, local, cap, width):
    top, tokens = ids.shape
    row = iota((experts, tokens), 0)
    hits = [ids[k : k + 1, :] == row for k in range(top)]
    named = functools.reduce(jnp.logical_or, hits)
    before = dot(ones_where(named), earlier(tokens), NN)
    base = row // local * width + lax.rem(row, local) * cap
    slot = before + base.astype(F32)
    return [
        jnp.sum(jnp.where(hit, slot, 0.0), axis=0, keepdims=True).astype(jnp.int32)
        for hit in hits
    ]


def named_here(ids, me, local):
    top, tokens = ids.shape
    row = iota((8, tokens), 0) + me * local
    return functools.reduce(
        jnp.logical_or, [ids[k : k + 1, :] == row for k in range(top)]
    )


def slots_by_lane(ids, me, local, cap, width):
    tokens = ids.shape[1]
    named = named_here(ids, me, local)
    before = dot(ones_where(named), earlier(tokens), NN)
    slot = before.astype(jnp.int32) + iota((8, tokens), 0) * cap
    slot = jnp.where(named, slot, -1)
    rows = iota((cap, tokens), 0)
    return [ones_where(rows + l * cap == slot[l : l + 1, :]) for l in range(local)]


def slots_by_row(ids, me, local, cap, width):
    tokens = ids.shape[1]
    named = ones_where(named_here(ids, me, local))
    later = ones_where(iota((tokens, tokens), 1) < iota((tokens, tokens), 0))
    same = ones_where(iota((tokens, tokens), 1) == iota((tokens, tokens), 0))
    before = dot(later, named, NT)
    present = dot(same, named, NT)
    slot = before + (iota((tokens, 8), 1) * cap).astype(F32)
    slot = jnp.where(present > 0.5, slot, -1.0).astype(jnp.int32)
    lanes = iota((tokens, width), 1)
    return [ones_where(lanes == slot[:, l : l + 1]) for l in range(local)]


def picks_of(meta, dims):
    experts, local, cap, width = dims
    top = meta.shape[0] // 2
    slots = token_slots(meta[:top], experts, local, cap, width)
    rows = iota((experts // local * width, meta.shape[1]), 0)
    picks = jnp.concatenate([ones_where(rows == slot) for slot in slots], axis=1)
    return picks, meta[top:].astype(F32) * (1.0 / 65536.0)


def dispatch_kernel(dims, meta_ref, hid_ref, out):
    n, width, _ = out.shape
    picks, gate = picks_of(meta_ref[...], dims)
    scaled = [
        (hid_ref[k].astype(F32) * gate[k : k + 1, :]).astype(BF16)
        for k in range(hid_ref.shape[0])
    ]
    sent = dot(picks, jnp.concatenate(scaled, axis=1), NT)
    for s in range(n):
        out[s] = sent[s * width : (s + 1) * width].astype(BF16)


def by_expert(rows, local, cap):
    return [
        jnp.concatenate([r[l * cap : (l + 1) * cap] for r in rows], axis=0)
        for l in range(local)
    ]


def by_source(rows, count, cap):
    return [
        jnp.concatenate([r[s * cap : (s + 1) * cap] for r in rows], axis=0)
        for s in range(count)
    ]


def grad_kernel(dims, top, place, *refs):
    experts, local, cap, width = dims
    n = experts // local
    own, other = refs[:n], refs[n : 2 * n]
    w_ref, out, held_ref, x_ref = refs[2 * n :]
    half = own[0].shape[1]
    tokens = held_ref.shape[0] // n
    chunk = min(half, 512)
    held = []
    for s in range(n):
        ids = own[s][tokens:, :tokens].astype(F32).astype(jnp.int32)[:top]
        held.append(
            jnp.concatenate(slots_by_lane(ids, place[0], local, cap, width), axis=0)
        )
        held_ref[pl.ds(s * tokens, tokens), :] = sum(
            slots_by_row(ids, place[0], local, cap, width)
        )
    for side, halves in ((place[1], own), (1 - place[1], other)):
        for c in range(0, half, chunk):
            rows = [dot(held[s], halves[s][:tokens, c : c + chunk], NN) for s in range(n)]
            at = pl.ds(pl.multiple_of(side * half + c, chunk), chunk)
            for l, x in enumerate(by_expert(rows, local, cap)):
                x_ref[l, :, at] = x.astype(BF16)
    grads = [dot(x_ref[l], w_ref[l], NT) for l in range(local)]
    for s, rows in enumerate(by_source(grads, n, cap)):
        out[jnp.bitwise_xor(place[0], s)] = rows.astype(BF16)


def mix_rows(dims, side, me, hid, held_ref, w_ref, half, store):
    experts, local, cap, width = dims
    n = experts // local
    tokens = held_ref.shape[0] // n
    chunk = min(half, 256)
    rows = [hid[jnp.bitwise_xor(me, s)].astype(F32) for s in range(n)]
    x = [r.astype(BF16) for r in by_expert(rows, local, cap)]
    for c in range(0, half, chunk):
        at = pl.ds(pl.multiple_of(side * half + c, chunk), chunk)
        products = [dot(x[l], w_ref[l, :, at], NN) for l in range(local)]
        for s, rows in enumerate(by_source(products, n, cap)):
            held = held_ref[pl.ds(s * tokens, tokens), :]
            store(s, slice(c, c + chunk), dot(held, rows.astype(BF16), NN))


def mix_kernel(dims, sibling, place, hid, held_ref, w_ref, out):
    tokens = held_ref.shape[0] // hid.shape[0]

    def store(s, columns, part):
        out[pl.ds(s * tokens, tokens), columns] = part.astype(out.dtype)

    side = 1 - place[1] if sibling else place[1]
    mix_rows(dims, side, place[0], hid, held_ref, w_ref, out.shape[1], store)


def mix_add_kernel(dims, place, hid, held_ref, w_ref, arrived, *outs):
    tokens, half = outs[0].shape

    def store(s, columns, part):
        theirs = arrived[pl.ds(s * tokens, tokens), columns].astype(F32)
        outs[s][:, columns] = (part + theirs).astype(BF16)

    mix_rows(dims, place[1], place[0], hid, held_ref, w_ref, half, store)


def add_split_kernel(own, arrived, mine, one, two, low, high):
    tokens, half = mine.shape
    cut = half // 2
    for s, out in enumerate((mine, one, two)):
        at = pl.ds(s * tokens, tokens)
        out[...] = own[at, :] + arrived[at, :].astype(F32)
    at = pl.ds(3 * tokens, tokens)
    far = own[at, :] + arrived[at, :].astype(F32)
    low[...] = far[:, :cut].astype(BF16)
    high[...] = far[:, cut:].astype(BF16)


def join_kernel(one, two, low, high, to_one, to_two):
    cut = one.shape[1] // 2
    to_one[:, :cut] = one[:, :cut].astype(BF16)
    to_one[:, cut:] = (one[:, cut:] + high[...].astype(F32)).astype(BF16)
    to_two[:, :cut] = (two[:, :cut] + low[...].astype(F32)).astype(BF16)
    to_two[:, cut:] = two[:, cut:].astype(BF16)


def restore_kernel(dims, meta_ref, back_ref, out):
    n, width, ff = back_ref.shape
    top, _, tokens = out.shape
    picks, gate = picks_of(meta_ref[...], dims)
    back = jnp.concatenate([back_ref[s] for s in range(n)], axis=0)
    grads = dot(back, picks, TN)
    for k in range(top):
        out[k] = (grads[:, k * tokens : (k + 1) * tokens] * gate[k : k + 1, :]).astype(BF16)


def shaped(shape, dtype=BF16):
    return jax.ShapeDtypeStruct(shape, dtype)


def call(kernel, outs, args, where=(), scratch=(), grant=24, name=None):
    where = dict(where)
    return pl.pallas_call(
        kernel,
        out_shape=outs,
        in_specs=[
            pl.BlockSpec(memory_space=where.get(i, pltpu.VMEM)) for i in range(len(args))
        ],
        out_specs=[pl.BlockSpec(memory_space=pltpu.VMEM)] * len(outs),
        scratch_shapes=scratch,
        compiler_params=pltpu.CompilerParams(vmem_limit_bytes=grant * 1024 * 1024),
        cost_estimate=pl.CostEstimate(flops=1, bytes_accessed=1, transcendentals=0),
        name=name,
    )(*args)


def body(hidden, expert_ids, gate_fix, grad_out, w_down):
    tokens, top, ff = hidden.shape
    half = grad_out.shape[1]
    local, _, full = w_down.shape
    n = lax.axis_size("ctx")
    experts = n * local
    assigned = tokens * top
    cap = min(tokens, assigned // experts + max(1, assigned // (8 * experts)))
    unit = 8 if local % 2 == 0 else 16
    cap = -(-cap // unit) * unit
    width = local * cap
    dims = (experts, local, cap, width)
    run = functools.partial(call, grant=24 if n <= 4 else 56)
    place = jnp.stack([lax.axis_index("ctx"), lax.axis_index("tp")]).astype(jnp.int32)
    placed = {0: pltpu.SMEM}

    def send(x, s):
        return lax.ppermute(x, "ctx", [(i, i ^ s) for i in range(n)]) if s else x

    def swap(x):
        return lax.ppermute(x, "tp", [(0, 1), (1, 0)])

    def spread(x):
        return lax.all_to_all(x, "ctx", split_axis=0, concat_axis=0, tiled=True)

    meta = jnp.concatenate([expert_ids.T, gate_fix.T], axis=0)
    hid_t = hidden.transpose(1, 2, 0)
    named = jnp.pad(expert_ids.T.astype(BF16), ((0, 8 - top), (0, half - tokens)))
    packed = jnp.concatenate([grad_out, named], axis=0)
    own = [send(packed, s) for s in range(n)]
    swapped = swap(packed)
    meta, swapped = lax.optimization_barrier((meta, swapped))
    slots = shaped((n, width, ff))
    (hid_sent,) = run(functools.partial(dispatch_kernel, dims), [slots], [meta, hid_t], name="dispatch")
    hid = spread(hid_sent)
    for s in range(1, n):
        own[s], hid_sent = lax.optimization_barrier((own[s], hid_sent))
    other = [swapped] + [swap(x) for x in own[1:]]

    grad_sent, held = run(
        functools.partial(grad_kernel, dims, top),
        [slots, shaped((n * tokens, width))],
        [place, *own, *other, w_down], where=placed,
        scratch=[pltpu.VMEM((local, n * cap, full), BF16)],
        name="grad",
    )
    grad_back = spread(grad_sent)

    (theirs,) = run(
        functools.partial(mix_kernel, dims, True), [shaped((n * tokens, half))],
        [place, hid, held, w_down], where=placed, name="mix_sibling",
    )
    arrived = swap(theirs)
    if n == 4:
        (mine,) = run(
            functools.partial(mix_kernel, dims, False), [shaped((n * tokens, half), F32)],
            [place, hid, held, w_down], where=placed, name="mix_own",
        )
        block, cut = shaped((tokens, half), F32), shaped((tokens, half // 2))
        kept, one, two, low, high = run(
            add_split_kernel, [block] * 3 + [cut] * 2, [mine, arrived], name="add"
        )
        low, high = send(low, 1), send(high, 2)
        to_one, to_two = run(
            join_kernel, [shaped((tokens, half))] * 2, [one, two, low, high], name="join"
        )
        parts = [kept, send(to_one, 1), send(to_two, 2)]
    else:
        sums = run(
            functools.partial(mix_add_kernel, dims), [shaped((tokens, half))] * n,
            [place, hid, held, w_down, arrived], where=placed, name="mix_own",
        )
        parts = [send(sums[s], s) for s in range(n)]

    (grad_t,) = run(
        functools.partial(restore_kernel, dims), [shaped((top, ff, tokens))],
        [meta, grad_back], name="restore",
    )
    mixed = sum(x.astype(F32) for x in parts).astype(BF16)
    return mixed, grad_t.transpose(2, 0, 1)


def solution(mesh):
    placed = (
        P(("ctx", "exp"), None, "tp"),
        P(("ctx", "exp"), None),
        P(("ctx", "exp"), None),
        P(("ctx", "exp"), "tp"),
        P("ctx", "tp", None),
    )
    return jax.shard_map(
        body,
        mesh=mesh,
        in_specs=placed,
        out_specs=(P(("ctx", "exp"), "tp"), P(("ctx", "exp"), None, "tp")),
        check_vma=False,
    )
```

```python
import functools

import jax
import jax.numpy as jnp
from jax import lax
from jax.experimental import pallas as pl
from jax.experimental.pallas import tpu as pltpu
from jax.sharding import PartitionSpec as P

BF16 = jnp.bfloat16
F32 = jnp.float32
NN = (((1,), (0,)), ((), ()))
NT = (((1,), (1,)), ((), ()))
TN = (((0,), (0,)), ((), ()))
BIG = 10**11


def dot(a, b, dims):
    return lax.dot_general(a, b, dims, preferred_element_type=F32)


def iota(shape, axis):
    return lax.broadcasted_iota(jnp.int32, shape, axis)


def ones_where(mask):
    return mask.astype(F32).astype(BF16)


def earlier(tokens):
    return ones_where(iota((tokens, tokens), 0) < iota((tokens, tokens), 1))


def token_slots(ids, me, experts, local, cap, width):
    top, tokens = ids.shape
    row = iota((experts, tokens), 0)
    hits = [ids[k : k + 1, :] == row for k in range(top)]
    named = functools.reduce(jnp.logical_or, hits)
    before = dot(ones_where(named), earlier(tokens), NN)
    base = jnp.bitwise_xor(row // local, me) * width + lax.rem(row, local) * cap
    slot = before + base.astype(F32)
    return [
        jnp.sum(jnp.where(hit, slot, 0.0), axis=0, keepdims=True).astype(jnp.int32)
        for hit in hits
    ]


def named_here(ids, me, local):
    top, tokens = ids.shape
    row = iota((8, tokens), 0) + me * local
    return functools.reduce(
        jnp.logical_or, [ids[k : k + 1, :] == row for k in range(top)]
    )


def slots_by_lane(ids, me, local, cap, width):
    tokens = ids.shape[1]
    named = named_here(ids, me, local)
    before = dot(ones_where(named), earlier(tokens), NN)
    slot = before.astype(jnp.int32) + iota((8, tokens), 0) * cap
    slot = jnp.where(named, slot, -1)
    rows = iota((cap, tokens), 0)
    return [ones_where(rows + l * cap == slot[l : l + 1, :]) for l in range(local)]


def picks_of(meta, me, dims):
    experts, local, cap, width = dims
    top = meta.shape[0] // 2
    slots = token_slots(meta[:top], me, experts, local, cap, width)
    rows = iota((experts // local * width, meta.shape[1]), 0)
    picks = jnp.concatenate([ones_where(rows == slot) for slot in slots], axis=1)
    return picks, meta[top:].astype(F32) * (1.0 / 65536.0)


def dispatch_kernel(dims, place, meta_ref, hid_ref, *outs):
    width = outs[0].shape[0]
    picks, gate = picks_of(meta_ref[...], place[0], dims)
    scaled = [
        (hid_ref[k].astype(F32) * gate[k : k + 1, :]).astype(BF16)
        for k in range(hid_ref.shape[0])
    ]
    rows = jnp.concatenate(scaled, axis=1)
    spare = outs[0].shape[1] - rows.shape[0]
    tokens = hid_ref.shape[2]
    number = jnp.bitwise_and(iota((spare, rows.shape[1]), 1), tokens - 1) + 1
    number = jnp.where(iota(number.shape, 0) == 0, number.astype(F32), 0.0)
    sent = dot(picks, jnp.concatenate([rows, number.astype(BF16)], axis=0), NT)
    for s, out in enumerate(outs):
        out[...] = sent[s * width : (s + 1) * width].astype(BF16)


def by_expert(rows, local, cap):
    return [
        jnp.concatenate([r[l * cap : (l + 1) * cap] for r in rows], axis=0)
        for l in range(local)
    ]


def by_source(rows, count, cap):
    return [
        jnp.concatenate([r[s * cap : (s + 1) * cap] for r in rows], axis=0)
        for s in range(count)
    ]


def routes(dims, top, me, packed, tokens):
    experts, local, cap, width = dims
    ids = packed[tokens:, :tokens].astype(F32).astype(jnp.int32)[:top]
    return jnp.concatenate(slots_by_lane(ids, me, local, cap, width), axis=0)


def gather_rows(dims, held, halves, x_ref):
    experts, local, cap, width = dims
    tokens, half = held[0].shape[1], halves[0].shape[1]
    chunk = min(half, 512)
    for c in range(0, half, chunk):
        rows = [dot(h, ref[:tokens, c : c + chunk], NN) for h, ref in zip(held, halves)]
        for l, x in enumerate(by_expert(rows, local, cap)):
            x_ref[l, :, c : c + chunk] = x.astype(BF16)


def gather_kernel(dims, top, place, *refs):
    x_ref, held_ref = refs[-2:]
    own = refs[:-2]
    tokens = held_ref.shape[2]
    held = [routes(dims, top, place[0], ref, tokens) for ref in own]
    for s, h in enumerate(held):
        held_ref[s] = h
    gather_rows(dims, held, own, x_ref)


def products(dims, place, x_ref, x_other, w_ref):
    half = x_ref.shape[2]
    mine = pl.ds(pl.multiple_of(place[1] * half, half), half)
    theirs = pl.ds(pl.multiple_of((1 - place[1]) * half, half), half)
    return [
        dot(x_ref[l], w_ref[l, :, mine], NT) + dot(x_other[l], w_ref[l, :, theirs], NT)
        for l in range(dims[1])
    ]


def grad_kernel(dims, place, *refs):
    n = (len(refs) - 4) // 2
    other = refs[:n]
    x_ref, held_ref, w_ref = refs[n : n + 3]
    outs, x_other = refs[n + 3 : 2 * n + 3], refs[-1]
    gather_rows(dims, [held_ref[s] for s in range(n)], other, x_other)
    grads = products(dims, place, x_ref, x_other, w_ref)
    for s, rows in enumerate(by_source(grads, n, dims[2])):
        outs[s][...] = rows.astype(BF16)


def mix_rows(dims, side, hid, w_ref, tokens, half, store):
    experts, local, cap, width = dims
    n = len(hid)
    ff = w_ref.shape[1]
    chunk = min(half, 256)
    same = ones_where(iota((tokens, tokens), 0) == iota((tokens, tokens), 1))
    held = []
    for h in hid:
        number = h[:, ff : ff + 1].astype(F32).astype(jnp.int32) - 1
        slots = ones_where(iota((width, tokens), 1) == number)
        held.append(dot(same, slots, NT).astype(BF16))
    rows = [h[:, :ff].astype(F32) for h in hid]
    x = [r.astype(BF16) for r in by_expert(rows, local, cap)]
    for c in range(0, half, chunk):
        at = pl.ds(pl.multiple_of(side * half + c, chunk), chunk)
        out = [dot(x[l], w_ref[l, :, at], NN) for l in range(local)]
        for s, rows in enumerate(by_source(out, n, cap)):
            store(s, slice(c, c + chunk), dot(held[s], rows.astype(BF16), NN))


def mix_kernel(dims, sibling, place, *refs):
    hid, (w_ref, out) = refs[:-2], refs[-2:]
    tokens = out.shape[0] // len(hid)

    def store(s, columns, part):
        out[pl.ds(s * tokens, tokens), columns] = part.astype(out.dtype)

    side = 1 - place[1] if sibling else place[1]
    mix_rows(dims, side, hid, w_ref, tokens, out.shape[1], store)


def mix_add_kernel(dims, place, *refs):
    n = (len(refs) - 2) // 2
    hid, (w_ref, arrived), outs = refs[:n], refs[n : n + 2], refs[n + 2 :]
    tokens, half = outs[0].shape

    def store(s, columns, part):
        theirs = arrived[pl.ds(s * tokens, tokens), columns].astype(F32)
        outs[s][:, columns] = (part + theirs).astype(BF16)

    mix_rows(dims, place[1], hid, w_ref, tokens, half, store)


def add_split_kernel(own, arrived, mine, one, two, low, high):
    tokens, half = mine.shape
    cut = half // 2
    for s, out in enumerate((mine, one, two)):
        at = pl.ds(s * tokens, tokens)
        out[...] = own[at, :] + arrived[at, :].astype(F32)
    at = pl.ds(3 * tokens, tokens)
    far = own[at, :] + arrived[at, :].astype(F32)
    low[...] = far[:, :cut].astype(BF16)
    high[...] = far[:, cut:].astype(BF16)


def join_kernel(one, two, low, high, to_one, to_two):
    cut = one.shape[1] // 2
    to_one[:, :cut] = one[:, :cut].astype(BF16)
    to_one[:, cut:] = (one[:, cut:] + high[...].astype(F32)).astype(BF16)
    to_two[:, :cut] = (two[:, :cut] + low[...].astype(F32)).astype(BF16)
    to_two[:, cut:] = two[:, cut:].astype(BF16)


def restore_kernel(dims, place, meta_ref, *refs):
    back_refs, out = refs[:-1], refs[-1]
    top, _, tokens = out.shape
    picks, gate = picks_of(meta_ref[...], place[0], dims)
    back = jnp.concatenate([ref[...] for ref in back_refs], axis=0)
    grads = dot(back, picks, TN)
    for k in range(top):
        out[k] = (grads[:, k * tokens : (k + 1) * tokens] * gate[k : k + 1, :]).astype(BF16)


def shaped(shape, dtype=BF16):
    return jax.ShapeDtypeStruct(shape, dtype)


def call(kernel, outs, args, where=(), scratch=(), grant=24, weight=1, name=None):
    where = dict(where)
    return pl.pallas_call(
        kernel,
        out_shape=outs,
        in_specs=[
            pl.BlockSpec(memory_space=where.get(i, pltpu.VMEM)) for i in range(len(args))
        ],
        out_specs=[pl.BlockSpec(memory_space=pltpu.VMEM)] * len(outs),
        scratch_shapes=scratch,
        compiler_params=pltpu.CompilerParams(vmem_limit_bytes=grant * 1024 * 1024),
        cost_estimate=pl.CostEstimate(
            flops=weight, bytes_accessed=1, transcendentals=0
        ),
        name=name,
    )(*args)


def body(hidden, expert_ids, gate_fix, grad_out, w_down):
    tokens, top, ff = hidden.shape
    half = grad_out.shape[1]
    local, _, full = w_down.shape
    n = lax.axis_size("ctx")
    experts = n * local
    assigned = tokens * top
    cap = min(tokens, assigned // experts + max(1, assigned // (8 * experts)))
    unit = 8 if local % 2 == 0 else 16
    cap = -(-cap // unit) * unit
    width = local * cap
    dims = (experts, local, cap, width)
    run = functools.partial(call, grant=24 if n <= 4 else 56)
    place = jnp.stack([lax.axis_index("ctx"), lax.axis_index("tp")]).astype(jnp.int32)
    placed = {0: pltpu.SMEM}

    def send(x, s):
        return lax.ppermute(x, "ctx", [(i, i ^ s) for i in range(n)]) if s else x

    def swap(x):
        return lax.ppermute(x, "tp", [(0, 1), (1, 0)])

    meta = jnp.concatenate([expert_ids.T, gate_fix.T], axis=0)
    hid_t = hidden.transpose(1, 2, 0)
    named = jnp.pad(expert_ids.T.astype(BF16), ((0, 8 - top), (0, half - tokens)))
    packed = jnp.concatenate([grad_out, named], axis=0)
    forward = n == 4
    own = [send(packed, s) for s in range(n)]
    hid_sent = run(
        functools.partial(dispatch_kernel, dims), [shaped((width, -(-(ff + 1) // 128) * 128))] * n,
        [place, meta, hid_t], where=placed, name="dispatch",
    )
    hid = [send(hid_sent[s], s) for s in range(n)]
    for s in range(1, n):
        own[s], hid[0] = lax.optimization_barrier((own[s], hid[0]))
    other = [swap(x) for x in own]

    slot = shaped((width, ff))
    x, held = run(
        functools.partial(gather_kernel, dims, top),
        [shaped((local, n * cap, half)), shaped((n, width, tokens))],
        [place, *own], where=placed, name="gather", weight=BIG,
    )
    grad_sent = run(
        functools.partial(grad_kernel, dims), [slot] * n,
        [place, *other, x, held, w_down], where=placed,
        scratch=[pltpu.VMEM((local, n * cap, half), BF16)], name="grad",
    )
    hid[0], grad_own = lax.optimization_barrier((hid[0], grad_sent[0]))
    grad_back = [grad_own] + [send(grad_sent[s], s) for s in range(1, n)]

    (theirs,) = run(
        functools.partial(mix_kernel, dims, True), [shaped((n * tokens, half))],
        [place, *hid, w_down], where=placed, name="mix_sibling",
    )
    arrived = swap(theirs)
    if forward:
        (mine,) = run(
            functools.partial(mix_kernel, dims, False), [shaped((n * tokens, half), F32)],
            [place, *hid, w_down], where=placed, name="mix_own", weight=BIG,
        )
        cut = half // 2
        block, piece = shaped((tokens, half), F32), shaped((tokens, cut))
        kept, one, two, one_low, two_high = run(
            add_split_kernel, [block] * 3 + [piece] * 2, [mine, arrived], name="add"
        )
        one_low, two_high = send(one_low, 1), send(two_high, 2)
        to_one, to_two = run(
            join_kernel, [shaped((tokens, half))] * 2, [one, two, one_low, two_high],
            name="join",
        )
        parts = [kept, send(to_one, 1), send(to_two, 2)]
    else:
        sums = run(
            functools.partial(mix_add_kernel, dims), [shaped((tokens, half))] * n,
            [place, *hid, w_down, arrived], where=placed, name="mix_own",
        )
        parts = [send(sums[s], s) for s in range(n)]

    (grad_t,) = run(
        functools.partial(restore_kernel, dims), [shaped((top, ff, tokens))],
        [place, meta, *grad_back], where=placed, name="restore", weight=BIG,
    )
    mixed = sum(x.astype(F32) for x in parts).astype(BF16)
    return mixed, grad_t.transpose(2, 0, 1)


def solution(mesh):
    placed = (
        P(("ctx", "exp"), None, "tp"),
        P(("ctx", "exp"), None),
        P(("ctx", "exp"), None),
        P(("ctx", "exp"), "tp"),
        P("ctx", "tp", None),
    )
    return jax.shard_map(
        body,
        mesh=mesh,
        in_specs=placed,
        out_specs=(P(("ctx", "exp"), "tp"), P(("ctx", "exp"), None, "tp")),
        check_vma=False,
    )
```

```python
import functools

import jax
import jax.numpy as jnp
from jax import lax
from jax.experimental import pallas as pl
from jax.experimental.pallas import tpu as pltpu
from jax.sharding import PartitionSpec as P

BF16 = jnp.bfloat16
F32 = jnp.float32
NN = (((1,), (0,)), ((), ()))
NT = (((1,), (1,)), ((), ()))
TN = (((0,), (0,)), ((), ()))
BIG = 10**11
W_GATHER, W_GRAD, W_FAR, FAR_LATE = 1, 1, 1, False


def dot(a, b, dims):
    return lax.dot_general(a, b, dims, preferred_element_type=F32)


def iota(shape, axis):
    return lax.broadcasted_iota(jnp.int32, shape, axis)


def ones_where(mask):
    return mask.astype(F32).astype(BF16)


def earlier(tokens):
    return ones_where(iota((tokens, tokens), 0) < iota((tokens, tokens), 1))


def token_slots(ids, me, experts, local, cap, width):
    top, tokens = ids.shape
    row = iota((experts, tokens), 0)
    hits = [ids[k : k + 1, :] == row for k in range(top)]
    named = functools.reduce(jnp.logical_or, hits)
    before = dot(ones_where(named), earlier(tokens), NN)
    base = jnp.bitwise_xor(row // local, me) * width + lax.rem(row, local) * cap
    slot = before + base.astype(F32)
    return [
        jnp.sum(jnp.where(hit, slot, 0.0), axis=0, keepdims=True).astype(jnp.int32)
        for hit in hits
    ]


def named_here(ids, me, local):
    top, tokens = ids.shape
    row = iota((8, tokens), 0) + me * local
    return functools.reduce(
        jnp.logical_or, [ids[k : k + 1, :] == row for k in range(top)]
    )


def slots_by_lane(ids, me, local, cap, width):
    tokens = ids.shape[1]
    named = named_here(ids, me, local)
    before = dot(ones_where(named), earlier(tokens), NN)
    slot = before.astype(jnp.int32) + iota((8, tokens), 0) * cap
    slot = jnp.where(named, slot, -1)
    rows = iota((cap, tokens), 0)
    return [ones_where(rows + l * cap == slot[l : l + 1, :]) for l in range(local)]


def picks_of(meta, me, dims):
    experts, local, cap, width = dims
    top = meta.shape[0] // 2
    slots = token_slots(meta[:top], me, experts, local, cap, width)
    rows = iota((experts // local * width, meta.shape[1]), 0)
    picks = jnp.concatenate([ones_where(rows == slot) for slot in slots], axis=1)
    return picks, meta[top:].astype(F32) * (1.0 / 65536.0)


def dispatch_kernel(dims, place, meta_ref, hid_ref, *outs):
    experts, local, cap, width = dims
    count = experts // local
    picks, gate = picks_of(meta_ref[...], place[0], dims)
    scaled = [
        (hid_ref[k].astype(F32) * gate[k : k + 1, :]).astype(BF16)
        for k in range(hid_ref.shape[0])
    ]
    rows = jnp.concatenate(scaled, axis=1)
    spare = outs[0].shape[1] - rows.shape[0]
    tokens = hid_ref.shape[2]
    number = jnp.bitwise_and(iota((spare, rows.shape[1]), 1), tokens - 1) + 1
    number = jnp.where(iota(number.shape, 0) == 0, number.astype(F32), 0.0)
    sent = dot(picks, jnp.concatenate([rows, number.astype(BF16)], axis=0), NT)
    sent = [sent[s * width : (s + 1) * width] for s in range(count)]
    if len(outs) < count:
        mine, one, two, far = sent
        first = outs[1].shape[0] - width
        sent = [
            mine,
            jnp.concatenate([one, far[:first]], axis=0),
            jnp.concatenate([two, far[first:]], axis=0),
        ]
    for rows, out in zip(sent, outs):
        out[...] = rows.astype(BF16)


def pass_rows_kernel(one, two, to_two, to_one):
    first, second = to_two.shape[0], to_one.shape[0]
    to_two[...] = one[one.shape[0] - first :]
    to_one[...] = two[two.shape[0] - second :]


def by_expert(rows, local, cap):
    return [
        jnp.concatenate([r[l * cap : (l + 1) * cap] for r in rows], axis=0)
        for l in range(local)
    ]


def by_source(rows, count, cap):
    return [
        jnp.concatenate([r[s * cap : (s + 1) * cap] for r in rows], axis=0)
        for s in range(count)
    ]


def routes(dims, top, me, packed, tokens):
    experts, local, cap, width = dims
    ids = packed[tokens:, :tokens].astype(F32).astype(jnp.int32)[:top]
    return jnp.concatenate(slots_by_lane(ids, me, local, cap, width), axis=0)


def gather_rows(dims, held, halves, x_ref):
    experts, local, cap, width = dims
    tokens, half = held[0].shape[1], halves[0].shape[1]
    chunk = min(half, 512)
    for c in range(0, half, chunk):
        rows = [dot(h, ref[:tokens, c : c + chunk], NN) for h, ref in zip(held, halves)]
        for l, x in enumerate(by_expert(rows, local, cap)):
            x_ref[l, :, c : c + chunk] = x.astype(BF16)


def gather_kernel(dims, top, place, *refs):
    x_ref, held_ref = refs[-2:]
    own = refs[:-2]
    tokens = held_ref.shape[2]
    held = [routes(dims, top, place[0], ref, tokens) for ref in own]
    for s, h in enumerate(held):
        held_ref[s] = h
    gather_rows(dims, held, own, x_ref)


def gather_pass_kernel(dims, top, place, *refs):
    own, (x_ref, held_ref, low, high) = refs[:3], refs[3:]
    cut = low.shape[1]
    low[...] = own[1][:, :cut]
    high[...] = own[2][:, cut:]
    gather_kernel(dims, top, place, *own, x_ref, held_ref)


def products(dims, place, x_ref, x_other, w_ref):
    half = x_ref.shape[2]
    mine = pl.ds(pl.multiple_of(place[1] * half, half), half)
    theirs = pl.ds(pl.multiple_of((1 - place[1]) * half, half), half)
    return [
        dot(x_ref[l], w_ref[l, :, mine], NT) + dot(x_other[l], w_ref[l, :, theirs], NT)
        for l in range(dims[1])
    ]


def grad_kernel(dims, place, *refs):
    n = (len(refs) - 4) // 2
    other = refs[:n]
    x_ref, held_ref, w_ref = refs[n : n + 3]
    outs, x_other = refs[n + 3 : 2 * n + 3], refs[-1]
    gather_rows(dims, [held_ref[s] for s in range(n)], other, x_other)
    grads = products(dims, place, x_ref, x_other, w_ref)
    for s, rows in enumerate(by_source(grads, n, dims[2])):
        outs[s][...] = rows.astype(BF16)


def grad_far_kernel(dims, top, place, low, high, low_other, high_other, w_ref, out, x_ref, x_other):
    experts, local, cap, width = dims
    cut = low.shape[1]
    tokens = low.shape[0] - 8
    held = [routes(dims, top, place[0], low, tokens)]
    for ref, at, x in (
        (low, 0, x_ref), (high, cut, x_ref), (low_other, 0, x_other), (high_other, cut, x_other)
    ):
        gather_rows(dims, held, [ref], x.at[:, :, pl.ds(at, cut)])
    grads = products(dims, place, x_ref, x_other, w_ref)
    out[...] = jnp.concatenate(grads, axis=0).astype(BF16)


def whole_rows(dims, hid):
    experts, local, cap, width = dims
    if len(hid) <= experts // local:
        return [h[...].astype(F32) for h in hid]
    mine, one, two, first, second = [h[...].astype(F32) for h in hid]
    return [mine, one[:width], two[:width], jnp.concatenate([first, second], axis=0)]


def mix_rows(dims, side, hid, w_ref, tokens, half, store):
    experts, local, cap, width = dims
    n = dims[0] // dims[1]
    ff = w_ref.shape[1]
    chunk = min(half, 256)
    same = ones_where(iota((tokens, tokens), 0) == iota((tokens, tokens), 1))
    hid = whole_rows(dims, hid)
    held = []
    for h in hid:
        number = h[:, ff : ff + 1].astype(jnp.int32) - 1
        slots = ones_where(iota((width, tokens), 1) == number)
        held.append(dot(same, slots, NT).astype(BF16))
    rows = [h[:, :ff] for h in hid]
    x = [r.astype(BF16) for r in by_expert(rows, local, cap)]
    for c in range(0, half, chunk):
        at = pl.ds(pl.multiple_of(side * half + c, chunk), chunk)
        out = [dot(x[l], w_ref[l, :, at], NN) for l in range(local)]
        for s, rows in enumerate(by_source(out, n, cap)):
            store(s, slice(c, c + chunk), dot(held[s], rows.astype(BF16), NN))


def mix_kernel(dims, sibling, place, *refs):
    hid, (w_ref, out) = refs[:-2], refs[-2:]
    tokens = out.shape[0] // (dims[0] // dims[1])

    def store(s, columns, part):
        out[pl.ds(s * tokens, tokens), columns] = part.astype(out.dtype)

    side = 1 - place[1] if sibling else place[1]
    mix_rows(dims, side, hid, w_ref, tokens, out.shape[1], store)


def mix_add_kernel(dims, place, *refs):
    n = (len(refs) - 2) // 2
    hid, (w_ref, arrived), outs = refs[:n], refs[n : n + 2], refs[n + 2 :]
    tokens, half = outs[0].shape

    def store(s, columns, part):
        theirs = arrived[pl.ds(s * tokens, tokens), columns].astype(F32)
        outs[s][:, columns] = (part + theirs).astype(BF16)

    mix_rows(dims, place[1], hid, w_ref, tokens, half, store)


def add_split_kernel(own, arrived, mine, one, two, low, high):
    tokens, half = mine.shape
    cut = half // 2
    for s, out in enumerate((mine, one, two)):
        at = pl.ds(s * tokens, tokens)
        out[...] = own[at, :] + arrived[at, :].astype(F32)
    at = pl.ds(3 * tokens, tokens)
    far = own[at, :] + arrived[at, :].astype(F32)
    low[...] = far[:, :cut].astype(BF16)
    high[...] = far[:, cut:].astype(BF16)


def join_kernel(one, two, low, high, to_one, to_two):
    cut = one.shape[1] // 2
    to_one[:, :cut] = one[:, :cut].astype(BF16)
    to_one[:, cut:] = (one[:, cut:] + high[...].astype(F32)).astype(BF16)
    to_two[:, :cut] = (two[:, :cut] + low[...].astype(F32)).astype(BF16)
    to_two[:, cut:] = two[:, cut:].astype(BF16)


def restore_kernel(dims, place, meta_ref, *refs):
    back_refs, out = refs[:-1], refs[-1]
    top, _, tokens = out.shape
    picks, gate = picks_of(meta_ref[...], place[0], dims)
    back = jnp.concatenate([ref[...] for ref in back_refs], axis=0)
    grads = dot(back, picks, TN)
    for k in range(top):
        out[k] = (grads[:, k * tokens : (k + 1) * tokens] * gate[k : k + 1, :]).astype(BF16)


def shaped(shape, dtype=BF16):
    return jax.ShapeDtypeStruct(shape, dtype)


def call(kernel, outs, args, where=(), scratch=(), grant=24, weight=1, name=None):
    where = dict(where)
    return pl.pallas_call(
        kernel,
        out_shape=outs,
        in_specs=[
            pl.BlockSpec(memory_space=where.get(i, pltpu.VMEM)) for i in range(len(args))
        ],
        out_specs=[pl.BlockSpec(memory_space=pltpu.VMEM)] * len(outs),
        scratch_shapes=scratch,
        compiler_params=pltpu.CompilerParams(vmem_limit_bytes=grant * 1024 * 1024),
        cost_estimate=pl.CostEstimate(
            flops=weight, bytes_accessed=1, transcendentals=0
        ),
        name=name,
    )(*args)


def body(hidden, expert_ids, gate_fix, grad_out, w_down):
    tokens, top, ff = hidden.shape
    half = grad_out.shape[1]
    local, _, full = w_down.shape
    n = lax.axis_size("ctx")
    experts = n * local
    assigned = tokens * top
    cap = min(tokens, assigned // experts + max(1, assigned // (8 * experts)))
    unit = 8 if local % 2 == 0 else 16
    cap = -(-cap // unit) * unit
    width = local * cap
    dims = (experts, local, cap, width)
    run = functools.partial(call, grant=24 if n <= 4 else 56)
    place = jnp.stack([lax.axis_index("ctx"), lax.axis_index("tp")]).astype(jnp.int32)
    placed = {0: pltpu.SMEM}

    def send(x, s):
        return lax.ppermute(x, "ctx", [(i, i ^ s) for i in range(n)]) if s else x

    def swap(x):
        return lax.ppermute(x, "tp", [(0, 1), (1, 0)])

    meta = jnp.concatenate([expert_ids.T, gate_fix.T], axis=0)
    hid_t = hidden.transpose(1, 2, 0)
    named = jnp.pad(expert_ids.T.astype(BF16), ((0, 8 - top), (0, half - tokens)))
    packed = jnp.concatenate([grad_out, named], axis=0)
    forward = n == 4
    near = 3 if forward else n
    own = [send(packed, s) for s in range(near)]
    swapped = swap(packed)
    lanes = -(-(ff + 1) // 128) * 128
    first = -(-(width // 2) // 16) * 16
    rows = [width, width + first, 2 * width - first] if forward else [width] * n
    hid_sent = run(
        functools.partial(dispatch_kernel, dims), [shaped((r, lanes)) for r in rows],
        [place, meta, hid_t], where=placed, name="dispatch",
    )
    hid = [send(hid_sent[s], s) for s in range(near)]
    for s in range(1, near):
        own[s], hid[0] = lax.optimization_barrier((own[s], hid[0]))
    other = [swapped] + [swap(x) for x in own[1:]]

    slot = shaped((width, ff))
    x_near = shaped((local, near * cap, half))
    held_near = shaped((near, width, tokens))
    if forward:
        cut = half // 2
        passed = shaped((tokens + 8, cut))
        x, held, low, high = run(
            functools.partial(gather_pass_kernel, dims, top),
            [x_near, held_near, passed, passed], [place, *own],
            where=placed, name="gather", weight=W_GATHER,
        )
        low, high = send(low, 2), send(high, 1)
    else:
        x, held = run(
            functools.partial(gather_kernel, dims, top), [x_near, held_near],
            [place, *own], where=placed, name="gather",
        )
    grad_sent = run(
        functools.partial(grad_kernel, dims), [slot] * near,
        [place, *other, x, held, w_down], where=placed,
        scratch=[pltpu.VMEM(x_near.shape, BF16)], name="grad", weight=W_GRAD,
    )
    if forward:
        hid[1], hid[2], grad_own = lax.optimization_barrier((hid[1], hid[2], grad_sent[0]))
        to_two, to_one = run(
            pass_rows_kernel, [shaped((first, lanes)), shaped((width - first, lanes))],
            hid[1:], name="pass_rows", weight=BIG,
        )
        hid += [send(to_two, 2), send(to_one, 1)]
        low, high, *hid[3:] = lax.optimization_barrier((low, high, *hid[3:]))
    else:
        hid[0], grad_own = lax.optimization_barrier((hid[0], grad_sent[0]))
    grad_back = [grad_own] + [send(grad_sent[s], s) for s in range(1, near)]

    (theirs,) = run(
        functools.partial(mix_kernel, dims, True), [shaped((n * tokens, half))],
        [place, *hid, w_down], where=placed, name="mix_sibling",
    )
    arrived = swap(theirs)
    if forward:
        (mine,) = run(
            functools.partial(mix_kernel, dims, False), [shaped((n * tokens, half), F32)],
            [place, *hid, w_down], where=placed, name="mix_own", weight=BIG,
        )
        block, piece = shaped((tokens, half), F32), shaped((tokens, cut))
        kept, one, two, one_low, two_high = run(
            add_split_kernel, [block] * 3 + [piece] * 2, [mine, arrived], name="add"
        )
        if FAR_LATE:
            low, kept = lax.optimization_barrier((low, kept))
        x_far = pltpu.VMEM((local, cap, half), BF16)
        (grad_far,) = run(
            functools.partial(grad_far_kernel, dims, top), [slot],
            [place, low, high, swap(low), swap(high), w_down], where=placed,
            scratch=[x_far, x_far], name="grad_far", weight=W_FAR,
        )
        grad_back.append(send(grad_far, 3))
        one_low, two_high = send(one_low, 1), send(two_high, 2)
        to_one, to_two = run(
            join_kernel, [shaped((tokens, half))] * 2, [one, two, one_low, two_high],
            name="join",
        )
        parts = [kept, send(to_one, 1), send(to_two, 2)]
    else:
        sums = run(
            functools.partial(mix_add_kernel, dims), [shaped((tokens, half))] * n,
            [place, *hid, w_down, arrived], where=placed, name="mix_own",
        )
        parts = [send(sums[s], s) for s in range(n)]

    (grad_t,) = run(
        functools.partial(restore_kernel, dims), [shaped((top, ff, tokens))],
        [place, meta, *grad_back], where=placed, name="restore", weight=BIG,
    )
    mixed = sum(x.astype(F32) for x in parts).astype(BF16)
    return mixed, grad_t.transpose(2, 0, 1)


def solution(mesh):
    placed = (
        P(("ctx", "exp"), None, "tp"),
        P(("ctx", "exp"), None),
        P(("ctx", "exp"), None),
        P(("ctx", "exp"), "tp"),
        P("ctx", "tp", None),
    )
    return jax.shard_map(
        body,
        mesh=mesh,
        in_specs=placed,
        out_specs=(P(("ctx", "exp"), "tp"), P(("ctx", "exp"), None, "tp")),
        check_vma=False,
    )
```

```python
import functools

import jax
import jax.numpy as jnp
from jax import lax
from jax.experimental import pallas as pl
from jax.experimental.pallas import tpu as pltpu
from jax.sharding import PartitionSpec as P

BF16 = jnp.bfloat16
F32 = jnp.float32
NN = (((1,), (0,)), ((), ()))
NT = (((1,), (1,)), ((), ()))
TN = (((0,), (0,)), ((), ()))
BIG = 10**11
W_GATHER, TIE_OWN = BIG, True


def dot(a, b, dims):
    return lax.dot_general(a, b, dims, preferred_element_type=F32)


def iota(shape, axis):
    return lax.broadcasted_iota(jnp.int32, shape, axis)


def ones_where(mask):
    return mask.astype(F32).astype(BF16)


def earlier(tokens):
    return ones_where(iota((tokens, tokens), 0) < iota((tokens, tokens), 1))


def token_slots(ids, me, experts, local, cap, width):
    top, tokens = ids.shape
    row = iota((experts, tokens), 0)
    hits = [ids[k : k + 1, :] == row for k in range(top)]
    named = functools.reduce(jnp.logical_or, hits)
    before = dot(ones_where(named), earlier(tokens), NN)
    base = jnp.bitwise_xor(row // local, me) * width + lax.rem(row, local) * cap
    slot = before + base.astype(F32)
    return [
        jnp.sum(jnp.where(hit, slot, 0.0), axis=0, keepdims=True).astype(jnp.int32)
        for hit in hits
    ]


def named_here(ids, me, local):
    top, tokens = ids.shape
    row = iota((8, tokens), 0) + me * local
    return functools.reduce(
        jnp.logical_or, [ids[k : k + 1, :] == row for k in range(top)]
    )


def slots_by_lane(ids, me, local, cap, width):
    tokens = ids.shape[1]
    named = named_here(ids, me, local)
    before = dot(ones_where(named), earlier(tokens), NN)
    slot = before.astype(jnp.int32) + iota((8, tokens), 0) * cap
    slot = jnp.where(named, slot, -1)
    rows = iota((cap, tokens), 0)
    return [ones_where(rows + l * cap == slot[l : l + 1, :]) for l in range(local)]


def picks_of(meta, me, dims):
    experts, local, cap, width = dims
    top = meta.shape[0] // 2
    slots = token_slots(meta[:top], me, experts, local, cap, width)
    rows = iota((experts // local * width, meta.shape[1]), 0)
    picks = jnp.concatenate([ones_where(rows == slot) for slot in slots], axis=1)
    return picks, meta[top:].astype(F32) * (1.0 / 65536.0)


def dispatch_kernel(dims, place, meta_ref, hid_ref, *outs):
    width = outs[0].shape[0]
    picks, gate = picks_of(meta_ref[...], place[0], dims)
    scaled = [
        (hid_ref[k].astype(F32) * gate[k : k + 1, :]).astype(BF16)
        for k in range(hid_ref.shape[0])
    ]
    rows = jnp.concatenate(scaled, axis=1)
    spare = outs[0].shape[1] - rows.shape[0]
    tokens = hid_ref.shape[2]
    number = jnp.bitwise_and(iota((spare, rows.shape[1]), 1), tokens - 1) + 1
    number = jnp.where(iota(number.shape, 0) == 0, number.astype(F32), 0.0)
    sent = dot(picks, jnp.concatenate([rows, number.astype(BF16)], axis=0), NT)
    for s, out in enumerate(outs):
        out[...] = sent[s * width : (s + 1) * width].astype(BF16)


def by_expert(rows, local, cap):
    return [
        jnp.concatenate([r[l * cap : (l + 1) * cap] for r in rows], axis=0)
        for l in range(local)
    ]


def by_source(rows, count, cap):
    return [
        jnp.concatenate([r[s * cap : (s + 1) * cap] for r in rows], axis=0)
        for s in range(count)
    ]


def routes(dims, top, me, packed, tokens):
    experts, local, cap, width = dims
    ids = packed[tokens:, :tokens].astype(F32).astype(jnp.int32)[:top]
    return jnp.concatenate(slots_by_lane(ids, me, local, cap, width), axis=0)


def gather_rows(dims, held, halves, x_ref):
    experts, local, cap, width = dims
    tokens, half = held[0].shape[1], halves[0].shape[1]
    chunk = min(half, 512)
    for c in range(0, half, chunk):
        rows = [dot(h, ref[:tokens, c : c + chunk], NN) for h, ref in zip(held, halves)]
        for l, x in enumerate(by_expert(rows, local, cap)):
            x_ref[l, :, c : c + chunk] = x.astype(BF16)


def join_far(refs, n, tokens):
    blocks = [[ref] for ref in refs[:n]]
    if len(refs) > n:
        blocks = blocks[: n - 1] + [list(refs[n - 1 :])]
    return blocks


def gather_rows(dims, held, blocks, x_ref):
    experts, local, cap, width = dims
    tokens, half = held[0].shape[1], x_ref.shape[2]
    chunk = min(half, 512)
    for c in range(0, half, chunk):
        rows = []
        for h, block in zip(held, blocks):
            size = half // len(block)
            ref, at = block[c // size], c % size
            rows.append(dot(h, ref[:tokens, at : at + chunk], NN))
        for l, x in enumerate(by_expert(rows, local, cap)):
            x_ref[l, :, c : c + chunk] = x.astype(BF16)


def gather_kernel(dims, top, place, *refs):
    experts, local, cap, width = dims
    own, (x_ref, held_ref) = refs[:-2], refs[-2:]
    n, _, tokens = held_ref.shape
    blocks = join_far(own, n, tokens)
    for s, block in enumerate(blocks):
        ids = block[0][tokens:, :tokens].astype(F32).astype(jnp.int32)[:top]
        held_ref[s] = jnp.concatenate(
            slots_by_lane(ids, place[0], local, cap, width), axis=0
        )
    gather_rows(dims, [held_ref[s] for s in range(n)], blocks, x_ref)


def grad_kernel(dims, place, *refs):
    experts, local, cap, width = dims
    n = experts // local
    x_other, outs, (x_ref, held_ref, w_ref) = refs[-1], refs[-1 - n : -1], refs[-4 - n : -1 - n]
    other = refs[: -4 - n]
    half = x_ref.shape[2]
    blocks = join_far(other, n, held_ref.shape[2])
    gather_rows(dims, [held_ref[s] for s in range(n)], blocks, x_other)
    mine = pl.ds(pl.multiple_of(place[1] * half, half), half)
    theirs = pl.ds(pl.multiple_of((1 - place[1]) * half, half), half)
    grads = [
        dot(x_ref[l], w_ref[l, :, mine], NT) + dot(x_other[l], w_ref[l, :, theirs], NT)
        for l in range(local)
    ]
    for s, rows in enumerate(by_source(grads, n, cap)):
        outs[s][...] = rows.astype(BF16)


def pass_kernel(one, two, low, high):
    cut = low.shape[1]
    low[...] = one[:, :cut]
    high[...] = two[:, cut:]


def mix_rows(dims, side, hid, w_ref, tokens, half, store):
    experts, local, cap, width = dims
    n = len(hid)
    ff = w_ref.shape[1]
    chunk = min(half, 256)
    same = ones_where(iota((tokens, tokens), 0) == iota((tokens, tokens), 1))
    held = []
    for h in hid:
        number = h[:, ff : ff + 1].astype(F32).astype(jnp.int32) - 1
        slots = ones_where(iota((width, tokens), 1) == number)
        held.append(dot(same, slots, NT).astype(BF16))
    rows = [h[:, :ff].astype(F32) for h in hid]
    x = [r.astype(BF16) for r in by_expert(rows, local, cap)]
    for c in range(0, half, chunk):
        at = pl.ds(pl.multiple_of(side * half + c, chunk), chunk)
        out = [dot(x[l], w_ref[l, :, at], NN) for l in range(local)]
        for s, rows in enumerate(by_source(out, n, cap)):
            store(s, slice(c, c + chunk), dot(held[s], rows.astype(BF16), NN))


def mix_kernel(dims, sibling, place, *refs):
    hid, (w_ref, out) = refs[:-2], refs[-2:]
    tokens = out.shape[0] // len(hid)

    def store(s, columns, part):
        out[pl.ds(s * tokens, tokens), columns] = part.astype(out.dtype)

    side = 1 - place[1] if sibling else place[1]
    mix_rows(dims, side, hid, w_ref, tokens, out.shape[1], store)


def mix_add_kernel(dims, place, *refs):
    n = (len(refs) - 2) // 2
    hid, (w_ref, arrived), outs = refs[:n], refs[n : n + 2], refs[n + 2 :]
    tokens, half = outs[0].shape

    def store(s, columns, part):
        theirs = arrived[pl.ds(s * tokens, tokens), columns].astype(F32)
        outs[s][:, columns] = (part + theirs).astype(BF16)

    mix_rows(dims, place[1], hid, w_ref, tokens, half, store)


def add_split_kernel(own, arrived, mine, one, two, low, high):
    tokens, half = mine.shape
    cut = half // 2
    for s, out in enumerate((mine, one, two)):
        at = pl.ds(s * tokens, tokens)
        out[...] = own[at, :] + arrived[at, :].astype(F32)
    at = pl.ds(3 * tokens, tokens)
    far = own[at, :] + arrived[at, :].astype(F32)
    low[...] = far[:, :cut].astype(BF16)
    high[...] = far[:, cut:].astype(BF16)


def join_kernel(one, two, low, high, to_one, to_two):
    cut = one.shape[1] // 2
    to_one[:, :cut] = one[:, :cut].astype(BF16)
    to_one[:, cut:] = (one[:, cut:] + high[...].astype(F32)).astype(BF16)
    to_two[:, :cut] = (two[:, :cut] + low[...].astype(F32)).astype(BF16)
    to_two[:, cut:] = two[:, cut:].astype(BF16)


def restore_kernel(dims, place, meta_ref, *refs):
    back_refs, out = refs[:-1], refs[-1]
    top, _, tokens = out.shape
    picks, gate = picks_of(meta_ref[...], place[0], dims)
    back = jnp.concatenate([ref[...] for ref in back_refs], axis=0)
    grads = dot(back, picks, TN)
    for k in range(top):
        out[k] = (grads[:, k * tokens : (k + 1) * tokens] * gate[k : k + 1, :]).astype(BF16)


def shaped(shape, dtype=BF16):
    return jax.ShapeDtypeStruct(shape, dtype)


def call(kernel, outs, args, where=(), scratch=(), grant=24, weight=1, name=None):
    where = dict(where)
    return pl.pallas_call(
        kernel,
        out_shape=outs,
        in_specs=[
            pl.BlockSpec(memory_space=where.get(i, pltpu.VMEM)) for i in range(len(args))
        ],
        out_specs=[pl.BlockSpec(memory_space=pltpu.VMEM)] * len(outs),
        scratch_shapes=scratch,
        compiler_params=pltpu.CompilerParams(vmem_limit_bytes=grant * 1024 * 1024),
        cost_estimate=pl.CostEstimate(
            flops=weight, bytes_accessed=1, transcendentals=0
        ),
        name=name,
    )(*args)


def body(hidden, expert_ids, gate_fix, grad_out, w_down):
    tokens, top, ff = hidden.shape
    half = grad_out.shape[1]
    local, _, full = w_down.shape
    n = lax.axis_size("ctx")
    experts = n * local
    assigned = tokens * top
    cap = min(tokens, assigned // experts + max(1, assigned // (8 * experts)))
    unit = 8 if local % 2 == 0 else 16
    cap = -(-cap // unit) * unit
    width = local * cap
    dims = (experts, local, cap, width)
    run = functools.partial(call, grant=24 if n <= 4 else 56)
    place = jnp.stack([lax.axis_index("ctx"), lax.axis_index("tp")]).astype(jnp.int32)
    placed = {0: pltpu.SMEM}

    def send(x, s):
        return lax.ppermute(x, "ctx", [(i, i ^ s) for i in range(n)]) if s else x

    def swap(x):
        return lax.ppermute(x, "tp", [(0, 1), (1, 0)])

    meta = jnp.concatenate([expert_ids.T, gate_fix.T], axis=0)
    hid_t = hidden.transpose(1, 2, 0)
    named = jnp.pad(expert_ids.T.astype(BF16), ((0, 8 - top), (0, half - tokens)))
    packed = jnp.concatenate([grad_out, named], axis=0)
    forward = n == 4
    near = 3 if forward else n
    own = [send(packed, s) for s in range(near)]
    swapped = swap(packed)
    if TIE_OWN:
        meta, swapped = lax.optimization_barrier((meta, swapped))
    hid_sent = run(
        functools.partial(dispatch_kernel, dims), [shaped((width, -(-(ff + 1) // 128) * 128))] * n,
        [place, meta, hid_t], where=placed, name="dispatch",
    )
    hid = [send(hid_sent[s], s) for s in range(n)]
    for s in range(1, near):
        own[s], hid[0] = lax.optimization_barrier((own[s], hid[0]))
    if forward:
        cut = half // 2
        low, high = run(pass_kernel, [shaped((tokens + 8, cut))] * 2, own[1:], name="pass")
        own += [send(low, 2), send(high, 1)]
    other = [swapped] + [swap(x) for x in own[1:near]]
    if forward:
        *own[3:], other[1], other[2] = lax.optimization_barrier((*own[3:], other[1], other[2]))
        other += [swap(x) for x in own[3:]]

    slot = shaped((width, ff))
    x, held = run(
        functools.partial(gather_kernel, dims, top),
        [shaped((local, n * cap, half)), shaped((n, width, tokens))],
        [place, *own], where=placed, name="gather", weight=W_GATHER,
    )
    grad_sent = run(
        functools.partial(grad_kernel, dims), [slot] * n,
        [place, *other, x, held, w_down], where=placed,
        scratch=[pltpu.VMEM((local, n * cap, half), BF16)], name="grad",
    )
    hid[0], grad_own = lax.optimization_barrier((hid[0], grad_sent[0]))
    grad_back = [grad_own] + [send(grad_sent[s], s) for s in range(1, n)]

    (theirs,) = run(
        functools.partial(mix_kernel, dims, True), [shaped((n * tokens, half))],
        [place, *hid, w_down], where=placed, name="mix_sibling",
    )
    arrived = swap(theirs)
    if forward:
        (mine,) = run(
            functools.partial(mix_kernel, dims, False), [shaped((n * tokens, half), F32)],
            [place, *hid, w_down], where=placed, name="mix_own", weight=BIG,
        )
        block, piece = shaped((tokens, half), F32), shaped((tokens, cut))
        kept, one, two, one_low, two_high = run(
            add_split_kernel, [block] * 3 + [piece] * 2, [mine, arrived], name="add"
        )
        one_low, two_high = send(one_low, 1), send(two_high, 2)
        to_one, to_two = run(
            join_kernel, [shaped((tokens, half))] * 2, [one, two, one_low, two_high],
            name="join",
        )
        parts = [kept, send(to_one, 1), send(to_two, 2)]
    else:
        sums = run(
            functools.partial(mix_add_kernel, dims), [shaped((tokens, half))] * n,
            [place, *hid, w_down, arrived], where=placed, name="mix_own",
        )
        parts = [send(sums[s], s) for s in range(n)]

    (grad_t,) = run(
        functools.partial(restore_kernel, dims), [shaped((top, ff, tokens))],
        [place, meta, *grad_back], where=placed, name="restore", weight=BIG,
    )
    mixed = sum(x.astype(F32) for x in parts).astype(BF16)
    return mixed, grad_t.transpose(2, 0, 1)


def solution(mesh):
    placed = (
        P(("ctx", "exp"), None, "tp"),
        P(("ctx", "exp"), None),
        P(("ctx", "exp"), None),
        P(("ctx", "exp"), "tp"),
        P("ctx", "tp", None),
    )
    return jax.shard_map(
        body,
        mesh=mesh,
        in_specs=placed,
        out_specs=(P(("ctx", "exp"), "tp"), P(("ctx", "exp"), None, "tp")),
        check_vma=False,
    )
```

```python
import functools

import jax
import jax.numpy as jnp
from jax import lax
from jax.experimental import pallas as pl
from jax.experimental.pallas import tpu as pltpu
from jax.sharding import PartitionSpec as P

BF16 = jnp.bfloat16
F32 = jnp.float32
NN = (((1,), (0,)), ((), ()))
NT = (((1,), (1,)), ((), ()))
TN = (((0,), (0,)), ((), ()))
BIG = 10**11


def dot(a, b, dims):
    return lax.dot_general(a, b, dims, preferred_element_type=F32)


def iota(shape, axis):
    return lax.broadcasted_iota(jnp.int32, shape, axis)


def ones_where(mask):
    return mask.astype(F32).astype(BF16)


def earlier(tokens):
    return ones_where(iota((tokens, tokens), 0) < iota((tokens, tokens), 1))


def token_slots(ids, me, experts, local, cap, width):
    top, tokens = ids.shape
    row = iota((experts, tokens), 0)
    hits = [ids[k : k + 1, :] == row for k in range(top)]
    named = functools.reduce(jnp.logical_or, hits)
    before = dot(ones_where(named), earlier(tokens), NN)
    base = jnp.bitwise_xor(row // local, me) * width + lax.rem(row, local) * cap
    slot = before + base.astype(F32)
    return [
        jnp.sum(jnp.where(hit, slot, 0.0), axis=0, keepdims=True).astype(jnp.int32)
        for hit in hits
    ]


def named_here(ids, me, local):
    top, tokens = ids.shape
    row = iota((8, tokens), 0) + me * local
    return functools.reduce(
        jnp.logical_or, [ids[k : k + 1, :] == row for k in range(top)]
    )


def slots_by_lane(ids, me, local, cap, width):
    tokens = ids.shape[1]
    named = named_here(ids, me, local)
    before = dot(ones_where(named), earlier(tokens), NN)
    slot = before.astype(jnp.int32) + iota((8, tokens), 0) * cap
    slot = jnp.where(named, slot, -1)
    rows = iota((cap, tokens), 0)
    return [ones_where(rows + l * cap == slot[l : l + 1, :]) for l in range(local)]


def picks_of(meta, me, dims):
    experts, local, cap, width = dims
    top = meta.shape[0] // 2
    slots = token_slots(meta[:top], me, experts, local, cap, width)
    rows = iota((experts // local * width, meta.shape[1]), 0)
    picks = jnp.concatenate([ones_where(rows == slot) for slot in slots], axis=1)
    return picks, meta[top:].astype(F32) * (1.0 / 65536.0)


def dispatch_kernel(dims, place, meta_ref, hid_ref, *outs):
    width = outs[0].shape[0]
    picks, gate = picks_of(meta_ref[...], place[0], dims)
    scaled = [
        (hid_ref[k].astype(F32) * gate[k : k + 1, :]).astype(BF16)
        for k in range(hid_ref.shape[0])
    ]
    rows = jnp.concatenate(scaled, axis=1)
    spare = outs[0].shape[1] - rows.shape[0]
    tokens = hid_ref.shape[2]
    number = jnp.bitwise_and(iota((spare, rows.shape[1]), 1), tokens - 1) + 1
    number = jnp.where(iota(number.shape, 0) == 0, number.astype(F32), 0.0)
    sent = dot(picks, jnp.concatenate([rows, number.astype(BF16)], axis=0), NT)
    for s, out in enumerate(outs):
        out[...] = sent[s * width : (s + 1) * width].astype(BF16)


def by_expert(rows, local, cap):
    return [
        jnp.concatenate([r[l * cap : (l + 1) * cap] for r in rows], axis=0)
        for l in range(local)
    ]


def by_source(rows, count, cap):
    return [
        jnp.concatenate([r[s * cap : (s + 1) * cap] for r in rows], axis=0)
        for s in range(count)
    ]


def routes(dims, top, me, packed, tokens):
    experts, local, cap, width = dims
    ids = packed[tokens:, :tokens].astype(F32).astype(jnp.int32)[:top]
    return jnp.concatenate(slots_by_lane(ids, me, local, cap, width), axis=0)


def gather_rows(dims, held, halves, x_ref):
    experts, local, cap, width = dims
    tokens, half = held[0].shape[1], halves[0].shape[1]
    chunk = min(half, 512)
    for c in range(0, half, chunk):
        rows = [dot(h, ref[:tokens, c : c + chunk], NN) for h, ref in zip(held, halves)]
        for l, x in enumerate(by_expert(rows, local, cap)):
            x_ref[l, :, c : c + chunk] = x.astype(BF16)


def gather_kernel(dims, top, place, *refs):
    experts, local, cap, width = dims
    own, x_ref = refs[:-1], refs[-1]
    half = own[0].shape[1]
    tokens = own[0].shape[0] - 8
    chunk = min(half, 512)
    held = []
    for ref in own:
        ids = ref[tokens:, :tokens].astype(F32).astype(jnp.int32)[:top]
        held.append(
            jnp.concatenate(slots_by_lane(ids, place[0], local, cap, width), axis=0)
        )
    for c in range(0, half, chunk):
        rows = [dot(h, ref[:tokens, c : c + chunk], NN) for h, ref in zip(held, own)]
        for l, x in enumerate(by_expert(rows, local, cap)):
            x_ref[l, :, c : c + chunk] = x.astype(BF16)


def grad_kernel(dims, place, x_ref, x_other, w_ref, *outs):
    experts, local, cap, width = dims
    half = x_ref.shape[2]
    mine = pl.ds(pl.multiple_of(place[1] * half, half), half)
    theirs = pl.ds(pl.multiple_of((1 - place[1]) * half, half), half)
    grads = [
        dot(x_ref[l], w_ref[l, :, mine], NT) + dot(x_other[l], w_ref[l, :, theirs], NT)
        for l in range(local)
    ]
    for s, rows in enumerate(by_source(grads, len(outs), cap)):
        outs[s][...] = rows.astype(BF16)


def mix_rows(dims, side, hid, w_ref, tokens, half, store):
    experts, local, cap, width = dims
    n = len(hid)
    ff = w_ref.shape[1]
    chunk = min(half, 256)
    same = ones_where(iota((tokens, tokens), 0) == iota((tokens, tokens), 1))
    held = []
    for h in hid:
        number = h[:, ff : ff + 1].astype(F32).astype(jnp.int32) - 1
        slots = ones_where(iota((width, tokens), 1) == number)
        held.append(dot(same, slots, NT).astype(BF16))
    rows = [h[:, :ff].astype(F32) for h in hid]
    x = [r.astype(BF16) for r in by_expert(rows, local, cap)]
    for c in range(0, half, chunk):
        at = pl.ds(pl.multiple_of(side * half + c, chunk), chunk)
        out = [dot(x[l], w_ref[l, :, at], NN) for l in range(local)]
        for s, rows in enumerate(by_source(out, n, cap)):
            store(s, slice(c, c + chunk), dot(held[s], rows.astype(BF16), NN))


def mix_kernel(dims, sibling, place, *refs):
    hid, (w_ref, out) = refs[:-2], refs[-2:]
    tokens = out.shape[0] // len(hid)

    def store(s, columns, part):
        out[pl.ds(s * tokens, tokens), columns] = part.astype(out.dtype)

    side = 1 - place[1] if sibling else place[1]
    mix_rows(dims, side, hid, w_ref, tokens, out.shape[1], store)


def mix_add_kernel(dims, place, *refs):
    n = (len(refs) - 2) // 2
    hid, (w_ref, arrived), outs = refs[:n], refs[n : n + 2], refs[n + 2 :]
    tokens, half = outs[0].shape

    def store(s, columns, part):
        theirs = arrived[pl.ds(s * tokens, tokens), columns].astype(F32)
        outs[s][:, columns] = (part + theirs).astype(BF16)

    mix_rows(dims, place[1], hid, w_ref, tokens, half, store)


def add_split_kernel(own, arrived, mine, one, two, low, high):
    tokens, half = mine.shape
    cut = half // 2
    for s, out in enumerate((mine, one, two)):
        at = pl.ds(s * tokens, tokens)
        out[...] = own[at, :] + arrived[at, :].astype(F32)
    at = pl.ds(3 * tokens, tokens)
    far = own[at, :] + arrived[at, :].astype(F32)
    low[...] = far[:, :cut].astype(BF16)
    high[...] = far[:, cut:].astype(BF16)


def join_kernel(one, two, low, high, to_one, to_two):
    cut = one.shape[1] // 2
    to_one[:, :cut] = one[:, :cut].astype(BF16)
    to_one[:, cut:] = (one[:, cut:] + high[...].astype(F32)).astype(BF16)
    to_two[:, :cut] = (two[:, :cut] + low[...].astype(F32)).astype(BF16)
    to_two[:, cut:] = two[:, cut:].astype(BF16)


def restore_kernel(dims, place, meta_ref, *refs):
    back_refs, out = refs[:-1], refs[-1]
    top, _, tokens = out.shape
    picks, gate = picks_of(meta_ref[...], place[0], dims)
    back = jnp.concatenate([ref[...] for ref in back_refs], axis=0)
    grads = dot(back, picks, TN)
    for k in range(top):
        out[k] = (grads[:, k * tokens : (k + 1) * tokens] * gate[k : k + 1, :]).astype(BF16)


def shaped(shape, dtype=BF16):
    return jax.ShapeDtypeStruct(shape, dtype)


def call(kernel, outs, args, where=(), scratch=(), grant=24, weight=1, name=None):
    where = dict(where)
    return pl.pallas_call(
        kernel,
        out_shape=outs,
        in_specs=[
            pl.BlockSpec(memory_space=where.get(i, pltpu.VMEM)) for i in range(len(args))
        ],
        out_specs=[pl.BlockSpec(memory_space=pltpu.VMEM)] * len(outs),
        scratch_shapes=scratch,
        compiler_params=pltpu.CompilerParams(vmem_limit_bytes=grant * 1024 * 1024),
        cost_estimate=pl.CostEstimate(
            flops=weight, bytes_accessed=1, transcendentals=0
        ),
        name=name,
    )(*args)


def body(hidden, expert_ids, gate_fix, grad_out, w_down):
    tokens, top, ff = hidden.shape
    half = grad_out.shape[1]
    local, _, full = w_down.shape
    n = lax.axis_size("ctx")
    experts = n * local
    assigned = tokens * top
    cap = min(tokens, assigned // experts + max(1, assigned // (8 * experts)))
    unit = 8 if local % 2 == 0 else 16
    cap = -(-cap // unit) * unit
    width = local * cap
    dims = (experts, local, cap, width)
    run = functools.partial(call, grant=24 if n <= 4 else 56)
    place = jnp.stack([lax.axis_index("ctx"), lax.axis_index("tp")]).astype(jnp.int32)
    placed = {0: pltpu.SMEM}

    def send(x, s):
        return lax.ppermute(x, "ctx", [(i, i ^ s) for i in range(n)]) if s else x

    def swap(x):
        return lax.ppermute(x, "tp", [(0, 1), (1, 0)])

    meta = jnp.concatenate([expert_ids.T, gate_fix.T], axis=0)
    hid_t = hidden.transpose(1, 2, 0)
    named = jnp.pad(expert_ids.T.astype(BF16), ((0, 8 - top), (0, half - tokens)))
    packed = jnp.concatenate([grad_out, named], axis=0)
    forward = n == 4
    own = [send(packed, s) for s in range(n)]
    hid_sent = run(
        functools.partial(dispatch_kernel, dims), [shaped((width, -(-(ff + 1) // 128) * 128))] * n,
        [place, meta, hid_t], where=placed, name="dispatch",
    )
    hid = [send(hid_sent[s], s) for s in range(n)]
    slot = shaped((width, ff))

    def taken(own, w_down):
        (x,) = run(
            functools.partial(gather_kernel, dims, top),
            [shaped((local, n * cap, half))], [place, *own], where=placed, name="gather",
        )
        return list(run(
            functools.partial(grad_kernel, dims), [slot] * n,
            [place, x, swap(x), w_down], where=placed, name="grad",
        ))

    def skipped(own, w_down):
        return [jnp.zeros((width, ff), BF16)] * n

    grad_sent = lax.cond(
        place[0] < 1000, taken, skipped, own, w_down
    )
    hid[0], grad_own = lax.optimization_barrier((hid[0], grad_sent[0]))
    grad_back = [grad_own] + [send(grad_sent[s], s) for s in range(1, n)]

    (theirs,) = run(
        functools.partial(mix_kernel, dims, True), [shaped((n * tokens, half))],
        [place, *hid, w_down], where=placed, name="mix_sibling",
    )
    arrived = swap(theirs)
    if forward:
        (mine,) = run(
            functools.partial(mix_kernel, dims, False), [shaped((n * tokens, half), F32)],
            [place, *hid, w_down], where=placed, name="mix_own", weight=BIG,
        )
        cut = half // 2
        block, piece = shaped((tokens, half), F32), shaped((tokens, cut))
        kept, one, two, one_low, two_high = run(
            add_split_kernel, [block] * 3 + [piece] * 2, [mine, arrived], name="add"
        )
        one_low, two_high = send(one_low, 1), send(two_high, 2)
        to_one, to_two = run(
            join_kernel, [shaped((tokens, half))] * 2, [one, two, one_low, two_high],
            name="join",
        )
        parts = [kept, send(to_one, 1), send(to_two, 2)]
    else:
        sums = run(
            functools.partial(mix_add_kernel, dims), [shaped((tokens, half))] * n,
            [place, *hid, w_down, arrived], where=placed, name="mix_own",
        )
        parts = [send(sums[s], s) for s in range(n)]

    (grad_t,) = run(
        functools.partial(restore_kernel, dims), [shaped((top, ff, tokens))],
        [place, meta, *grad_back], where=placed, name="restore", weight=BIG,
    )
    mixed = sum(x.astype(F32) for x in parts).astype(BF16)
    return mixed, grad_t.transpose(2, 0, 1)


def solution(mesh):
    placed = (
        P(("ctx", "exp"), None, "tp"),
        P(("ctx", "exp"), None),
        P(("ctx", "exp"), None),
        P(("ctx", "exp"), "tp"),
        P("ctx", "tp", None),
    )
    return jax.shard_map(
        body,
        mesh=mesh,
        in_specs=placed,
        out_specs=(P(("ctx", "exp"), "tp"), P(("ctx", "exp"), None, "tp")),
        check_vma=False,
    )
```

```python
import functools

import jax
import jax.numpy as jnp
from jax import lax
from jax.experimental import pallas as pl
from jax.experimental.pallas import tpu as pltpu
from jax.sharding import PartitionSpec as P

BF16 = jnp.bfloat16
F32 = jnp.float32
NN = (((1,), (0,)), ((), ()))
NT = (((1,), (1,)), ((), ()))
TN = (((0,), (0,)), ((), ()))
BIG = 10**11


def dot(a, b, dims):
    return lax.dot_general(a, b, dims, preferred_element_type=F32)


def iota(shape, axis):
    return lax.broadcasted_iota(jnp.int32, shape, axis)


def ones_where(mask):
    return mask.astype(F32).astype(BF16)


def earlier(tokens):
    return ones_where(iota((tokens, tokens), 0) < iota((tokens, tokens), 1))


def token_slots(ids, me, experts, local, cap, width):
    top, tokens = ids.shape
    row = iota((experts, tokens), 0)
    hits = [ids[k : k + 1, :] == row for k in range(top)]
    named = functools.reduce(jnp.logical_or, hits)
    before = dot(ones_where(named), earlier(tokens), NN)
    base = jnp.bitwise_xor(row // local, me) * width + lax.rem(row, local) * cap
    slot = before + base.astype(F32)
    return [
        jnp.sum(jnp.where(hit, slot, 0.0), axis=0, keepdims=True).astype(jnp.int32)
        for hit in hits
    ]


def named_here(ids, me, local):
    top, tokens = ids.shape
    row = iota((8, tokens), 0) + me * local
    return functools.reduce(
        jnp.logical_or, [ids[k : k + 1, :] == row for k in range(top)]
    )


def slots_by_lane(ids, me, local, cap, width):
    tokens = ids.shape[1]
    named = named_here(ids, me, local)
    before = dot(ones_where(named), earlier(tokens), NN)
    slot = before.astype(jnp.int32) + iota((8, tokens), 0) * cap
    slot = jnp.where(named, slot, -1)
    rows = iota((cap, tokens), 0)
    return [ones_where(rows + l * cap == slot[l : l + 1, :]) for l in range(local)]


def picks_of(meta, me, dims):
    experts, local, cap, width = dims
    top = meta.shape[0] // 2
    slots = token_slots(meta[:top], me, experts, local, cap, width)
    rows = iota((experts // local * width, meta.shape[1]), 0)
    picks = jnp.concatenate([ones_where(rows == slot) for slot in slots], axis=1)
    return picks, meta[top:].astype(F32) * (1.0 / 65536.0)


def dispatch_kernel(dims, place, meta_ref, hid_ref, *outs):
    width = outs[0].shape[0]
    picks, gate = picks_of(meta_ref[...], place[0], dims)
    scaled = [
        (hid_ref[k].astype(F32) * gate[k : k + 1, :]).astype(BF16)
        for k in range(hid_ref.shape[0])
    ]
    rows = jnp.concatenate(scaled, axis=1)
    spare = outs[0].shape[1] - rows.shape[0]
    tokens = hid_ref.shape[2]
    number = jnp.bitwise_and(iota((spare, rows.shape[1]), 1), tokens - 1) + 1
    number = jnp.where(iota(number.shape, 0) == 0, number.astype(F32), 0.0)
    sent = dot(picks, jnp.concatenate([rows, number.astype(BF16)], axis=0), NT)
    for s, out in enumerate(outs):
        out[...] = sent[s * width : (s + 1) * width].astype(BF16)


def load_kernel(w_in, w_ref):
    local, ff, _ = w_in.shape
    step = 64 if ff % 64 == 0 else ff
    for l in range(local):
        for i in range(0, ff, step):
            w_ref[l, i : i + step, :] = w_in[l, i : i + step, :]


def by_expert(rows, local, cap):
    return [
        jnp.concatenate([r[l * cap : (l + 1) * cap] for r in rows], axis=0)
        for l in range(local)
    ]


def by_source(rows, count, cap):
    return [
        jnp.concatenate([r[s * cap : (s + 1) * cap] for r in rows], axis=0)
        for s in range(count)
    ]


def routes(dims, top, me, packed, tokens):
    experts, local, cap, width = dims
    ids = packed[tokens:, :tokens].astype(F32).astype(jnp.int32)[:top]
    return jnp.concatenate(slots_by_lane(ids, me, local, cap, width), axis=0)


def gather_rows(dims, held, halves, x_ref):
    experts, local, cap, width = dims
    tokens, half = held[0].shape[1], halves[0].shape[1]
    chunk = min(half, 512)
    for c in range(0, half, chunk):
        rows = [dot(h, ref[:tokens, c : c + chunk], NN) for h, ref in zip(held, halves)]
        for l, x in enumerate(by_expert(rows, local, cap)):
            x_ref[l, :, c : c + chunk] = x.astype(BF16)


def gather_kernel(dims, top, place, *refs):
    experts, local, cap, width = dims
    own, x_ref = refs[:-1], refs[-1]
    half = own[0].shape[1]
    tokens = own[0].shape[0] - 8
    chunk = min(half, 512)
    held = []
    for ref in own:
        ids = ref[tokens:, :tokens].astype(F32).astype(jnp.int32)[:top]
        held.append(
            jnp.concatenate(slots_by_lane(ids, place[0], local, cap, width), axis=0)
        )
    for c in range(0, half, chunk):
        rows = [dot(h, ref[:tokens, c : c + chunk], NN) for h, ref in zip(held, own)]
        for l, x in enumerate(by_expert(rows, local, cap)):
            x_ref[l, :, c : c + chunk] = x.astype(BF16)


def grad_kernel(dims, place, x_ref, x_other, w_ref, *outs):
    experts, local, cap, width = dims
    half = x_ref.shape[2]
    mine = pl.ds(pl.multiple_of(place[1] * half, half), half)
    theirs = pl.ds(pl.multiple_of((1 - place[1]) * half, half), half)
    grads = [
        dot(x_ref[l], w_ref[l, :, mine], NT) + dot(x_other[l], w_ref[l, :, theirs], NT)
        for l in range(local)
    ]
    for s, rows in enumerate(by_source(grads, len(outs), cap)):
        outs[s][...] = rows.astype(BF16)


def mix_rows(dims, side, hid, w_ref, tokens, half, store):
    experts, local, cap, width = dims
    n = len(hid)
    ff = w_ref.shape[1]
    chunk = min(half, 256)
    same = ones_where(iota((tokens, tokens), 0) == iota((tokens, tokens), 1))
    held = []
    for h in hid:
        number = h[:, ff : ff + 1].astype(F32).astype(jnp.int32) - 1
        slots = ones_where(iota((width, tokens), 1) == number)
        held.append(dot(same, slots, NT).astype(BF16))
    rows = [h[:, :ff].astype(F32) for h in hid]
    x = [r.astype(BF16) for r in by_expert(rows, local, cap)]
    for c in range(0, half, chunk):
        at = pl.ds(pl.multiple_of(side * half + c, chunk), chunk)
        out = [dot(x[l], w_ref[l, :, at], NN) for l in range(local)]
        for s, rows in enumerate(by_source(out, n, cap)):
            store(s, slice(c, c + chunk), dot(held[s], rows.astype(BF16), NN))


def mix_kernel(dims, sibling, place, *refs):
    hid, (w_ref, out) = refs[:-2], refs[-2:]
    tokens = out.shape[0] // len(hid)

    def store(s, columns, part):
        out[pl.ds(s * tokens, tokens), columns] = part.astype(out.dtype)

    side = 1 - place[1] if sibling else place[1]
    mix_rows(dims, side, hid, w_ref, tokens, out.shape[1], store)


def mix_add_kernel(dims, place, *refs):
    n = (len(refs) - 2) // 2
    hid, (w_ref, arrived), outs = refs[:n], refs[n : n + 2], refs[n + 2 :]
    tokens, half = outs[0].shape

    def store(s, columns, part):
        theirs = arrived[pl.ds(s * tokens, tokens), columns].astype(F32)
        outs[s][:, columns] = (part + theirs).astype(BF16)

    mix_rows(dims, place[1], hid, w_ref, tokens, half, store)


def add_split_kernel(own, arrived, mine, one, two, low, high):
    tokens, half = mine.shape
    cut = half // 2
    for s, out in enumerate((mine, one, two)):
        at = pl.ds(s * tokens, tokens)
        out[...] = own[at, :] + arrived[at, :].astype(F32)
    at = pl.ds(3 * tokens, tokens)
    far = own[at, :] + arrived[at, :].astype(F32)
    low[...] = far[:, :cut].astype(BF16)
    high[...] = far[:, cut:].astype(BF16)


def join_kernel(one, two, low, high, to_one, to_two):
    cut = one.shape[1] // 2
    to_one[:, :cut] = one[:, :cut].astype(BF16)
    to_one[:, cut:] = (one[:, cut:] + high[...].astype(F32)).astype(BF16)
    to_two[:, :cut] = (two[:, :cut] + low[...].astype(F32)).astype(BF16)
    to_two[:, cut:] = two[:, cut:].astype(BF16)


def restore_kernel(dims, place, meta_ref, *refs):
    back_refs, out = refs[:-1], refs[-1]
    top, _, tokens = out.shape
    picks, gate = picks_of(meta_ref[...], place[0], dims)
    back = jnp.concatenate([ref[...] for ref in back_refs], axis=0)
    grads = dot(back, picks, TN)
    for k in range(top):
        out[k] = (grads[:, k * tokens : (k + 1) * tokens] * gate[k : k + 1, :]).astype(BF16)


def shaped(shape, dtype=BF16):
    return jax.ShapeDtypeStruct(shape, dtype)


def call(kernel, outs, args, where=(), scratch=(), grant=24, weight=1, name=None):
    where = dict(where)
    return pl.pallas_call(
        kernel,
        out_shape=outs,
        in_specs=[
            pl.BlockSpec(memory_space=where.get(i, pltpu.VMEM)) for i in range(len(args))
        ],
        out_specs=[pl.BlockSpec(memory_space=pltpu.VMEM)] * len(outs),
        scratch_shapes=scratch,
        compiler_params=pltpu.CompilerParams(vmem_limit_bytes=grant * 1024 * 1024),
        cost_estimate=pl.CostEstimate(
            flops=weight, bytes_accessed=1, transcendentals=0
        ),
        name=name,
    )(*args)


def body(hidden, expert_ids, gate_fix, grad_out, w_down):
    tokens, top, ff = hidden.shape
    half = grad_out.shape[1]
    local, _, full = w_down.shape
    n = lax.axis_size("ctx")
    experts = n * local
    assigned = tokens * top
    cap = min(tokens, assigned // experts + max(1, assigned // (8 * experts)))
    unit = 8 if local % 2 == 0 else 16
    cap = -(-cap // unit) * unit
    width = local * cap
    dims = (experts, local, cap, width)
    run = functools.partial(call, grant=24 if n <= 4 else 56)
    place = jnp.stack([lax.axis_index("ctx"), lax.axis_index("tp")]).astype(jnp.int32)
    placed = {0: pltpu.SMEM}

    def send(x, s):
        return lax.ppermute(x, "ctx", [(i, i ^ s) for i in range(n)]) if s else x

    def swap(x):
        return lax.ppermute(x, "tp", [(0, 1), (1, 0)])

    meta = jnp.concatenate([expert_ids.T, gate_fix.T], axis=0)
    hid_t = hidden.transpose(1, 2, 0)
    named = jnp.pad(expert_ids.T.astype(BF16), ((0, 8 - top), (0, half - tokens)))
    packed = jnp.concatenate([grad_out, named], axis=0)
    forward = n == 4
    own = [send(packed, s) for s in range(n)]
    hid_sent = run(
        functools.partial(dispatch_kernel, dims), [shaped((width, -(-(ff + 1) // 128) * 128))] * n,
        [place, meta, hid_t], where=placed, name="dispatch",
    )
    hid = [send(hid_sent[s], s) for s in range(n)]
    slot = shaped((width, ff))
    if n == 4:
        w_down, hid[0] = lax.optimization_barrier((w_down, hid[0]))
        (w_down,) = run(
            load_kernel, [shaped(w_down.shape)], [w_down], name="load"
        )

    def taken(own, w_down):
        (x,) = run(
            functools.partial(gather_kernel, dims, top),
            [shaped((local, n * cap, half))], [place, *own], where=placed, name="gather",
        )
        return list(run(
            functools.partial(grad_kernel, dims), [slot] * n,
            [place, x, swap(x), w_down], where=placed, name="grad",
        ))

    def skipped(own, w_down):
        return [jnp.zeros((width, ff), BF16)] * n

    grad_sent = lax.cond(
        place[0] < 1000, taken, skipped, own, w_down
    )
    hid[0], grad_own = lax.optimization_barrier((hid[0], grad_sent[0]))
    grad_back = [grad_own] + [send(grad_sent[s], s) for s in range(1, n)]

    (theirs,) = run(
        functools.partial(mix_kernel, dims, True), [shaped((n * tokens, half))],
        [place, *hid, w_down], where=placed, name="mix_sibling",
    )
    arrived = swap(theirs)
    if forward:
        (mine,) = run(
            functools.partial(mix_kernel, dims, False), [shaped((n * tokens, half), F32)],
            [place, *hid, w_down], where=placed, name="mix_own", weight=BIG,
        )
        cut = half // 2
        block, piece = shaped((tokens, half), F32), shaped((tokens, cut))
        kept, one, two, one_low, two_high = run(
            add_split_kernel, [block] * 3 + [piece] * 2, [mine, arrived], name="add"
        )
        one_low, two_high = send(one_low, 1), send(two_high, 2)
        to_one, to_two = run(
            join_kernel, [shaped((tokens, half))] * 2, [one, two, one_low, two_high],
            name="join",
        )
        parts = [kept, send(to_one, 1), send(to_two, 2)]
    else:
        sums = run(
            functools.partial(mix_add_kernel, dims), [shaped((tokens, half))] * n,
            [place, *hid, w_down, arrived], where=placed, name="mix_own",
        )
        parts = [send(sums[s], s) for s in range(n)]

    (grad_t,) = run(
        functools.partial(restore_kernel, dims), [shaped((top, ff, tokens))],
        [place, meta, *grad_back], where=placed, name="restore", weight=BIG,
    )
    mixed = sum(x.astype(F32) for x in parts).astype(BF16)
    return mixed, grad_t.transpose(2, 0, 1)


def solution(mesh):
    placed = (
        P(("ctx", "exp"), None, "tp"),
        P(("ctx", "exp"), None),
        P(("ctx", "exp"), None),
        P(("ctx", "exp"), "tp"),
        P("ctx", "tp", None),
    )
    return jax.shard_map(
        body,
        mesh=mesh,
        in_specs=placed,
        out_specs=(P(("ctx", "exp"), "tp"), P(("ctx", "exp"), None, "tp")),
        check_vma=False,
    )
```

```python
import functools

import jax
import jax.numpy as jnp
from jax import lax
from jax.experimental import pallas as pl
from jax.experimental.pallas import tpu as pltpu
from jax.sharding import PartitionSpec as P

BF16 = jnp.bfloat16
F32 = jnp.float32
NN = (((1,), (0,)), ((), ()))
NT = (((1,), (1,)), ((), ()))
TN = (((0,), (0,)), ((), ()))
BIG = 10**11


def dot(a, b, dims):
    return lax.dot_general(a, b, dims, preferred_element_type=F32)


def iota(shape, axis):
    return lax.broadcasted_iota(jnp.int32, shape, axis)


def ones_where(mask):
    return mask.astype(F32).astype(BF16)


def earlier(tokens):
    return ones_where(iota((tokens, tokens), 0) < iota((tokens, tokens), 1))


def token_slots(ids, me, experts, local, cap, width):
    top, tokens = ids.shape
    row = iota((experts, tokens), 0)
    hits = [ids[k : k + 1, :] == row for k in range(top)]
    named = functools.reduce(jnp.logical_or, hits)
    before = dot(ones_where(named), earlier(tokens), NN)
    base = jnp.bitwise_xor(row // local, me) * width + lax.rem(row, local) * cap
    slot = before + base.astype(F32)
    return [
        jnp.sum(jnp.where(hit, slot, 0.0), axis=0, keepdims=True).astype(jnp.int32)
        for hit in hits
    ]


def named_here(ids, me, local):
    top, tokens = ids.shape
    row = iota((8, tokens), 0) + me * local
    return functools.reduce(
        jnp.logical_or, [ids[k : k + 1, :] == row for k in range(top)]
    )


def slots_by_lane(ids, me, local, cap, width):
    tokens = ids.shape[1]
    named = named_here(ids, me, local)
    before = dot(ones_where(named), earlier(tokens), NN)
    slot = before.astype(jnp.int32) + iota((8, tokens), 0) * cap
    slot = jnp.where(named, slot, -1)
    rows = iota((cap, tokens), 0)
    return [ones_where(rows + l * cap == slot[l : l + 1, :]) for l in range(local)]


def picks_of(meta, me, dims):
    experts, local, cap, width = dims
    top = meta.shape[0] // 2
    slots = token_slots(meta[:top], me, experts, local, cap, width)
    rows = iota((experts // local * width, meta.shape[1]), 0)
    picks = jnp.concatenate([ones_where(rows == slot) for slot in slots], axis=1)
    return picks, meta[top:].astype(F32) * (1.0 / 65536.0)


def dispatch_kernel(dims, place, meta_ref, hid_ref, *outs):
    width = outs[0].shape[0]
    picks, gate = picks_of(meta_ref[...], place[0], dims)
    scaled = [
        (hid_ref[k].astype(F32) * gate[k : k + 1, :]).astype(BF16)
        for k in range(hid_ref.shape[0])
    ]
    rows = jnp.concatenate(scaled, axis=1)
    spare = outs[0].shape[1] - rows.shape[0]
    tokens = hid_ref.shape[2]
    number = jnp.bitwise_and(iota((spare, rows.shape[1]), 1), tokens - 1) + 1
    number = jnp.where(iota(number.shape, 0) == 0, number.astype(F32), 0.0)
    sent = dot(picks, jnp.concatenate([rows, number.astype(BF16)], axis=0), NT)
    for s, out in enumerate(outs):
        out[...] = sent[s * width : (s + 1) * width].astype(BF16)


def by_expert(rows, local, cap):
    return [
        jnp.concatenate([r[l * cap : (l + 1) * cap] for r in rows], axis=0)
        for l in range(local)
    ]


def by_source(rows, count, cap):
    return [
        jnp.concatenate([r[s * cap : (s + 1) * cap] for r in rows], axis=0)
        for s in range(count)
    ]


def routes(dims, top, me, packed, tokens):
    experts, local, cap, width = dims
    ids = packed[tokens:, :tokens].astype(F32).astype(jnp.int32)[:top]
    return jnp.concatenate(slots_by_lane(ids, me, local, cap, width), axis=0)


def gather_rows(dims, held, halves, x_ref):
    experts, local, cap, width = dims
    tokens, half = held[0].shape[1], halves[0].shape[1]
    chunk = min(half, 512)
    for c in range(0, half, chunk):
        rows = [dot(h, ref[:tokens, c : c + chunk], NN) for h, ref in zip(held, halves)]
        for l, x in enumerate(by_expert(rows, local, cap)):
            x_ref[l, :, c : c + chunk] = x.astype(BF16)


def gather_kernel(dims, top, place, *refs):
    experts, local, cap, width = dims
    own, x_ref = refs[:-1], refs[-1]
    half = own[0].shape[1]
    tokens = own[0].shape[0] - 8
    chunk = min(half, 512)
    held = []
    for ref in own:
        ids = ref[tokens:, :tokens].astype(F32).astype(jnp.int32)[:top]
        held.append(
            jnp.concatenate(slots_by_lane(ids, place[0], local, cap, width), axis=0)
        )
    for c in range(0, half, chunk):
        rows = [dot(h, ref[:tokens, c : c + chunk], NN) for h, ref in zip(held, own)]
        for l, x in enumerate(by_expert(rows, local, cap)):
            x_ref[l, :, c : c + chunk] = x.astype(BF16)


def pieces_of(size, step):
    return [(i, min(step, size - i)) for i in range(0, size, step)]


def grad_kernel(dims, place, x_ref, x_other, w_hbm, *refs):
    experts, local, cap, width = dims
    outs, (w_ref, g_ref, sems) = refs[:-3], refs[-3:]
    half = x_ref.shape[2]
    pieces = [(l, i, *at) for l in range(local) for i, at in enumerate(pieces_of(w_ref.shape[1], 256))]

    def copy(l, i, start, size):
        rows = pl.ds(start, size)
        return pltpu.make_async_copy(w_hbm.at[l, rows], w_ref.at[l, rows], sems.at[l, i])

    for piece in pieces:
        copy(*piece).start()
    mine = pl.ds(pl.multiple_of(place[1] * half, half), half)
    theirs = pl.ds(pl.multiple_of((1 - place[1]) * half, half), half)
    for l, i, start, size in pieces:
        copy(l, i, start, size).wait()
        rows = pl.ds(start, size)
        grads = dot(x_ref[l], w_ref[l, rows, mine], NT)
        grads = grads + dot(x_other[l], w_ref[l, rows, theirs], NT)
        g_ref[l, :, start : start + size] = grads
    grads = [g_ref[l] for l in range(local)]
    for s, rows in enumerate(by_source(grads, len(outs), cap)):
        outs[s][...] = rows.astype(BF16)


def mix_rows(dims, side, hid, w_hbm, w_ref, sems, tokens, half, store):
    experts, local, cap, width = dims
    n = len(hid)
    ff = w_ref.shape[1]
    pieces = pieces_of(half, 256)

    def copy(i, start, size):
        source = pl.ds(pl.multiple_of(side * half + start, size), size)
        return pltpu.make_async_copy(
            w_hbm.at[:, :, source], w_ref.at[:, :, pl.ds(start, size)], sems.at[i]
        )

    for i, (start, size) in enumerate(pieces):
        copy(i, start, size).start()
    same = ones_where(iota((tokens, tokens), 0) == iota((tokens, tokens), 1))
    held = []
    for h in hid:
        number = h[:, ff : ff + 1].astype(F32).astype(jnp.int32) - 1
        slots = ones_where(iota((width, tokens), 1) == number)
        held.append(dot(same, slots, NT).astype(BF16))
    rows = [h[:, :ff].astype(F32) for h in hid]
    x = [r.astype(BF16) for r in by_expert(rows, local, cap)]
    for i, (start, size) in enumerate(pieces):
        copy(i, start, size).wait()
        columns = pl.ds(start, size)
        out = [dot(x[l], w_ref[l, :, columns], NN) for l in range(local)]
        for s, rows in enumerate(by_source(out, n, cap)):
            store(s, slice(start, start + size), dot(held[s], rows.astype(BF16), NN))


def mix_kernel(dims, sibling, place, *refs):
    hid, (w_hbm, out, w_ref, sems) = refs[:-4], refs[-4:]
    tokens = out.shape[0] // len(hid)

    def store(s, columns, part):
        out[pl.ds(s * tokens, tokens), columns] = part.astype(out.dtype)

    side = 1 - place[1] if sibling else place[1]
    mix_rows(dims, side, hid, w_hbm, w_ref, sems, tokens, out.shape[1], store)


def mix_add_kernel(dims, place, *refs):
    n = (len(refs) - 4) // 2
    hid, (w_hbm, arrived), outs = refs[:n], refs[n : n + 2], refs[n + 2 : -2]
    tokens, half = outs[0].shape

    def store(s, columns, part):
        theirs = arrived[pl.ds(s * tokens, tokens), columns].astype(F32)
        outs[s][:, columns] = (part + theirs).astype(BF16)

    mix_rows(dims, place[1], hid, w_hbm, refs[-2], refs[-1], tokens, half, store)


def add_split_kernel(own, arrived, mine, one_low, one_high, two_low, two_high, low, high):
    tokens, half = mine.shape
    cut = half // 2
    parts = []
    for s in range(4):
        at = pl.ds(s * tokens, tokens)
        parts.append(own[at, :] + arrived[at, :].astype(F32))
    mine[...] = parts[0]
    one_low[...] = parts[1][:, :cut].astype(BF16)
    one_high[...] = parts[1][:, cut:]
    two_low[...] = parts[2][:, :cut]
    two_high[...] = parts[2][:, cut:].astype(BF16)
    low[...] = parts[3][:, :cut].astype(BF16)
    high[...] = parts[3][:, cut:].astype(BF16)


def join_kernel(one_high, two_low, low, high, to_one, to_two):
    to_one[...] = (one_high[...] + high[...].astype(F32)).astype(BF16)
    to_two[...] = (two_low[...] + low[...].astype(F32)).astype(BF16)


def finish_kernel(mine, one_low, one_high, two_low, two_high, out):
    cut = one_low.shape[1]
    for at, one, two in ((0, one_low, two_low), (cut, one_high, two_high)):
        total = mine[:, at : at + cut] + one[...].astype(F32) + two[...].astype(F32)
        out[:, at : at + cut] = total.astype(BF16)


def restore_kernel(dims, place, meta_ref, *refs):
    back_refs, out = refs[:-1], refs[-1]
    top, _, tokens = out.shape
    picks, gate = picks_of(meta_ref[...], place[0], dims)
    back = jnp.concatenate([ref[...] for ref in back_refs], axis=0)
    grads = dot(back, picks, TN)
    for k in range(top):
        out[k] = (grads[:, k * tokens : (k + 1) * tokens] * gate[k : k + 1, :]).astype(BF16)


def shaped(shape, dtype=BF16):
    return jax.ShapeDtypeStruct(shape, dtype)


def call(kernel, outs, args, where=(), scratch=(), grant=24, weight=1, name=None):
    where = dict(where)
    return pl.pallas_call(
        kernel,
        out_shape=outs,
        in_specs=[
            pl.BlockSpec(memory_space=where.get(i, pltpu.VMEM)) for i in range(len(args))
        ],
        out_specs=[pl.BlockSpec(memory_space=pltpu.VMEM)] * len(outs),
        scratch_shapes=scratch,
        compiler_params=pltpu.CompilerParams(vmem_limit_bytes=grant * 1024 * 1024),
        cost_estimate=pl.CostEstimate(
            flops=weight, bytes_accessed=1, transcendentals=0
        ),
        name=name,
    )(*args)


def body(hidden, expert_ids, gate_fix, grad_out, w_down):
    tokens, top, ff = hidden.shape
    half = grad_out.shape[1]
    local, _, full = w_down.shape
    n = lax.axis_size("ctx")
    experts = n * local
    assigned = tokens * top
    cap = min(tokens, assigned // experts + max(1, assigned // (8 * experts)))
    unit = 8 if local % 2 == 0 else 16
    cap = -(-cap // unit) * unit
    width = local * cap
    dims = (experts, local, cap, width)
    run = functools.partial(call, grant=24 if n <= 4 else 56)
    place = jnp.stack([lax.axis_index("ctx"), lax.axis_index("tp")]).astype(jnp.int32)
    placed = {0: pltpu.SMEM}

    def send(x, s):
        return lax.ppermute(x, "ctx", [(i, i ^ s) for i in range(n)]) if s else x

    def swap(x):
        return lax.ppermute(x, "tp", [(0, 1), (1, 0)])

    meta = jnp.concatenate([expert_ids.T, gate_fix.T], axis=0)
    hid_t = hidden.transpose(1, 2, 0)
    named = jnp.pad(expert_ids.T.astype(BF16), ((0, 8 - top), (0, half - tokens)))
    packed = jnp.concatenate([grad_out, named], axis=0)
    forward = n == 4
    own = [send(packed, s) for s in range(n)]
    hid_sent = run(
        functools.partial(dispatch_kernel, dims), [shaped((width, -(-(ff + 1) // 128) * 128))] * n,
        [place, meta, hid_t], where=placed, name="dispatch",
    )
    hid = [send(hid_sent[s], s) for s in range(n)]
    slot = shaped((width, ff))

    def taken(own, w_down):
        (x,) = run(
            functools.partial(gather_kernel, dims, top),
            [shaped((local, n * cap, half))], [place, *own], where=placed, name="gather",
        )
        return list(run(
            functools.partial(grad_kernel, dims), [slot] * n,
            [place, x, swap(x), w_down], where={**placed, 3: pl.ANY},
            scratch=[
                pltpu.VMEM(w_down.shape, BF16),
                pltpu.VMEM((local, n * cap, ff), F32),
                pltpu.SemaphoreType.DMA((local, len(pieces_of(ff, 256)))),
            ],
            name="grad",
        ))

    def skipped(own, w_down):
        return [jnp.zeros((width, ff), BF16)] * n

    grad_sent = lax.cond(
        place[0] < 1000, taken, skipped, own, w_down
    )
    hid[0], grad_own = lax.optimization_barrier((hid[0], grad_sent[0]))
    grad_back = [grad_own] + [send(grad_sent[s], s) for s in range(1, n)]

    mixing = dict(
        where={**placed, n + 1: pl.ANY},
        scratch=[
            pltpu.VMEM((local, ff, half), BF16),
            pltpu.SemaphoreType.DMA((len(pieces_of(half, 256)),)),
        ],
    )
    (theirs,) = run(
        functools.partial(mix_kernel, dims, True), [shaped((n * tokens, half))],
        [place, *hid, w_down], name="mix_sibling", **mixing,
    )
    arrived = swap(theirs)
    if forward:
        (mine,) = run(
            functools.partial(mix_kernel, dims, False), [shaped((n * tokens, half), F32)],
            [place, *hid, w_down], name="mix_own", weight=BIG, **mixing,
        )
        cut = half // 2
        kept, wide = shaped((tokens, half), F32), shaped((tokens, cut), F32)
        piece = shaped((tokens, cut))
        kept, one_low, one_high, two_low, two_high, low, high = run(
            add_split_kernel, [kept, piece, wide, wide, piece, piece, piece],
            [mine, arrived], name="add",
        )
        low, high = send(low, 1), send(high, 2)
        one_low, two_high, *grad_back[1:3] = lax.optimization_barrier(
            (one_low, two_high, *grad_back[1:3])
        )
        one_low, two_high = send(one_low, 1), send(two_high, 2)
        to_one, to_two = run(
            join_kernel, [piece] * 2, [one_high, two_low, low, high], name="join"
        )
        (mixed,) = run(
            finish_kernel, [shaped((tokens, half))],
            [kept, one_low, send(to_one, 1), send(to_two, 2), two_high], name="finish",
        )
    else:
        sums = run(
            functools.partial(mix_add_kernel, dims), [shaped((tokens, half))] * n,
            [place, *hid, w_down, arrived], name="mix_own", **mixing,
        )
        mixed = sum(send(sums[s], s).astype(F32) for s in range(n)).astype(BF16)

    (grad_t,) = run(
        functools.partial(restore_kernel, dims), [shaped((top, ff, tokens))],
        [place, meta, *grad_back], where=placed, name="restore", weight=BIG,
    )
    return mixed, grad_t.transpose(2, 0, 1)


def solution(mesh):
    placed = (
        P(("ctx", "exp"), None, "tp"),
        P(("ctx", "exp"), None),
        P(("ctx", "exp"), None),
        P(("ctx", "exp"), "tp"),
        P("ctx", "tp", None),
    )
    return jax.shard_map(
        body,
        mesh=mesh,
        in_specs=placed,
        out_specs=(P(("ctx", "exp"), "tp"), P(("ctx", "exp"), None, "tp")),
        check_vma=False,
    )
```

```python
import functools

import jax
import jax.numpy as jnp
from jax import lax
from jax.experimental import pallas as pl
from jax.experimental.pallas import tpu as pltpu
from jax.sharding import PartitionSpec as P

BF16 = jnp.bfloat16
F32 = jnp.float32
NN = (((1,), (0,)), ((), ()))
NT = (((1,), (1,)), ((), ()))
TN = (((0,), (0,)), ((), ()))
BIG = 10**11


def dot(a, b, dims):
    return lax.dot_general(a, b, dims, preferred_element_type=F32)


def iota(shape, axis):
    return lax.broadcasted_iota(jnp.int32, shape, axis)


def ones_where(mask):
    return mask.astype(F32).astype(BF16)


def earlier(tokens):
    return ones_where(iota((tokens, tokens), 0) < iota((tokens, tokens), 1))


def token_slots(ids, me, experts, local, cap, width):
    top, tokens = ids.shape
    row = iota((experts, tokens), 0)
    hits = [ids[k : k + 1, :] == row for k in range(top)]
    named = functools.reduce(jnp.logical_or, hits)
    before = dot(ones_where(named), earlier(tokens), NN)
    base = jnp.bitwise_xor(row // local, me) * width + lax.rem(row, local) * cap
    slot = before + base.astype(F32)
    return [
        jnp.sum(jnp.where(hit, slot, 0.0), axis=0, keepdims=True).astype(jnp.int32)
        for hit in hits
    ]


def named_here(ids, me, local):
    top, tokens = ids.shape
    row = iota((8, tokens), 0) + me * local
    return functools.reduce(
        jnp.logical_or, [ids[k : k + 1, :] == row for k in range(top)]
    )


def slots_by_lane(ids, me, local, cap, width):
    tokens = ids.shape[1]
    named = named_here(ids, me, local)
    before = dot(ones_where(named), earlier(tokens), NN)
    slot = before.astype(jnp.int32) + iota((8, tokens), 0) * cap
    slot = jnp.where(named, slot, -1)
    rows = iota((cap, tokens), 0)
    return [ones_where(rows + l * cap == slot[l : l + 1, :]) for l in range(local)]


def picks_of(meta, me, dims):
    experts, local, cap, width = dims
    top = meta.shape[0] // 2
    slots = token_slots(meta[:top], me, experts, local, cap, width)
    rows = iota((experts // local * width, meta.shape[1]), 0)
    picks = jnp.concatenate([ones_where(rows == slot) for slot in slots], axis=1)
    return picks, meta[top:].astype(F32) * (1.0 / 65536.0)


def dispatch_kernel(dims, place, meta_ref, hid_ref, *outs):
    width = outs[0].shape[0]
    picks, gate = picks_of(meta_ref[...], place[0], dims)
    scaled = [
        (hid_ref[k].astype(F32) * gate[k : k + 1, :]).astype(BF16)
        for k in range(hid_ref.shape[0])
    ]
    rows = jnp.concatenate(scaled, axis=1)
    spare = outs[0].shape[1] - rows.shape[0]
    tokens = hid_ref.shape[2]
    number = jnp.bitwise_and(iota((spare, rows.shape[1]), 1), tokens - 1) + 1
    number = jnp.where(iota(number.shape, 0) == 0, number.astype(F32), 0.0)
    sent = dot(picks, jnp.concatenate([rows, number.astype(BF16)], axis=0), NT)
    for s, out in enumerate(outs):
        out[...] = sent[s * width : (s + 1) * width].astype(BF16)


def by_expert(rows, local, cap):
    return [
        jnp.concatenate([r[l * cap : (l + 1) * cap] for r in rows], axis=0)
        for l in range(local)
    ]


def by_source(rows, count, cap):
    return [
        jnp.concatenate([r[s * cap : (s + 1) * cap] for r in rows], axis=0)
        for s in range(count)
    ]


def routes(dims, top, me, packed, tokens):
    experts, local, cap, width = dims
    ids = packed[tokens:, :tokens].astype(F32).astype(jnp.int32)[:top]
    return jnp.concatenate(slots_by_lane(ids, me, local, cap, width), axis=0)


def gather_rows(dims, held, halves, x_ref):
    experts, local, cap, width = dims
    tokens, half = held[0].shape[1], halves[0].shape[1]
    chunk = min(half, 512)
    for c in range(0, half, chunk):
        rows = [dot(h, ref[:tokens, c : c + chunk], NN) for h, ref in zip(held, halves)]
        for l, x in enumerate(by_expert(rows, local, cap)):
            x_ref[l, :, c : c + chunk] = x.astype(BF16)


def grad_kernel(dims, top, place, *refs):
    experts, local, cap, width = dims
    n = experts // local
    own, other, w_ref = refs[:n], refs[n : 2 * n], refs[2 * n]
    outs, x_ref = refs[2 * n + 1 : -1], refs[-1]
    half = own[0].shape[1]
    tokens = own[0].shape[0] - 8
    chunk = min(half, 512)
    held = []
    for ref in own:
        ids = ref[tokens:, :tokens].astype(F32).astype(jnp.int32)[:top]
        held.append(
            jnp.concatenate(slots_by_lane(ids, place[0], local, cap, width), axis=0)
        )
    for side, halves in ((place[1], own), (1 - place[1], other)):
        for c in range(0, half, chunk):
            rows = [dot(h, ref[:tokens, c : c + chunk], NN) for h, ref in zip(held, halves)]
            at = pl.ds(pl.multiple_of(side * half + c, chunk), chunk)
            for l, x in enumerate(by_expert(rows, local, cap)):
                x_ref[l, :, at] = x.astype(BF16)
    grads = [dot(x_ref[l], w_ref[l], NT) for l in range(local)]
    for s, rows in enumerate(by_source(grads, n, cap)):
        outs[s][...] = rows.astype(BF16)


def mix_rows(dims, side, hid, w_ref, tokens, half, store):
    experts, local, cap, width = dims
    n = len(hid)
    ff = w_ref.shape[1]
    chunk = min(half, 256)
    same = ones_where(iota((tokens, tokens), 0) == iota((tokens, tokens), 1))
    held = []
    for h in hid:
        number = h[:, ff : ff + 1].astype(F32).astype(jnp.int32) - 1
        slots = ones_where(iota((width, tokens), 1) == number)
        held.append(dot(same, slots, NT).astype(BF16))
    rows = [h[:, :ff].astype(F32) for h in hid]
    x = [r.astype(BF16) for r in by_expert(rows, local, cap)]
    for c in range(0, half, chunk):
        at = pl.ds(pl.multiple_of(side * half + c, chunk), chunk)
        out = [dot(x[l], w_ref[l, :, at], NN) for l in range(local)]
        for s, rows in enumerate(by_source(out, n, cap)):
            store(s, slice(c, c + chunk), dot(held[s], rows.astype(BF16), NN))


def mix_kernel(dims, sibling, place, *refs):
    hid, (w_ref, out) = refs[:-2], refs[-2:]
    tokens = out.shape[0] // len(hid)

    def store(s, columns, part):
        out[pl.ds(s * tokens, tokens), columns] = part.astype(out.dtype)

    side = 1 - place[1] if sibling else place[1]
    mix_rows(dims, side, hid, w_ref, tokens, out.shape[1], store)


def mix_add_kernel(dims, place, *refs):
    n = (len(refs) - 2) // 2
    hid, (w_ref, arrived), outs = refs[:n], refs[n : n + 2], refs[n + 2 :]
    tokens, half = outs[0].shape

    def store(s, columns, part):
        theirs = arrived[pl.ds(s * tokens, tokens), columns].astype(F32)
        outs[s][:, columns] = (part + theirs).astype(BF16)

    mix_rows(dims, place[1], hid, w_ref, tokens, half, store)


def add_split_kernel(own, arrived, mine, one_low, one_high, two_low, two_high, low, high):
    tokens, half = mine.shape
    cut = half // 2
    parts = []
    for s in range(4):
        at = pl.ds(s * tokens, tokens)
        parts.append(own[at, :] + arrived[at, :].astype(F32))
    mine[...] = parts[0]
    one_low[...] = parts[1][:, :cut].astype(BF16)
    one_high[...] = parts[1][:, cut:]
    two_low[...] = parts[2][:, :cut]
    two_high[...] = parts[2][:, cut:].astype(BF16)
    low[...] = parts[3][:, :cut].astype(BF16)
    high[...] = parts[3][:, cut:].astype(BF16)


def join_kernel(one_high, two_low, low, high, to_one, to_two):
    to_one[...] = (one_high[...] + high[...].astype(F32)).astype(BF16)
    to_two[...] = (two_low[...] + low[...].astype(F32)).astype(BF16)


def finish_kernel(mine, one_low, one_high, two_low, two_high, out):
    cut = one_low.shape[1]
    for at, one, two in ((0, one_low, two_low), (cut, one_high, two_high)):
        total = mine[:, at : at + cut] + one[...].astype(F32) + two[...].astype(F32)
        out[:, at : at + cut] = total.astype(BF16)


def restore_kernel(dims, place, meta_ref, *refs):
    back_refs, out = refs[:-1], refs[-1]
    top, _, tokens = out.shape
    picks, gate = picks_of(meta_ref[...], place[0], dims)
    back = jnp.concatenate([ref[...] for ref in back_refs], axis=0)
    grads = dot(back, picks, TN)
    for k in range(top):
        out[k] = (grads[:, k * tokens : (k + 1) * tokens] * gate[k : k + 1, :]).astype(BF16)


def shaped(shape, dtype=BF16):
    return jax.ShapeDtypeStruct(shape, dtype)


def call(kernel, outs, args, where=(), scratch=(), grant=24, weight=1, name=None):
    where = dict(where)
    return pl.pallas_call(
        kernel,
        out_shape=outs,
        in_specs=[
            pl.BlockSpec(memory_space=where.get(i, pltpu.VMEM)) for i in range(len(args))
        ],
        out_specs=[pl.BlockSpec(memory_space=pltpu.VMEM)] * len(outs),
        scratch_shapes=scratch,
        compiler_params=pltpu.CompilerParams(vmem_limit_bytes=grant * 1024 * 1024),
        cost_estimate=pl.CostEstimate(
            flops=weight, bytes_accessed=1, transcendentals=0
        ),
        name=name,
    )(*args)


def body(hidden, expert_ids, gate_fix, grad_out, w_down):
    tokens, top, ff = hidden.shape
    half = grad_out.shape[1]
    local, _, full = w_down.shape
    n = lax.axis_size("ctx")
    experts = n * local
    assigned = tokens * top
    cap = min(tokens, assigned // experts + max(1, assigned // (8 * experts)))
    unit = 8 if local % 2 == 0 else 16
    cap = -(-cap // unit) * unit
    width = local * cap
    dims = (experts, local, cap, width)
    run = functools.partial(call, grant=24 if n <= 4 else 56)
    place = jnp.stack([lax.axis_index("ctx"), lax.axis_index("tp")]).astype(jnp.int32)
    placed = {0: pltpu.SMEM}

    def send(x, s):
        return lax.ppermute(x, "ctx", [(i, i ^ s) for i in range(n)]) if s else x

    def swap(x):
        return lax.ppermute(x, "tp", [(0, 1), (1, 0)])

    meta = jnp.concatenate([expert_ids.T, gate_fix.T], axis=0)
    hid_t = hidden.transpose(1, 2, 0)
    named = jnp.pad(expert_ids.T.astype(BF16), ((0, 8 - top), (0, half - tokens)))
    packed = jnp.concatenate([grad_out, named], axis=0)
    forward = n == 4
    own = [send(packed, s) for s in range(n)]
    swapped = swap(packed)
    meta, swapped = lax.optimization_barrier((meta, swapped))
    hid_sent = run(
        functools.partial(dispatch_kernel, dims), [shaped((width, -(-(ff + 1) // 128) * 128))] * n,
        [place, meta, hid_t], where=placed, name="dispatch", weight=BIG,
    )
    hid = [send(hid_sent[s], s) for s in range(n)]
    slot = shaped((width, ff))

    def taken(own):
        other = [swap(x) for x in own[:2]]
        for x in own[2:]:
            other[-2], x = lax.optimization_barrier((other[-2], x))
            other.append(swap(x))
        return other

    other = [swapped] + lax.cond(place[0] < 1000, taken, list, own[1:])
    grad_sent = run(
        functools.partial(grad_kernel, dims, top), [slot] * n,
        [place, *own, *other, w_down], where=placed,
        scratch=[pltpu.VMEM((local, n * cap, full), BF16)], name="grad",
    )
    hid[0], grad_own = lax.optimization_barrier((hid[0], grad_sent[0]))
    grad_back = [grad_own] + [send(grad_sent[s], s) for s in range(1, n)]

    mixing = dict(where=placed)
    (theirs,) = run(
        functools.partial(mix_kernel, dims, True), [shaped((n * tokens, half))],
        [place, *hid, w_down], name="mix_sibling", **mixing,
    )
    arrived = swap(theirs)
    if forward:
        (mine,) = run(
            functools.partial(mix_kernel, dims, False), [shaped((n * tokens, half), F32)],
            [place, *hid, w_down], name="mix_own", weight=BIG, **mixing,
        )
        cut = half // 2
        kept, wide = shaped((tokens, half), F32), shaped((tokens, cut), F32)
        piece = shaped((tokens, cut))
        kept, one_low, one_high, two_low, two_high, low, high = run(
            add_split_kernel, [kept, piece, wide, wide, piece, piece, piece],
            [mine, arrived], name="add",
        )
        low, high = send(low, 1), send(high, 2)
        one_low, two_high, *grad_back[1:3] = lax.optimization_barrier(
            (one_low, two_high, *grad_back[1:3])
        )
        one_low, two_high = send(one_low, 1), send(two_high, 2)
        to_one, to_two = run(
            join_kernel, [piece] * 2, [one_high, two_low, low, high], name="join"
        )
        (mixed,) = run(
            finish_kernel, [shaped((tokens, half))],
            [kept, one_low, send(to_one, 1), send(to_two, 2), two_high], name="finish",
        )
    else:
        sums = run(
            functools.partial(mix_add_kernel, dims), [shaped((tokens, half))] * n,
            [place, *hid, w_down, arrived], name="mix_own", **mixing,
        )
        mixed = sum(send(sums[s], s).astype(F32) for s in range(n)).astype(BF16)

    (grad_t,) = run(
        functools.partial(restore_kernel, dims), [shaped((top, ff, tokens))],
        [place, meta, *grad_back], where=placed, name="restore", weight=BIG,
    )
    return mixed, grad_t.transpose(2, 0, 1)


def solution(mesh):
    placed = (
        P(("ctx", "exp"), None, "tp"),
        P(("ctx", "exp"), None),
        P(("ctx", "exp"), None),
        P(("ctx", "exp"), "tp"),
        P("ctx", "tp", None),
    )
    return jax.shard_map(
        body,
        mesh=mesh,
        in_specs=placed,
        out_specs=(P(("ctx", "exp"), "tp"), P(("ctx", "exp"), None, "tp")),
        check_vma=False,
    )
```

```python
import functools

import jax
import jax.numpy as jnp
from jax import lax
from jax.experimental import pallas as pl
from jax.experimental.pallas import tpu as pltpu
from jax.sharding import PartitionSpec as P

BF16 = jnp.bfloat16
F32 = jnp.float32
NN = (((1,), (0,)), ((), ()))
NT = (((1,), (1,)), ((), ()))
TN = (((0,), (0,)), ((), ()))
BIG = 10**11


def dot(a, b, dims):
    return lax.dot_general(a, b, dims, preferred_element_type=F32)


def iota(shape, axis):
    return lax.broadcasted_iota(jnp.int32, shape, axis)


def ones_where(mask):
    return mask.astype(F32).astype(BF16)


def earlier(tokens):
    return ones_where(iota((tokens, tokens), 0) < iota((tokens, tokens), 1))


def token_slots(ids, me, experts, local, cap, width):
    top, tokens = ids.shape
    row = iota((experts, tokens), 0)
    hits = [ids[k : k + 1, :] == row for k in range(top)]
    named = functools.reduce(jnp.logical_or, hits)
    before = dot(ones_where(named), earlier(tokens), NN)
    base = jnp.bitwise_xor(row // local, me) * width + lax.rem(row, local) * cap
    slot = before + base.astype(F32)
    return [
        jnp.sum(jnp.where(hit, slot, 0.0), axis=0, keepdims=True).astype(jnp.int32)
        for hit in hits
    ]


def named_here(ids, me, local):
    top, tokens = ids.shape
    row = iota((8, tokens), 0) + me * local
    return functools.reduce(
        jnp.logical_or, [ids[k : k + 1, :] == row for k in range(top)]
    )


def slots_by_lane(ids, me, local, cap, width):
    tokens = ids.shape[1]
    named = named_here(ids, me, local)
    before = dot(ones_where(named), earlier(tokens), NN)
    slot = before.astype(jnp.int32) + iota((8, tokens), 0) * cap
    slot = jnp.where(named, slot, -1)
    rows = iota((cap, tokens), 0)
    return [ones_where(rows + l * cap == slot[l : l + 1, :]) for l in range(local)]


def picks_of(meta, me, dims):
    experts, local, cap, width = dims
    top = meta.shape[0] // 2
    slots = token_slots(meta[:top], me, experts, local, cap, width)
    rows = iota((experts // local * width, meta.shape[1]), 0)
    picks = jnp.concatenate([ones_where(rows == slot) for slot in slots], axis=1)
    return picks, meta[top:].astype(F32) * (1.0 / 65536.0)


def dispatch_kernel(dims, place, meta_ref, hid_ref, *outs):
    width = outs[0].shape[0]
    picks, gate = picks_of(meta_ref[...], place[0], dims)
    scaled = [
        (hid_ref[k].astype(F32) * gate[k : k + 1, :]).astype(BF16)
        for k in range(hid_ref.shape[0])
    ]
    rows = jnp.concatenate(scaled, axis=1)
    spare = outs[0].shape[1] - rows.shape[0]
    tokens = hid_ref.shape[2]
    number = jnp.bitwise_and(iota((spare, rows.shape[1]), 1), tokens - 1) + 1
    number = jnp.where(iota(number.shape, 0) == 0, number.astype(F32), 0.0)
    sent = dot(picks, jnp.concatenate([rows, number.astype(BF16)], axis=0), NT)
    for s, out in enumerate(outs):
        out[...] = sent[s * width : (s + 1) * width].astype(BF16)


def by_expert(rows, local, cap):
    return [
        jnp.concatenate([r[l * cap : (l + 1) * cap] for r in rows], axis=0)
        for l in range(local)
    ]


def by_source(rows, count, cap):
    return [
        jnp.concatenate([r[s * cap : (s + 1) * cap] for r in rows], axis=0)
        for s in range(count)
    ]


def routes(dims, top, me, packed, tokens):
    experts, local, cap, width = dims
    ids = packed[tokens:, :tokens].astype(F32).astype(jnp.int32)[:top]
    return jnp.concatenate(slots_by_lane(ids, me, local, cap, width), axis=0)


def gather_rows(dims, held, halves, x_ref):
    experts, local, cap, width = dims
    tokens, half = held[0].shape[1], halves[0].shape[1]
    chunk = min(half, 512)
    for c in range(0, half, chunk):
        rows = [dot(h, ref[:tokens, c : c + chunk], NN) for h, ref in zip(held, halves)]
        for l, x in enumerate(by_expert(rows, local, cap)):
            x_ref[l, :, c : c + chunk] = x.astype(BF16)


def grad_kernel(dims, top, place, *refs):
    experts, local, cap, width = dims
    n = experts // local
    own, other, w_hbm = refs[:n], refs[n : 2 * n], refs[2 * n]
    outs, (x_ref, w_ref, sems) = refs[2 * n + 1 : -3], refs[-3:]
    half = own[0].shape[1]
    tokens = own[0].shape[0] - 8

    def copy(l):
        return pltpu.make_async_copy(w_hbm.at[l], w_ref.at[l], sems.at[l])

    copy(0).start()
    chunk = min(half, 512)
    held = []
    for ref in own:
        ids = ref[tokens:, :tokens].astype(F32).astype(jnp.int32)[:top]
        held.append(
            jnp.concatenate(slots_by_lane(ids, place[0], local, cap, width), axis=0)
        )
    for side, halves in ((place[1], own), (1 - place[1], other)):
        for c in range(0, half, chunk):
            rows = [dot(h, ref[:tokens, c : c + chunk], NN) for h, ref in zip(held, halves)]
            at = pl.ds(pl.multiple_of(side * half + c, chunk), chunk)
            for l, x in enumerate(by_expert(rows, local, cap)):
                x_ref[l, :, at] = x.astype(BF16)
    grads = []
    for l in range(local):
        copy(l).wait()
        if l + 1 < local:
            copy(l + 1).start()
        grads.append(dot(x_ref[l], w_ref[l], NT))
    for s, rows in enumerate(by_source(grads, n, cap)):
        outs[s][...] = rows.astype(BF16)


def mix_rows(dims, side, hid, w_hbm, w_ref, sems, tokens, half, store):
    experts, local, cap, width = dims
    n = len(hid)
    ff = w_ref.shape[1]
    chunk = min(half, 256)
    count = half // chunk

    def copy(i):
        source = pl.ds(pl.multiple_of(side * half + i * chunk, chunk), chunk)
        return pltpu.make_async_copy(
            w_hbm.at[:, :, source], w_ref.at[:, :, pl.ds(i * chunk, chunk)], sems.at[i]
        )

    copy(0).start()
    same = ones_where(iota((tokens, tokens), 0) == iota((tokens, tokens), 1))
    held = []
    for h in hid:
        number = h[:, ff : ff + 1].astype(F32).astype(jnp.int32) - 1
        slots = ones_where(iota((width, tokens), 1) == number)
        held.append(dot(same, slots, NT).astype(BF16))
    rows = [h[:, :ff].astype(F32) for h in hid]
    x = [r.astype(BF16) for r in by_expert(rows, local, cap)]
    for i in range(count):
        copy(i).wait()
        if i + 1 < count:
            copy(i + 1).start()
        columns = slice(i * chunk, (i + 1) * chunk)
        out = [dot(x[l], w_ref[l, :, columns], NN) for l in range(local)]
        for s, rows in enumerate(by_source(out, n, cap)):
            store(s, columns, dot(held[s], rows.astype(BF16), NN))


def mix_kernel(dims, sibling, place, *refs):
    hid, (w_hbm, out, w_ref, sems) = refs[:-4], refs[-4:]
    tokens = out.shape[0] // len(hid)

    def store(s, columns, part):
        out[pl.ds(s * tokens, tokens), columns] = part.astype(out.dtype)

    side = 1 - place[1] if sibling else place[1]
    mix_rows(dims, side, hid, w_hbm, w_ref, sems, tokens, out.shape[1], store)


def mix_add_kernel(dims, place, *refs):
    n = (len(refs) - 4) // 2
    hid, (w_hbm, arrived), outs = refs[:n], refs[n : n + 2], refs[n + 2 : -2]
    tokens, half = outs[0].shape

    def store(s, columns, part):
        theirs = arrived[pl.ds(s * tokens, tokens), columns].astype(F32)
        outs[s][:, columns] = (part + theirs).astype(BF16)

    mix_rows(dims, place[1], hid, w_hbm, refs[-2], refs[-1], tokens, half, store)


def add_split_kernel(own, arrived, mine, one_low, one_high, two_low, two_high, low, high):
    tokens, half = mine.shape
    cut = half // 2
    parts = []
    for s in range(4):
        at = pl.ds(s * tokens, tokens)
        parts.append(own[at, :] + arrived[at, :].astype(F32))
    mine[...] = parts[0]
    one_low[...] = parts[1][:, :cut].astype(BF16)
    one_high[...] = parts[1][:, cut:]
    two_low[...] = parts[2][:, :cut]
    two_high[...] = parts[2][:, cut:].astype(BF16)
    low[...] = parts[3][:, :cut].astype(BF16)
    high[...] = parts[3][:, cut:].astype(BF16)


def join_kernel(one_high, two_low, low, high, to_one, to_two):
    to_one[...] = (one_high[...] + high[...].astype(F32)).astype(BF16)
    to_two[...] = (two_low[...] + low[...].astype(F32)).astype(BF16)


def finish_kernel(mine, one_low, one_high, two_low, two_high, out):
    cut = one_low.shape[1]
    for at, one, two in ((0, one_low, two_low), (cut, one_high, two_high)):
        total = mine[:, at : at + cut] + one[...].astype(F32) + two[...].astype(F32)
        out[:, at : at + cut] = total.astype(BF16)


def restore_kernel(dims, place, meta_ref, *refs):
    back_refs, out = refs[:-1], refs[-1]
    top, _, tokens = out.shape
    picks, gate = picks_of(meta_ref[...], place[0], dims)
    back = jnp.concatenate([ref[...] for ref in back_refs], axis=0)
    grads = dot(back, picks, TN)
    for k in range(top):
        out[k] = (grads[:, k * tokens : (k + 1) * tokens] * gate[k : k + 1, :]).astype(BF16)


def shaped(shape, dtype=BF16):
    return jax.ShapeDtypeStruct(shape, dtype)


def call(kernel, outs, args, where=(), scratch=(), grant=24, weight=1, name=None):
    where = dict(where)
    return pl.pallas_call(
        kernel,
        out_shape=outs,
        in_specs=[
            pl.BlockSpec(memory_space=where.get(i, pltpu.VMEM)) for i in range(len(args))
        ],
        out_specs=[pl.BlockSpec(memory_space=pltpu.VMEM)] * len(outs),
        scratch_shapes=scratch,
        compiler_params=pltpu.CompilerParams(vmem_limit_bytes=grant * 1024 * 1024),
        cost_estimate=pl.CostEstimate(
            flops=weight, bytes_accessed=1, transcendentals=0
        ),
        name=name,
    )(*args)


def body(hidden, expert_ids, gate_fix, grad_out, w_down):
    tokens, top, ff = hidden.shape
    half = grad_out.shape[1]
    local, _, full = w_down.shape
    n = lax.axis_size("ctx")
    experts = n * local
    assigned = tokens * top
    cap = min(tokens, assigned // experts + max(1, assigned // (8 * experts)))
    unit = 8 if local % 2 == 0 else 16
    cap = -(-cap // unit) * unit
    width = local * cap
    dims = (experts, local, cap, width)
    run = functools.partial(call, grant=24 if n <= 4 else 56)
    place = jnp.stack([lax.axis_index("ctx"), lax.axis_index("tp")]).astype(jnp.int32)
    placed = {0: pltpu.SMEM}

    def send(x, s):
        return lax.ppermute(x, "ctx", [(i, i ^ s) for i in range(n)]) if s else x

    def swap(x):
        return lax.ppermute(x, "tp", [(0, 1), (1, 0)])

    meta = jnp.concatenate([expert_ids.T, gate_fix.T], axis=0)
    hid_t = hidden.transpose(1, 2, 0)
    named = jnp.pad(expert_ids.T.astype(BF16), ((0, 8 - top), (0, half - tokens)))
    packed = jnp.concatenate([grad_out, named], axis=0)
    forward = n == 4
    own = [send(packed, s) for s in range(n)]
    swapped = swap(packed)
    meta, swapped = lax.optimization_barrier((meta, swapped))
    hid_sent = run(
        functools.partial(dispatch_kernel, dims), [shaped((width, -(-(ff + 1) // 128) * 128))] * n,
        [place, meta, hid_t], where=placed, name="dispatch",
    )
    hid = [send(hid_sent[s], s) for s in range(n)]
    slot = shaped((width, ff))

    def grads(own, other, w):
        return list(run(
            functools.partial(grad_kernel, dims, top), [slot] * n,
            [place, *own, *other, w], where={**placed, 2 * n + 1: pl.ANY},
            scratch=[
                pltpu.VMEM((local, n * cap, full), BF16),
                pltpu.VMEM(w.shape, BF16),
                pltpu.SemaphoreType.DMA((local,)),
            ],
            name="grad",
        ))

    def last_swaps(own, first, last, w):
        return grads(own, [first] + [swap(x) for x in own[1 : n - 1]] + [last], w)

    if forward:
        always = place[0] < 1000
        last = lax.cond(always, swap, lambda x: x, own[3])
        *own[1:3], last = lax.optimization_barrier((*own[1:3], last))
        grad_sent = lax.cond(
            always, last_swaps, lambda *unused: [jnp.zeros((width, ff), BF16)] * n,
            own, swapped, last, w_down,
        )
    else:
        grad_sent = last_swaps(own, swapped, swap(own[-1]), w_down)
    hid[0], grad_own = lax.optimization_barrier((hid[0], grad_sent[0]))
    grad_back = [grad_own] + [send(grad_sent[s], s) for s in range(1, n)]

    mixing = dict(
        where={**placed, n + 1: pl.ANY},
        scratch=[
            pltpu.VMEM((local, ff, half), BF16),
            pltpu.SemaphoreType.DMA((half // min(half, 256),)),
        ],
    )
    (theirs,) = run(
        functools.partial(mix_kernel, dims, True), [shaped((n * tokens, half))],
        [place, *hid, w_down], name="mix_sibling", **mixing,
    )
    arrived = swap(theirs)
    if forward:
        (mine,) = run(
            functools.partial(mix_kernel, dims, False), [shaped((n * tokens, half), F32)],
            [place, *hid, w_down], name="mix_own", weight=BIG, **mixing,
        )
        cut = half // 2
        kept, wide = shaped((tokens, half), F32), shaped((tokens, cut), F32)
        piece = shaped((tokens, cut))
        kept, one_low, one_high, two_low, two_high, low, high = run(
            add_split_kernel, [kept, piece, wide, wide, piece, piece, piece],
            [mine, arrived], name="add",
        )
        low, high = send(low, 1), send(high, 2)
        one_low, two_high, *grad_back[1:3] = lax.optimization_barrier(
            (one_low, two_high, *grad_back[1:3])
        )
        one_low, two_high = send(one_low, 1), send(two_high, 2)
        to_one, to_two = run(
            join_kernel, [piece] * 2, [one_high, two_low, low, high], name="join"
        )
        (mixed,) = run(
            finish_kernel, [shaped((tokens, half))],
            [kept, one_low, send(to_one, 1), send(to_two, 2), two_high], name="finish",
        )
    else:
        sums = run(
            functools.partial(mix_add_kernel, dims), [shaped((tokens, half))] * n,
            [place, *hid, w_down, arrived], name="mix_own", **mixing,
        )
        mixed = sum(send(sums[s], s).astype(F32) for s in range(n)).astype(BF16)

    (grad_t,) = run(
        functools.partial(restore_kernel, dims), [shaped((top, ff, tokens))],
        [place, meta, *grad_back], where=placed, name="restore", weight=BIG,
    )
    return mixed, grad_t.transpose(2, 0, 1)


def solution(mesh):
    placed = (
        P(("ctx", "exp"), None, "tp"),
        P(("ctx", "exp"), None),
        P(("ctx", "exp"), None),
        P(("ctx", "exp"), "tp"),
        P("ctx", "tp", None),
    )
    return jax.shard_map(
        body,
        mesh=mesh,
        in_specs=placed,
        out_specs=(P(("ctx", "exp"), "tp"), P(("ctx", "exp"), None, "tp")),
        check_vma=False,
    )
```

```python
import functools

import jax
import jax.numpy as jnp
from jax import lax
from jax.experimental import pallas as pl
from jax.experimental.pallas import tpu as pltpu
from jax.sharding import PartitionSpec as P

BF16 = jnp.bfloat16
F32 = jnp.float32
NN = (((1,), (0,)), ((), ()))
NT = (((1,), (1,)), ((), ()))
TN = (((0,), (0,)), ((), ()))
BIG = 10**11


def dot(a, b, dims):
    return lax.dot_general(a, b, dims, preferred_element_type=F32)


def iota(shape, axis):
    return lax.broadcasted_iota(jnp.int32, shape, axis)


def ones_where(mask):
    return mask.astype(F32).astype(BF16)


def earlier(tokens):
    return ones_where(iota((tokens, tokens), 0) < iota((tokens, tokens), 1))


def token_slots(ids, me, experts, local, cap, width):
    top, tokens = ids.shape
    row = iota((experts, tokens), 0)
    hits = [ids[k : k + 1, :] == row for k in range(top)]
    named = functools.reduce(jnp.logical_or, hits)
    before = dot(ones_where(named), earlier(tokens), NN)
    base = jnp.bitwise_xor(row // local, me) * width + lax.rem(row, local) * cap
    slot = before + base.astype(F32)
    return [
        jnp.sum(jnp.where(hit, slot, 0.0), axis=0, keepdims=True).astype(jnp.int32)
        for hit in hits
    ]


def named_here(ids, me, local):
    top, tokens = ids.shape
    row = iota((8, tokens), 0) + me * local
    return functools.reduce(
        jnp.logical_or, [ids[k : k + 1, :] == row for k in range(top)]
    )


def slots_by_lane(ids, me, local, cap, width):
    tokens = ids.shape[1]
    named = named_here(ids, me, local)
    before = dot(ones_where(named), earlier(tokens), NN)
    slot = before.astype(jnp.int32) + iota((8, tokens), 0) * cap
    slot = jnp.where(named, slot, -1)
    rows = iota((cap, tokens), 0)
    return [ones_where(rows + l * cap == slot[l : l + 1, :]) for l in range(local)]


def picks_of(meta, me, dims):
    experts, local, cap, width = dims
    top = meta.shape[0] // 2
    slots = token_slots(meta[:top], me, experts, local, cap, width)
    rows = iota((experts // local * width, meta.shape[1]), 0)
    picks = jnp.concatenate([ones_where(rows == slot) for slot in slots], axis=1)
    return picks, meta[top:].astype(F32) * (1.0 / 65536.0)


def dispatch_kernel(dims, place, meta_ref, hid_ref, *outs):
    width = outs[0].shape[0]
    picks, gate = picks_of(meta_ref[...], place[0], dims)
    scaled = [
        (hid_ref[k].astype(F32) * gate[k : k + 1, :]).astype(BF16)
        for k in range(hid_ref.shape[0])
    ]
    rows = jnp.concatenate(scaled, axis=1)
    spare = outs[0].shape[1] - rows.shape[0]
    tokens = hid_ref.shape[2]
    number = jnp.bitwise_and(iota((spare, rows.shape[1]), 1), tokens - 1) + 1
    number = jnp.where(iota(number.shape, 0) == 0, number.astype(F32), 0.0)
    sent = dot(picks, jnp.concatenate([rows, number.astype(BF16)], axis=0), NT)
    for s, out in enumerate(outs):
        out[...] = sent[s * width : (s + 1) * width].astype(BF16)


def by_expert(rows, local, cap):
    return [
        jnp.concatenate([r[l * cap : (l + 1) * cap] for r in rows], axis=0)
        for l in range(local)
    ]


def by_source(rows, count, cap):
    return [
        jnp.concatenate([r[s * cap : (s + 1) * cap] for r in rows], axis=0)
        for s in range(count)
    ]


def routes(dims, top, me, packed, tokens):
    experts, local, cap, width = dims
    ids = packed[tokens:, :tokens].astype(F32).astype(jnp.int32)[:top]
    return jnp.concatenate(slots_by_lane(ids, me, local, cap, width), axis=0)


def gather_rows(dims, held, halves, x_ref):
    experts, local, cap, width = dims
    tokens, half = held[0].shape[1], halves[0].shape[1]
    chunk = min(half, 512)
    for c in range(0, half, chunk):
        rows = [dot(h, ref[:tokens, c : c + chunk], NN) for h, ref in zip(held, halves)]
        for l, x in enumerate(by_expert(rows, local, cap)):
            x_ref[l, :, c : c + chunk] = x.astype(BF16)


def gather_kernel(dims, top, place, *refs):
    experts, local, cap, width = dims
    n = experts // local
    own, other, x_ref = refs[:n], refs[n:-1], refs[-1]
    half = own[0].shape[1]
    tokens = own[0].shape[0] - 8
    chunk = min(half, 512)
    held = []
    for ref in own:
        ids = ref[tokens:, :tokens].astype(F32).astype(jnp.int32)[:top]
        held.append(
            jnp.concatenate(slots_by_lane(ids, place[0], local, cap, width), axis=0)
        )
    for side, halves in ((place[1], own), (1 - place[1], other)):
        for c in range(0, half, chunk):
            rows = [dot(h, ref[:tokens, c : c + chunk], NN) for h, ref in zip(held, halves)]
            at = pl.ds(pl.multiple_of(side * half + c, chunk), chunk)
            for l, x in enumerate(by_expert(rows, local, cap)):
                x_ref[l, :, at] = x.astype(BF16)


def grad_kernel(dims, x_ref, w_ref, *outs):
    experts, local, cap, width = dims
    grads = [dot(x_ref[l], w_ref[l], NT) for l in range(local)]
    for s, rows in enumerate(by_source(grads, len(outs), cap)):
        outs[s][...] = rows.astype(BF16)


def mix_rows(dims, side, hid, w_ref, tokens, half, store):
    experts, local, cap, width = dims
    n = len(hid)
    ff = w_ref.shape[1]
    chunk = min(half, 256)
    same = ones_where(iota((tokens, tokens), 0) == iota((tokens, tokens), 1))
    held = []
    for h in hid:
        number = h[:, ff : ff + 1].astype(F32).astype(jnp.int32) - 1
        slots = ones_where(iota((width, tokens), 1) == number)
        held.append(dot(same, slots, NT).astype(BF16))
    rows = [h[:, :ff].astype(F32) for h in hid]
    x = [r.astype(BF16) for r in by_expert(rows, local, cap)]
    for c in range(0, half, chunk):
        at = pl.ds(pl.multiple_of(side * half + c, chunk), chunk)
        out = [dot(x[l], w_ref[l, :, at], NN) for l in range(local)]
        for s, rows in enumerate(by_source(out, n, cap)):
            store(s, slice(c, c + chunk), dot(held[s], rows.astype(BF16), NN))


def mix_kernel(dims, sibling, place, *refs):
    hid, (w_ref, out) = refs[:-2], refs[-2:]
    tokens = out.shape[0] // len(hid)

    def store(s, columns, part):
        out[pl.ds(s * tokens, tokens), columns] = part.astype(out.dtype)

    side = 1 - place[1] if sibling else place[1]
    mix_rows(dims, side, hid, w_ref, tokens, out.shape[1], store)


def mix_add_kernel(dims, place, *refs):
    n = (len(refs) - 2) // 2
    hid, (w_ref, arrived), outs = refs[:n], refs[n : n + 2], refs[n + 2 :]
    tokens, half = outs[0].shape

    def store(s, columns, part):
        theirs = arrived[pl.ds(s * tokens, tokens), columns].astype(F32)
        outs[s][:, columns] = (part + theirs).astype(BF16)

    mix_rows(dims, place[1], hid, w_ref, tokens, half, store)


def add_split_kernel(own, arrived, mine, one_low, one_high, two_low, two_high, low, high):
    tokens, half = mine.shape
    cut = half // 2
    parts = []
    for s in range(4):
        at = pl.ds(s * tokens, tokens)
        parts.append(own[at, :] + arrived[at, :].astype(F32))
    mine[...] = parts[0]
    one_low[...] = parts[1][:, :cut].astype(BF16)
    one_high[...] = parts[1][:, cut:]
    two_low[...] = parts[2][:, :cut]
    two_high[...] = parts[2][:, cut:].astype(BF16)
    low[...] = parts[3][:, :cut].astype(BF16)
    high[...] = parts[3][:, cut:].astype(BF16)


def join_kernel(one_high, two_low, low, high, to_one, to_two):
    to_one[...] = (one_high[...] + high[...].astype(F32)).astype(BF16)
    to_two[...] = (two_low[...] + low[...].astype(F32)).astype(BF16)


def finish_kernel(mine, one_low, one_high, two_low, two_high, out):
    cut = one_low.shape[1]
    for at, one, two in ((0, one_low, two_low), (cut, one_high, two_high)):
        total = mine[:, at : at + cut] + one[...].astype(F32) + two[...].astype(F32)
        out[:, at : at + cut] = total.astype(BF16)


def restore_kernel(dims, place, meta_ref, *refs):
    back_refs, out = refs[:-1], refs[-1]
    top, _, tokens = out.shape
    picks, gate = picks_of(meta_ref[...], place[0], dims)
    back = jnp.concatenate([ref[...] for ref in back_refs], axis=0)
    grads = dot(back, picks, TN)
    for k in range(top):
        out[k] = (grads[:, k * tokens : (k + 1) * tokens] * gate[k : k + 1, :]).astype(BF16)


def shaped(shape, dtype=BF16):
    return jax.ShapeDtypeStruct(shape, dtype)


def call(kernel, outs, args, where=(), scratch=(), grant=24, weight=1, name=None):
    where = dict(where)
    return pl.pallas_call(
        kernel,
        out_shape=outs,
        in_specs=[
            pl.BlockSpec(memory_space=where.get(i, pltpu.VMEM)) for i in range(len(args))
        ],
        out_specs=[pl.BlockSpec(memory_space=pltpu.VMEM)] * len(outs),
        scratch_shapes=scratch,
        compiler_params=pltpu.CompilerParams(vmem_limit_bytes=grant * 1024 * 1024),
        cost_estimate=pl.CostEstimate(
            flops=weight, bytes_accessed=1, transcendentals=0
        ),
        name=name,
    )(*args)


def body(hidden, expert_ids, gate_fix, grad_out, w_down):
    tokens, top, ff = hidden.shape
    half = grad_out.shape[1]
    local, _, full = w_down.shape
    n = lax.axis_size("ctx")
    experts = n * local
    assigned = tokens * top
    cap = min(tokens, assigned // experts + max(1, assigned // (8 * experts)))
    unit = 8 if local % 2 == 0 else 16
    cap = -(-cap // unit) * unit
    width = local * cap
    dims = (experts, local, cap, width)
    run = functools.partial(call, grant=24 if n <= 4 else 56)
    place = jnp.stack([lax.axis_index("ctx"), lax.axis_index("tp")]).astype(jnp.int32)
    placed = {0: pltpu.SMEM}

    def send(x, s):
        return lax.ppermute(x, "ctx", [(i, i ^ s) for i in range(n)]) if s else x

    def swap(x):
        return lax.ppermute(x, "tp", [(0, 1), (1, 0)])

    meta = jnp.concatenate([expert_ids.T, gate_fix.T], axis=0)
    hid_t = hidden.transpose(1, 2, 0)
    named = jnp.pad(expert_ids.T.astype(BF16), ((0, 8 - top), (0, half - tokens)))
    packed = jnp.concatenate([grad_out, named], axis=0)
    forward = n == 4
    own = [send(packed, s) for s in range(n)]
    swapped = swap(packed)
    meta, swapped = lax.optimization_barrier((meta, swapped))
    hid_sent = run(
        functools.partial(dispatch_kernel, dims), [shaped((width, -(-(ff + 1) // 128) * 128))] * n,
        [place, meta, hid_t], where=placed, name="dispatch",
    )
    hid = [send(hid_sent[s], s) for s in range(n)]
    slot = shaped((width, ff))

    def swaps(xs):
        return [swap(x) for x in xs]

    if forward:
        always = place[0] < 1000
        last = lax.cond(always, swaps, list, own[3:])
        *own[1:3], last[0] = lax.optimization_barrier((*own[1:3], last[0]))
        other = [swapped] + lax.cond(always, swaps, list, own[1:3]) + last
    else:
        other = [swapped] + swaps(own[1:])
    (x,) = run(
        functools.partial(gather_kernel, dims, top), [shaped((local, n * cap, full))],
        [place, *own, *other], where=placed, name="gather", weight=15 * 10**8,
    )
    grad_sent = run(
        functools.partial(grad_kernel, dims), [slot] * n, [x, w_down], name="grad"
    )
    hid[0], grad_own = lax.optimization_barrier((hid[0], grad_sent[0]))
    grad_back = [grad_own] + [send(grad_sent[s], s) for s in range(1, n)]

    mixing = dict(where=placed)
    (theirs,) = run(
        functools.partial(mix_kernel, dims, True), [shaped((n * tokens, half))],
        [place, *hid, w_down], name="mix_sibling", **mixing,
    )
    arrived = swap(theirs)
    if forward:
        (mine,) = run(
            functools.partial(mix_kernel, dims, False), [shaped((n * tokens, half), F32)],
            [place, *hid, w_down], name="mix_own", weight=BIG, **mixing,
        )
        cut = half // 2
        kept, wide = shaped((tokens, half), F32), shaped((tokens, cut), F32)
        piece = shaped((tokens, cut))
        kept, one_low, one_high, two_low, two_high, low, high = run(
            add_split_kernel, [kept, piece, wide, wide, piece, piece, piece],
            [mine, arrived], name="add",
        )
        low, high = send(low, 1), send(high, 2)
        one_low, two_high, *grad_back[1:3] = lax.optimization_barrier(
            (one_low, two_high, *grad_back[1:3])
        )
        one_low, two_high = send(one_low, 1), send(two_high, 2)
        to_one, to_two = run(
            join_kernel, [piece] * 2, [one_high, two_low, low, high], name="join"
        )
        (mixed,) = run(
            finish_kernel, [shaped((tokens, half))],
            [kept, one_low, send(to_one, 1), send(to_two, 2), two_high], name="finish",
        )
    else:
        sums = run(
            functools.partial(mix_add_kernel, dims), [shaped((tokens, half))] * n,
            [place, *hid, w_down, arrived], name="mix_own", **mixing,
        )
        mixed = sum(send(sums[s], s).astype(F32) for s in range(n)).astype(BF16)

    (grad_t,) = run(
        functools.partial(restore_kernel, dims), [shaped((top, ff, tokens))],
        [place, meta, *grad_back], where=placed, name="restore", weight=BIG,
    )
    return mixed, grad_t.transpose(2, 0, 1)


def solution(mesh):
    placed = (
        P(("ctx", "exp"), None, "tp"),
        P(("ctx", "exp"), None),
        P(("ctx", "exp"), None),
        P(("ctx", "exp"), "tp"),
        P("ctx", "tp", None),
    )
    return jax.shard_map(
        body,
        mesh=mesh,
        in_specs=placed,
        out_specs=(P(("ctx", "exp"), "tp"), P(("ctx", "exp"), None, "tp")),
        check_vma=False,
    )
```

```python
import functools

import jax
import jax.numpy as jnp
from jax import lax
from jax.experimental import pallas as pl
from jax.experimental.pallas import tpu as pltpu
from jax.sharding import PartitionSpec as P

BF16 = jnp.bfloat16
F32 = jnp.float32
NN = (((1,), (0,)), ((), ()))
NT = (((1,), (1,)), ((), ()))
TN = (((0,), (0,)), ((), ()))
BIG = 10**11


def dot(a, b, dims):
    return lax.dot_general(a, b, dims, preferred_element_type=F32)


def iota(shape, axis):
    return lax.broadcasted_iota(jnp.int32, shape, axis)


def ones_where(mask):
    return mask.astype(F32).astype(BF16)


def earlier(tokens):
    return ones_where(iota((tokens, tokens), 0) < iota((tokens, tokens), 1))


def token_slots(ids, me, experts, local, cap, width):
    top, tokens = ids.shape
    row = iota((experts, tokens), 0)
    hits = [ids[k : k + 1, :] == row for k in range(top)]
    named = functools.reduce(jnp.logical_or, hits)
    before = dot(ones_where(named), earlier(tokens), NN)
    base = jnp.bitwise_xor(row // local, me) * width + lax.rem(row, local) * cap
    slot = before + base.astype(F32)
    return [
        jnp.sum(jnp.where(hit, slot, 0.0), axis=0, keepdims=True).astype(jnp.int32)
        for hit in hits
    ]


def named_here(ids, me, local):
    top, tokens = ids.shape
    row = iota((8, tokens), 0) + me * local
    return functools.reduce(
        jnp.logical_or, [ids[k : k + 1, :] == row for k in range(top)]
    )


def slots_by_lane(ids, me, local, cap, width):
    tokens = ids.shape[1]
    named = named_here(ids, me, local)
    before = dot(ones_where(named), earlier(tokens), NN)
    slot = before.astype(jnp.int32) + iota((8, tokens), 0) * cap
    slot = jnp.where(named, slot, -1)
    rows = iota((cap, tokens), 0)
    return [ones_where(rows + l * cap == slot[l : l + 1, :]) for l in range(local)]


def picks_of(meta, me, dims):
    experts, local, cap, width = dims
    top = meta.shape[0] // 2
    slots = token_slots(meta[:top], me, experts, local, cap, width)
    rows = iota((experts // local * width, meta.shape[1]), 0)
    picks = jnp.concatenate([ones_where(rows == slot) for slot in slots], axis=1)
    return picks, meta[top:].astype(F32) * (1.0 / 65536.0)


def dispatch_kernel(dims, place, meta_ref, hid_ref, *outs):
    width = outs[0].shape[0]
    picks, gate = picks_of(meta_ref[...], place[0], dims)
    scaled = [
        (hid_ref[k].astype(F32) * gate[k : k + 1, :]).astype(BF16)
        for k in range(hid_ref.shape[0])
    ]
    rows = jnp.concatenate(scaled, axis=1)
    spare = outs[0].shape[1] - rows.shape[0]
    tokens = hid_ref.shape[2]
    number = jnp.bitwise_and(iota((spare, rows.shape[1]), 1), tokens - 1) + 1
    number = jnp.where(iota(number.shape, 0) == 0, number.astype(F32), 0.0)
    sent = dot(picks, jnp.concatenate([rows, number.astype(BF16)], axis=0), NT)
    for s, out in enumerate(outs):
        out[...] = sent[s * width : (s + 1) * width].astype(BF16)


def by_expert(rows, local, cap):
    return [
        jnp.concatenate([r[l * cap : (l + 1) * cap] for r in rows], axis=0)
        for l in range(local)
    ]


def by_source(rows, count, cap):
    return [
        jnp.concatenate([r[s * cap : (s + 1) * cap] for r in rows], axis=0)
        for s in range(count)
    ]


def routes(dims, top, me, packed, tokens):
    experts, local, cap, width = dims
    ids = packed[tokens:, :tokens].astype(F32).astype(jnp.int32)[:top]
    return jnp.concatenate(slots_by_lane(ids, me, local, cap, width), axis=0)


def gather_rows(dims, held, halves, x_ref):
    experts, local, cap, width = dims
    tokens, half = held[0].shape[1], halves[0].shape[1]
    chunk = min(half, 512)
    for c in range(0, half, chunk):
        rows = [dot(h, ref[:tokens, c : c + chunk], NN) for h, ref in zip(held, halves)]
        for l, x in enumerate(by_expert(rows, local, cap)):
            x_ref[l, :, c : c + chunk] = x.astype(BF16)


def gather_kernel(dims, top, place, *refs):
    experts, local, cap, width = dims
    n = experts // local
    own, other, x_ref = refs[:n], refs[n:-1], refs[-1]
    half = own[0].shape[1]
    tokens = own[0].shape[0] - 8
    chunk = min(half, 512)
    held = []
    for ref in own:
        ids = ref[tokens:, :tokens].astype(F32).astype(jnp.int32)[:top]
        held.append(
            jnp.concatenate(slots_by_lane(ids, place[0], local, cap, width), axis=0)
        )
    for side, halves in ((place[1], own), (1 - place[1], other)):
        for c in range(0, half, chunk):
            rows = [dot(h, ref[:tokens, c : c + chunk], NN) for h, ref in zip(held, halves)]
            at = pl.ds(pl.multiple_of(side * half + c, chunk), chunk)
            for l, x in enumerate(by_expert(rows, local, cap)):
                x_ref[l, :, at] = x.astype(BF16)


def grad_kernel(dims, x_ref, w_ref, *outs):
    experts, local, cap, width = dims
    grads = [dot(x_ref[l], w_ref[l], NT) for l in range(local)]
    for s, rows in enumerate(by_source(grads, len(outs), cap)):
        outs[s][...] = rows.astype(BF16)


def mix_rows(dims, side, hid, w_ref, tokens, half, store):
    experts, local, cap, width = dims
    n = len(hid)
    ff = w_ref.shape[1]
    chunk = min(half, 256)
    same = ones_where(iota((tokens, tokens), 0) == iota((tokens, tokens), 1))
    held = []
    for h in hid:
        number = h[:, ff : ff + 1].astype(F32).astype(jnp.int32) - 1
        slots = ones_where(iota((width, tokens), 1) == number)
        held.append(dot(same, slots, NT).astype(BF16))
    rows = [h[:, :ff].astype(F32) for h in hid]
    x = [r.astype(BF16) for r in by_expert(rows, local, cap)]
    for c in range(0, half, chunk):
        at = pl.ds(pl.multiple_of(side * half + c, chunk), chunk)
        out = [dot(x[l], w_ref[l, :, at], NN) for l in range(local)]
        for s, rows in enumerate(by_source(out, n, cap)):
            store(s, slice(c, c + chunk), dot(held[s], rows.astype(BF16), NN))


def mix_kernel(dims, sibling, place, *refs):
    hid, (w_ref, out) = refs[:-2], refs[-2:]
    tokens = out.shape[0] // len(hid)

    def store(s, columns, part):
        out[pl.ds(s * tokens, tokens), columns] = part.astype(out.dtype)

    side = 1 - place[1] if sibling else place[1]
    mix_rows(dims, side, hid, w_ref, tokens, out.shape[1], store)


def mix_add_kernel(dims, place, *refs):
    n = (len(refs) - 2) // 2
    hid, (w_ref, arrived), outs = refs[:n], refs[n : n + 2], refs[n + 2 :]
    tokens, half = outs[0].shape

    def store(s, columns, part):
        theirs = arrived[pl.ds(s * tokens, tokens), columns].astype(F32)
        outs[s][:, columns] = (part + theirs).astype(BF16)

    mix_rows(dims, place[1], hid, w_ref, tokens, half, store)


def add_split_kernel(own, arrived, mine, one_low, one_high, two_low, two_high, low, high):
    tokens, half = mine.shape
    cut = half // 2
    parts = []
    for s in range(4):
        at = pl.ds(s * tokens, tokens)
        parts.append(own[at, :] + arrived[at, :].astype(F32))
    mine[...] = parts[0]
    one_low[...] = parts[1][:, :cut].astype(BF16)
    one_high[...] = parts[1][:, cut:]
    two_low[...] = parts[2][:, :cut]
    two_high[...] = parts[2][:, cut:].astype(BF16)
    low[...] = parts[3][:, :cut].astype(BF16)
    high[...] = parts[3][:, cut:].astype(BF16)


def join_kernel(one_high, two_low, low, high, to_one, to_two):
    to_one[...] = (one_high[...] + high[...].astype(F32)).astype(BF16)
    to_two[...] = (two_low[...] + low[...].astype(F32)).astype(BF16)


def finish_kernel(mine, one_low, one_high, two_low, two_high, out):
    cut = one_low.shape[1]
    for at, one, two in ((0, one_low, two_low), (cut, one_high, two_high)):
        total = mine[:, at : at + cut] + one[...].astype(F32) + two[...].astype(F32)
        out[:, at : at + cut] = total.astype(BF16)


def restore_kernel(dims, place, meta_ref, *refs):
    back_refs, out = refs[:-1], refs[-1]
    top, _, tokens = out.shape
    picks, gate = picks_of(meta_ref[...], place[0], dims)
    back = jnp.concatenate([ref[...] for ref in back_refs], axis=0)
    grads = dot(back, picks, TN)
    for k in range(top):
        out[k] = (grads[:, k * tokens : (k + 1) * tokens] * gate[k : k + 1, :]).astype(BF16)


def shaped(shape, dtype=BF16):
    return jax.ShapeDtypeStruct(shape, dtype)


def call(kernel, outs, args, where=(), scratch=(), grant=24, weight=1, name=None):
    where = dict(where)
    return pl.pallas_call(
        kernel,
        out_shape=outs,
        in_specs=[
            pl.BlockSpec(memory_space=where.get(i, pltpu.VMEM)) for i in range(len(args))
        ],
        out_specs=[pl.BlockSpec(memory_space=pltpu.VMEM)] * len(outs),
        scratch_shapes=scratch,
        compiler_params=pltpu.CompilerParams(vmem_limit_bytes=grant * 1024 * 1024),
        cost_estimate=pl.CostEstimate(
            flops=weight, bytes_accessed=1, transcendentals=0
        ),
        name=name,
    )(*args)


def body(hidden, expert_ids, gate_fix, grad_out, w_down):
    tokens, top, ff = hidden.shape
    half = grad_out.shape[1]
    local, _, full = w_down.shape
    n = lax.axis_size("ctx")
    experts = n * local
    assigned = tokens * top
    cap = min(tokens, assigned // experts + max(1, assigned // (8 * experts)))
    unit = 8 if local % 2 == 0 else 16
    cap = -(-cap // unit) * unit
    width = local * cap
    dims = (experts, local, cap, width)
    run = functools.partial(call, grant=24 if n <= 4 else 56)
    place = jnp.stack([lax.axis_index("ctx"), lax.axis_index("tp")]).astype(jnp.int32)
    placed = {0: pltpu.SMEM}

    def send(x, s):
        return lax.ppermute(x, "ctx", [(i, i ^ s) for i in range(n)]) if s else x

    def swap(x):
        return lax.ppermute(x, "tp", [(0, 1), (1, 0)])

    meta = jnp.concatenate([expert_ids.T, gate_fix.T], axis=0)
    hid_t = hidden.transpose(1, 2, 0)
    named = jnp.pad(expert_ids.T.astype(BF16), ((0, 8 - top), (0, half - tokens)))
    packed = jnp.concatenate([grad_out, named], axis=0)
    forward = n == 4
    own = [send(packed, s) for s in range(n)]
    swapped = swap(packed)
    meta, swapped = lax.optimization_barrier((meta, swapped))
    hid_sent = run(
        functools.partial(dispatch_kernel, dims), [shaped((width, -(-(ff + 1) // 128) * 128))] * n,
        [place, meta, hid_t], where=placed, name="dispatch",
    )
    hid = [send(hid_sent[s], s) for s in range(n)]
    slot = shaped((width, ff))

    def swaps(xs):
        return [swap(x) for x in xs]

    if forward:
        always = place[0] < 1000
        last = lax.cond(always, swaps, list, own[3:])
        *own[1:3], last[0] = lax.optimization_barrier((*own[1:3], last[0]))
        other = [swapped] + lax.cond(always, swaps, list, own[1:3]) + last
    else:
        other = [swapped] + swaps(own[1:])
    (x,) = run(
        functools.partial(gather_kernel, dims, top), [shaped((local, n * cap, full))],
        [place, *own, *other], where=placed, name="gather", weight=20 * 10**8,
    )
    grad_sent = run(
        functools.partial(grad_kernel, dims), [slot] * n, [x, w_down], name="grad"
    )
    hid[0], grad_own = lax.optimization_barrier((hid[0], grad_sent[0]))
    grad_back = [grad_own] + [send(grad_sent[s], s) for s in range(1, n)]

    mixing = dict(where=placed)
    (theirs,) = run(
        functools.partial(mix_kernel, dims, True), [shaped((n * tokens, half))],
        [place, *hid, w_down], name="mix_sibling", **mixing,
    )
    arrived = swap(theirs)
    if forward:
        (mine,) = run(
            functools.partial(mix_kernel, dims, False), [shaped((n * tokens, half), F32)],
            [place, *hid, w_down], name="mix_own", weight=BIG, **mixing,
        )
        cut = half // 2
        kept, wide = shaped((tokens, half), F32), shaped((tokens, cut), F32)
        piece = shaped((tokens, cut))
        kept, one_low, one_high, two_low, two_high, low, high = run(
            add_split_kernel, [kept, piece, wide, wide, piece, piece, piece],
            [mine, arrived], name="add",
        )
        low, high = send(low, 1), send(high, 2)
        one_low, two_high, *grad_back[1:3] = lax.optimization_barrier(
            (one_low, two_high, *grad_back[1:3])
        )
        one_low, two_high = send(one_low, 1), send(two_high, 2)
        to_one, to_two = run(
            join_kernel, [piece] * 2, [one_high, two_low, low, high], name="join"
        )
        (mixed,) = run(
            finish_kernel, [shaped((tokens, half))],
            [kept, one_low, send(to_one, 1), send(to_two, 2), two_high], name="finish",
        )
    else:
        sums = run(
            functools.partial(mix_add_kernel, dims), [shaped((tokens, half))] * n,
            [place, *hid, w_down, arrived], name="mix_own", **mixing,
        )
        mixed = sum(send(sums[s], s).astype(F32) for s in range(n)).astype(BF16)

    (grad_t,) = run(
        functools.partial(restore_kernel, dims), [shaped((top, ff, tokens))],
        [place, meta, *grad_back], where=placed, name="restore", weight=BIG,
    )
    return mixed, grad_t.transpose(2, 0, 1)


def solution(mesh):
    placed = (
        P(("ctx", "exp"), None, "tp"),
        P(("ctx", "exp"), None),
        P(("ctx", "exp"), None),
        P(("ctx", "exp"), "tp"),
        P("ctx", "tp", None),
    )
    return jax.shard_map(
        body,
        mesh=mesh,
        in_specs=placed,
        out_specs=(P(("ctx", "exp"), "tp"), P(("ctx", "exp"), None, "tp")),
        check_vma=False,
    )
```

```python
import functools

import jax
import jax.numpy as jnp
from jax import lax
from jax.experimental import pallas as pl
from jax.experimental.pallas import tpu as pltpu
from jax.sharding import PartitionSpec as P

BF16 = jnp.bfloat16
F32 = jnp.float32
NN = (((1,), (0,)), ((), ()))
NT = (((1,), (1,)), ((), ()))
TN = (((0,), (0,)), ((), ()))
BIG = 10**11


def dot(a, b, dims):
    return lax.dot_general(a, b, dims, preferred_element_type=F32)


def iota(shape, axis):
    return lax.broadcasted_iota(jnp.int32, shape, axis)


def ones_where(mask):
    return mask.astype(F32).astype(BF16)


def earlier(tokens):
    return ones_where(iota((tokens, tokens), 0) < iota((tokens, tokens), 1))


def token_slots(ids, me, experts, local, cap, width):
    top, tokens = ids.shape
    row = iota((experts, tokens), 0)
    hits = [ids[k : k + 1, :] == row for k in range(top)]
    named = functools.reduce(jnp.logical_or, hits)
    before = dot(ones_where(named), earlier(tokens), NN)
    base = jnp.bitwise_xor(row // local, me) * width + lax.rem(row, local) * cap
    slot = before + base.astype(F32)
    return [
        jnp.sum(jnp.where(hit, slot, 0.0), axis=0, keepdims=True).astype(jnp.int32)
        for hit in hits
    ]


def named_here(ids, me, local):
    top, tokens = ids.shape
    row = iota((8, tokens), 0) + me * local
    return functools.reduce(
        jnp.logical_or, [ids[k : k + 1, :] == row for k in range(top)]
    )


def slots_by_lane(ids, me, local, cap, width):
    tokens = ids.shape[1]
    named = named_here(ids, me, local)
    before = dot(ones_where(named), earlier(tokens), NN)
    slot = before.astype(jnp.int32) + iota((8, tokens), 0) * cap
    slot = jnp.where(named, slot, -1)
    rows = iota((cap, tokens), 0)
    return [ones_where(rows + l * cap == slot[l : l + 1, :]) for l in range(local)]


def packed_rows(width, ff):
    first = -(-(width // 2) // 16) * 16
    return ff // 128 * width + (first if ff % 128 else 0), first


def pack_slots(rows, out):
    width, ff = rows.shape
    full, rest = ff // 128, ff % 128
    for c in range(full):
        out[c * width : (c + 1) * width, :] = rows[:, c * 128 : (c + 1) * 128].astype(BF16)
    if rest:
        end, first = packed_rows(width, ff)
        tail = rows[:, full * 128 :]
        right = tail[first:]
        if right.shape[0] < first:
            spare = jnp.zeros((first - right.shape[0], rest), F32)
            right = jnp.concatenate([right, spare], axis=0)
        pair = jnp.concatenate([tail[:first], right], axis=1)
        out[full * width : end, :] = pair.astype(BF16)


def unpack_slots(ref, width, ff):
    full, rest = ff // 128, ff % 128
    blocks = [ref[c * width : (c + 1) * width, :].astype(F32) for c in range(full)]
    if rest:
        end, first = packed_rows(width, ff)
        pair = ref[full * width : end, :].astype(F32)
        blocks.append(
            jnp.concatenate([pair[:, :rest], pair[: width - first, rest:]], axis=0)
        )
    return jnp.concatenate(blocks, axis=1)


def picks_of(meta, me, dims):
    experts, local, cap, width = dims
    top = meta.shape[0] // 2
    slots = token_slots(meta[:top], me, experts, local, cap, width)
    rows = iota((experts // local * width, meta.shape[1]), 0)
    picks = jnp.concatenate([ones_where(rows == slot) for slot in slots], axis=1)
    return picks, meta[top:].astype(F32) * (1.0 / 65536.0)


def dispatch_kernel(dims, place, meta_ref, hid_ref, *outs):
    width = dims[3]
    picks, gate = picks_of(meta_ref[...], place[0], dims)
    scaled = [
        (hid_ref[k].astype(F32) * gate[k : k + 1, :]).astype(BF16)
        for k in range(hid_ref.shape[0])
    ]
    sent = dot(picks, jnp.concatenate(scaled, axis=1), NT)
    tokens = hid_ref.shape[2]
    number = jnp.bitwise_and(iota((8, picks.shape[1]), 1), tokens - 1) + 1
    number = number.astype(F32).astype(BF16)
    for s, out in enumerate(outs):
        at = slice(s * width, (s + 1) * width)
        pack_slots(sent[at], out)
        names = dot(number, picks[at], NT)[:1]
        if width % 128:
            spare = jnp.zeros((1, -width % 128), F32)
            names = jnp.concatenate([names, spare], axis=1)
        lines = jnp.zeros((16, 128), F32)
        for i in range(names.shape[1] // 128):
            line = names[:, i * 128 : (i + 1) * 128]
            lines = jnp.where(iota((16, 128), 0) == i, line, lines)
        out[out.shape[0] - 16 :, :] = lines.astype(BF16)


def by_expert(rows, local, cap):
    return [
        jnp.concatenate([r[l * cap : (l + 1) * cap] for r in rows], axis=0)
        for l in range(local)
    ]


def by_source(rows, count, cap):
    return [
        jnp.concatenate([r[s * cap : (s + 1) * cap] for r in rows], axis=0)
        for s in range(count)
    ]


def routes(dims, top, me, packed, tokens):
    experts, local, cap, width = dims
    ids = packed[tokens:, :tokens].astype(F32).astype(jnp.int32)[:top]
    return jnp.concatenate(slots_by_lane(ids, me, local, cap, width), axis=0)


def gather_rows(dims, held, halves, x_ref):
    experts, local, cap, width = dims
    tokens, half = held[0].shape[1], halves[0].shape[1]
    chunk = min(half, 512)
    for c in range(0, half, chunk):
        rows = [dot(h, ref[:tokens, c : c + chunk], NN) for h, ref in zip(held, halves)]
        for l, x in enumerate(by_expert(rows, local, cap)):
            x_ref[l, :, c : c + chunk] = x.astype(BF16)


def gather_kernel(dims, top, place, *refs):
    experts, local, cap, width = dims
    n = experts // local
    own, other, x_ref = refs[:n], refs[n:-1], refs[-1]
    half = own[0].shape[1]
    tokens = own[0].shape[0] - 8
    chunk = min(half, 512)
    held = []
    for ref in own:
        ids = ref[tokens:, :tokens].astype(F32).astype(jnp.int32)[:top]
        held.append(
            jnp.concatenate(slots_by_lane(ids, place[0], local, cap, width), axis=0)
        )
    for side, halves in ((place[1], own), (1 - place[1], other)):
        for c in range(0, half, chunk):
            rows = [dot(h, ref[:tokens, c : c + chunk], NN) for h, ref in zip(held, halves)]
            at = pl.ds(pl.multiple_of(side * half + c, chunk), chunk)
            for l, x in enumerate(by_expert(rows, local, cap)):
                x_ref[l, :, at] = x.astype(BF16)


def grad_kernel(dims, x_ref, w_ref, *outs):
    experts, local, cap, width = dims
    grads = [dot(x_ref[l], w_ref[l], NT) for l in range(local)]
    for s, rows in enumerate(by_source(grads, len(outs), cap)):
        pack_slots(rows, outs[s])


def mix_rows(dims, side, hid, w_ref, tokens, half, store):
    experts, local, cap, width = dims
    n = len(hid)
    ff = w_ref.shape[1]
    chunk = min(half, 256)
    held, rows = [], []
    for h in hid:
        lines = h[h.shape[0] - 16 :, :].astype(F32)
        names = jnp.concatenate(
            [lines[i // 128 : i // 128 + 1, : min(128, width - i)] for i in range(0, width, 128)],
            axis=1,
        )
        held.append(ones_where(iota((tokens, width), 0) == names.astype(jnp.int32) - 1))
        rows.append(unpack_slots(h, width, ff))
    x = [r.astype(BF16) for r in by_expert(rows, local, cap)]
    for c in range(0, half, chunk):
        at = pl.ds(pl.multiple_of(side * half + c, chunk), chunk)
        out = [dot(x[l], w_ref[l, :, at], NN) for l in range(local)]
        for s, rows in enumerate(by_source(out, n, cap)):
            store(s, slice(c, c + chunk), dot(held[s], rows.astype(BF16), NN))


def mix_kernel(dims, sibling, place, *refs):
    hid, (w_ref, out) = refs[:-2], refs[-2:]
    tokens = out.shape[0] // len(hid)

    def store(s, columns, part):
        out[pl.ds(s * tokens, tokens), columns] = part.astype(out.dtype)

    side = 1 - place[1] if sibling else place[1]
    mix_rows(dims, side, hid, w_ref, tokens, out.shape[1], store)


def mix_add_kernel(dims, place, *refs):
    n = (len(refs) - 2) // 2
    hid, (w_ref, arrived), outs = refs[:n], refs[n : n + 2], refs[n + 2 :]
    tokens, half = outs[0].shape

    def store(s, columns, part):
        theirs = arrived[pl.ds(s * tokens, tokens), columns].astype(F32)
        outs[s][:, columns] = (part + theirs).astype(BF16)

    mix_rows(dims, place[1], hid, w_ref, tokens, half, store)


def add_split_kernel(own, arrived, mine, one_low, one_high, two_low, two_high, low, high):
    tokens, half = mine.shape
    cut = half // 2
    parts = []
    for s in range(4):
        at = pl.ds(s * tokens, tokens)
        parts.append(own[at, :] + arrived[at, :].astype(F32))
    mine[...] = parts[0]
    one_low[...] = parts[1][:, :cut].astype(BF16)
    one_high[...] = parts[1][:, cut:]
    two_low[...] = parts[2][:, :cut]
    two_high[...] = parts[2][:, cut:].astype(BF16)
    low[...] = parts[3][:, :cut].astype(BF16)
    high[...] = parts[3][:, cut:].astype(BF16)


def join_kernel(one_high, two_low, low, high, to_one, to_two):
    to_one[...] = (one_high[...] + high[...].astype(F32)).astype(BF16)
    to_two[...] = (two_low[...] + low[...].astype(F32)).astype(BF16)


def finish_kernel(mine, one_low, one_high, two_low, two_high, out):
    cut = one_low.shape[1]
    for at, one, two in ((0, one_low, two_low), (cut, one_high, two_high)):
        total = mine[:, at : at + cut] + one[...].astype(F32) + two[...].astype(F32)
        out[:, at : at + cut] = total.astype(BF16)


def restore_kernel(dims, place, meta_ref, *refs):
    back_refs, out = refs[:-1], refs[-1]
    top, _, tokens = out.shape
    picks, gate = picks_of(meta_ref[...], place[0], dims)
    ff = out.shape[1]
    back = [unpack_slots(ref, dims[3], ff).astype(BF16) for ref in back_refs]
    back = jnp.concatenate(back, axis=0)
    grads = dot(back, picks, TN)
    for k in range(top):
        out[k] = (grads[:, k * tokens : (k + 1) * tokens] * gate[k : k + 1, :]).astype(BF16)


def shaped(shape, dtype=BF16):
    return jax.ShapeDtypeStruct(shape, dtype)


def call(kernel, outs, args, where=(), scratch=(), grant=24, weight=1, name=None):
    where = dict(where)
    return pl.pallas_call(
        kernel,
        out_shape=outs,
        in_specs=[
            pl.BlockSpec(memory_space=where.get(i, pltpu.VMEM)) for i in range(len(args))
        ],
        out_specs=[pl.BlockSpec(memory_space=pltpu.VMEM)] * len(outs),
        scratch_shapes=scratch,
        compiler_params=pltpu.CompilerParams(vmem_limit_bytes=grant * 1024 * 1024),
        cost_estimate=pl.CostEstimate(
            flops=weight, bytes_accessed=1, transcendentals=0
        ),
        name=name,
    )(*args)


def body(hidden, expert_ids, gate_fix, grad_out, w_down):
    tokens, top, ff = hidden.shape
    half = grad_out.shape[1]
    local, _, full = w_down.shape
    n = lax.axis_size("ctx")
    experts = n * local
    assigned = tokens * top
    cap = min(tokens, assigned // experts + max(1, assigned // (8 * experts)))
    unit = 8 if local % 2 == 0 else 16
    cap = -(-cap // unit) * unit
    width = local * cap
    dims = (experts, local, cap, width)
    run = functools.partial(call, grant=24 if n <= 4 else 56)
    place = jnp.stack([lax.axis_index("ctx"), lax.axis_index("tp")]).astype(jnp.int32)
    placed = {0: pltpu.SMEM}

    def send(x, s):
        return lax.ppermute(x, "ctx", [(i, i ^ s) for i in range(n)]) if s else x

    def swap(x):
        return lax.ppermute(x, "tp", [(0, 1), (1, 0)])

    meta = jnp.concatenate([expert_ids.T, gate_fix.T], axis=0)
    hid_t = hidden.transpose(1, 2, 0)
    named = jnp.pad(expert_ids.T.astype(BF16), ((0, 8 - top), (0, half - tokens)))
    packed = jnp.concatenate([grad_out, named], axis=0)
    forward = n == 4
    own = [send(packed, s) for s in range(n)]
    hid_sent = run(
        functools.partial(dispatch_kernel, dims), [shaped((packed_rows(width, ff)[0] + 16, 128))] * n,
        [place, meta, hid_t], where=placed, name="dispatch",
    )
    hid = [send(hid_sent[s], s) for s in range(n)]
    slot = shaped((packed_rows(width, ff)[0], 128))

    def swaps(xs):
        return [swap(x) for x in xs]

    def swaps_in_turn(xs):
        first = swap(xs[0])
        second, first = lax.optimization_barrier((xs[1], first))
        return [first, swap(second)]

    if forward:
        always = place[0] < 1000
        last, mine = lax.cond(always, swaps_in_turn, list, [own[3], own[0]])
        *own[1:3], last = lax.optimization_barrier((*own[1:3], last))
        other = [mine] + lax.cond(always, swaps, list, own[1:3]) + [last]
    else:
        other = swaps(own)
    (x,) = run(
        functools.partial(gather_kernel, dims, top), [shaped((local, n * cap, full))],
        [place, *own, *other], where=placed, name="gather", weight=20 * 10**8,
    )
    grad_sent = run(
        functools.partial(grad_kernel, dims), [slot] * n, [x, w_down], name="grad"
    )
    hid[0], grad_own = lax.optimization_barrier((hid[0], grad_sent[0]))
    grad_back = [grad_own] + [send(grad_sent[s], s) for s in range(1, n)]

    mixing = dict(where=placed)
    (theirs,) = run(
        functools.partial(mix_kernel, dims, True), [shaped((n * tokens, half))],
        [place, *hid, w_down], name="mix_sibling", **mixing,
    )
    arrived = swap(theirs)
    if forward:
        (mine,) = run(
            functools.partial(mix_kernel, dims, False), [shaped((n * tokens, half), F32)],
            [place, *hid, w_down], name="mix_own", weight=BIG, **mixing,
        )
        cut = half // 2
        kept, wide = shaped((tokens, half), F32), shaped((tokens, cut), F32)
        piece = shaped((tokens, cut))
        kept, one_low, one_high, two_low, two_high, low, high = run(
            add_split_kernel, [kept, piece, wide, wide, piece, piece, piece],
            [mine, arrived], name="add",
        )
        low, high = send(low, 1), send(high, 2)
        one_low, two_high, *grad_back[1:3] = lax.optimization_barrier(
            (one_low, two_high, *grad_back[1:3])
        )
        one_low, two_high = send(one_low, 1), send(two_high, 2)
        to_one, to_two = run(
            join_kernel, [piece] * 2, [one_high, two_low, low, high], name="join"
        )
        (mixed,) = run(
            finish_kernel, [shaped((tokens, half))],
            [kept, one_low, send(to_one, 1), send(to_two, 2), two_high], name="finish",
        )
    else:
        sums = run(
            functools.partial(mix_add_kernel, dims), [shaped((tokens, half))] * n,
            [place, *hid, w_down, arrived], name="mix_own", **mixing,
        )
        mixed = sum(send(sums[s], s).astype(F32) for s in range(n)).astype(BF16)

    (grad_t,) = run(
        functools.partial(restore_kernel, dims), [shaped((top, ff, tokens))],
        [place, meta, *grad_back], where=placed, name="restore", weight=BIG,
    )
    return mixed, grad_t.transpose(2, 0, 1)


def solution(mesh):
    placed = (
        P(("ctx", "exp"), None, "tp"),
        P(("ctx", "exp"), None),
        P(("ctx", "exp"), None),
        P(("ctx", "exp"), "tp"),
        P("ctx", "tp", None),
    )
    return jax.shard_map(
        body,
        mesh=mesh,
        in_specs=placed,
        out_specs=(P(("ctx", "exp"), "tp"), P(("ctx", "exp"), None, "tp")),
        check_vma=False,
    )
```

```python
import functools

import jax
import jax.numpy as jnp
from jax import lax
from jax.experimental import pallas as pl
from jax.experimental.pallas import tpu as pltpu
from jax.sharding import PartitionSpec as P

BF16 = jnp.bfloat16
F32 = jnp.float32
NN = (((1,), (0,)), ((), ()))
NT = (((1,), (1,)), ((), ()))
TN = (((0,), (0,)), ((), ()))
BIG = 10**11


def dot(a, b, dims):
    return lax.dot_general(a, b, dims, preferred_element_type=F32)


def iota(shape, axis):
    return lax.broadcasted_iota(jnp.int32, shape, axis)


def ones_where(mask):
    return mask.astype(F32).astype(BF16)


def earlier(tokens):
    return ones_where(iota((tokens, tokens), 0) < iota((tokens, tokens), 1))


def token_slots(ids, me, experts, local, cap, width):
    top, tokens = ids.shape
    row = iota((experts, tokens), 0)
    hits = [ids[k : k + 1, :] == row for k in range(top)]
    named = functools.reduce(jnp.logical_or, hits)
    before = dot(ones_where(named), earlier(tokens), NN)
    base = jnp.bitwise_xor(row // local, me) * width + lax.rem(row, local) * cap
    slot = before + base.astype(F32)
    return [
        jnp.sum(jnp.where(hit, slot, 0.0), axis=0, keepdims=True).astype(jnp.int32)
        for hit in hits
    ]


def named_here(ids, me, local):
    top, tokens = ids.shape
    row = iota((8, tokens), 0) + me * local
    return functools.reduce(
        jnp.logical_or, [ids[k : k + 1, :] == row for k in range(top)]
    )


def slots_by_lane(ids, me, local, cap, width):
    tokens = ids.shape[1]
    named = named_here(ids, me, local)
    before = dot(ones_where(named), earlier(tokens), NN)
    slot = before.astype(jnp.int32) + iota((8, tokens), 0) * cap
    slot = jnp.where(named, slot, -1)
    rows = iota((cap, tokens), 0)
    return [ones_where(rows + l * cap == slot[l : l + 1, :]) for l in range(local)]


def packed_rows(width, ff):
    first = -(-(width // 2) // 16) * 16
    return ff // 128 * width + (first if ff % 128 else 0), first


def pack_slots(rows, out):
    width, ff = rows.shape
    full, rest = ff // 128, ff % 128
    for c in range(full):
        out[c * width : (c + 1) * width, :] = rows[:, c * 128 : (c + 1) * 128].astype(BF16)
    if rest:
        end, first = packed_rows(width, ff)
        tail = rows[:, full * 128 :]
        right = tail[first:]
        if right.shape[0] < first:
            spare = jnp.zeros((first - right.shape[0], rest), F32)
            right = jnp.concatenate([right, spare], axis=0)
        pair = jnp.concatenate([tail[:first], right], axis=1)
        out[full * width : end, :] = pair.astype(BF16)


def unpack_slots(ref, width, ff):
    full, rest = ff // 128, ff % 128
    blocks = [ref[c * width : (c + 1) * width, :].astype(F32) for c in range(full)]
    if rest:
        end, first = packed_rows(width, ff)
        pair = ref[full * width : end, :].astype(F32)
        blocks.append(
            jnp.concatenate([pair[:, :rest], pair[: width - first, rest:]], axis=0)
        )
    return jnp.concatenate(blocks, axis=1)


def picks_of(meta, me, dims):
    experts, local, cap, width = dims
    top = meta.shape[0] // 2
    slots = token_slots(meta[:top], me, experts, local, cap, width)
    rows = iota((experts // local * width, meta.shape[1]), 0)
    picks = jnp.concatenate([ones_where(rows == slot) for slot in slots], axis=1)
    return picks, meta[top:].astype(F32) * (1.0 / 65536.0)


def dispatch_kernel(dims, place, meta_ref, hid_ref, *outs):
    width = dims[3]
    picks, gate = picks_of(meta_ref[...], place[0], dims)
    scaled = [
        (hid_ref[k].astype(F32) * gate[k : k + 1, :]).astype(BF16)
        for k in range(hid_ref.shape[0])
    ]
    sent = dot(picks, jnp.concatenate(scaled, axis=1), NT)
    tokens = hid_ref.shape[2]
    number = jnp.bitwise_and(iota((8, picks.shape[1]), 1), tokens - 1) + 1
    number = number.astype(F32).astype(BF16)
    for s, out in enumerate(outs):
        at = slice(s * width, (s + 1) * width)
        pack_slots(sent[at], out)
        names = dot(number, picks[at], NT)[:1]
        if width % 128:
            spare = jnp.zeros((1, -width % 128), F32)
            names = jnp.concatenate([names, spare], axis=1)
        lines = jnp.zeros((16, 128), F32)
        for i in range(names.shape[1] // 128):
            line = names[:, i * 128 : (i + 1) * 128]
            lines = jnp.where(iota((16, 128), 0) == i, line, lines)
        out[out.shape[0] - 16 :, :] = lines.astype(BF16)


def names_kernel(ids_ref, out):
    top, tokens = ids_ref.shape
    ids = ids_ref[...].astype(F32)
    spare = jnp.zeros((out.shape[0] - top, tokens), F32)
    out[...] = jnp.concatenate([ids, spare], axis=0).astype(BF16)


def pack_kernel(dy_ref, names_ref, out):
    tokens, half = dy_ref.shape
    for c in range(half // 128):
        out[c * tokens : (c + 1) * tokens, :] = dy_ref[:, c * 128 : (c + 1) * 128]
    out[half // 128 * tokens :, :] = names_ref[...]


def by_expert(rows, local, cap):
    return [
        jnp.concatenate([r[l * cap : (l + 1) * cap] for r in rows], axis=0)
        for l in range(local)
    ]


def by_source(rows, count, cap):
    return [
        jnp.concatenate([r[s * cap : (s + 1) * cap] for r in rows], axis=0)
        for s in range(count)
    ]


def routes(dims, top, me, packed, tokens):
    experts, local, cap, width = dims
    ids = packed[tokens:, :tokens].astype(F32).astype(jnp.int32)[:top]
    return jnp.concatenate(slots_by_lane(ids, me, local, cap, width), axis=0)


def gather_rows(dims, held, halves, x_ref):
    experts, local, cap, width = dims
    tokens, half = held[0].shape[1], halves[0].shape[1]
    chunk = min(half, 512)
    for c in range(0, half, chunk):
        rows = [dot(h, ref[:tokens, c : c + chunk], NN) for h, ref in zip(held, halves)]
        for l, x in enumerate(by_expert(rows, local, cap)):
            x_ref[l, :, c : c + chunk] = x.astype(BF16)


def gather_kernel(dims, top, tokens, place, *refs):
    experts, local, cap, width = dims
    n = experts // local
    own, other, x_ref = refs[:n], refs[n:-1], refs[-1]
    half = x_ref.shape[2] // 2
    chunk = min(half, 512)
    held = []
    for ref in own:
        ids = ref[half // 128 * tokens :, :].astype(F32).astype(jnp.int32)[:top]
        held.append(
            jnp.concatenate(slots_by_lane(ids, place[0], local, cap, width), axis=0)
        )

    def features(ref, start):
        blocks = range(start // 128, (start + chunk) // 128)
        return jnp.concatenate([ref[c * tokens : (c + 1) * tokens, :] for c in blocks], axis=1)

    for side, halves in ((place[1], own), (1 - place[1], other)):
        for c in range(0, half, chunk):
            rows = [dot(h, features(ref, c), NN) for h, ref in zip(held, halves)]
            at = pl.ds(pl.multiple_of(side * half + c, chunk), chunk)
            for l, x in enumerate(by_expert(rows, local, cap)):
                x_ref[l, :, at] = x.astype(BF16)


def grad_kernel(dims, x_ref, w_ref, *outs):
    experts, local, cap, width = dims
    grads = [dot(x_ref[l], w_ref[l], NT) for l in range(local)]
    for s, rows in enumerate(by_source(grads, len(outs), cap)):
        pack_slots(rows, outs[s])


def mix_rows(dims, side, hid, w_ref, tokens, half, store):
    experts, local, cap, width = dims
    n = len(hid)
    ff = w_ref.shape[1]
    chunk = min(half, 256)
    held, rows = [], []
    for h in hid:
        lines = h[h.shape[0] - 16 :, :].astype(F32)
        names = jnp.concatenate(
            [lines[i // 128 : i // 128 + 1, : min(128, width - i)] for i in range(0, width, 128)],
            axis=1,
        )
        held.append(ones_where(iota((tokens, width), 0) == names.astype(jnp.int32) - 1))
        rows.append(unpack_slots(h, width, ff))
    x = [r.astype(BF16) for r in by_expert(rows, local, cap)]
    for c in range(0, half, chunk):
        at = pl.ds(pl.multiple_of(side * half + c, chunk), chunk)
        out = [dot(x[l], w_ref[l, :, at], NN) for l in range(local)]
        for s, rows in enumerate(by_source(out, n, cap)):
            store(s, slice(c, c + chunk), dot(held[s], rows.astype(BF16), NN))


def mix_kernel(dims, sibling, place, *refs):
    hid, (w_ref, out) = refs[:-2], refs[-2:]
    tokens = out.shape[0] // len(hid)

    def store(s, columns, part):
        out[pl.ds(s * tokens, tokens), columns] = part.astype(out.dtype)

    side = 1 - place[1] if sibling else place[1]
    mix_rows(dims, side, hid, w_ref, tokens, out.shape[1], store)


def mix_add_kernel(dims, place, *refs):
    n = (len(refs) - 2) // 2
    hid, (w_ref, arrived), outs = refs[:n], refs[n : n + 2], refs[n + 2 :]
    tokens, half = outs[0].shape

    def store(s, columns, part):
        theirs = arrived[pl.ds(s * tokens, tokens), columns].astype(F32)
        outs[s][:, columns] = (part + theirs).astype(BF16)

    mix_rows(dims, place[1], hid, w_ref, tokens, half, store)


def add_split_kernel(own, arrived, mine, one_low, one_high, two_low, two_high, low, high):
    tokens, half = mine.shape
    cut = half // 2
    parts = []
    for s in range(4):
        at = pl.ds(s * tokens, tokens)
        parts.append(own[at, :] + arrived[at, :].astype(F32))
    mine[...] = parts[0]
    one_low[...] = parts[1][:, :cut].astype(BF16)
    one_high[...] = parts[1][:, cut:]
    two_low[...] = parts[2][:, :cut]
    two_high[...] = parts[2][:, cut:].astype(BF16)
    low[...] = parts[3][:, :cut].astype(BF16)
    high[...] = parts[3][:, cut:].astype(BF16)


def join_kernel(one_high, two_low, low, high, to_one, to_two):
    to_one[...] = (one_high[...] + high[...].astype(F32)).astype(BF16)
    to_two[...] = (two_low[...] + low[...].astype(F32)).astype(BF16)


def finish_kernel(mine, one_low, one_high, two_low, two_high, out):
    cut = one_low.shape[1]
    for at, one, two in ((0, one_low, two_low), (cut, one_high, two_high)):
        total = mine[:, at : at + cut] + one[...].astype(F32) + two[...].astype(F32)
        out[:, at : at + cut] = total.astype(BF16)


def restore_kernel(dims, place, meta_ref, *refs):
    back_refs, out = refs[:-1], refs[-1]
    top, _, tokens = out.shape
    picks, gate = picks_of(meta_ref[...], place[0], dims)
    ff = out.shape[1]
    back = [unpack_slots(ref, dims[3], ff).astype(BF16) for ref in back_refs]
    back = jnp.concatenate(back, axis=0)
    grads = dot(back, picks, TN)
    for k in range(top):
        out[k] = (grads[:, k * tokens : (k + 1) * tokens] * gate[k : k + 1, :]).astype(BF16)


def shaped(shape, dtype=BF16):
    return jax.ShapeDtypeStruct(shape, dtype)


def call(kernel, outs, args, where=(), scratch=(), grant=24, weight=1, name=None):
    where = dict(where)
    return pl.pallas_call(
        kernel,
        out_shape=outs,
        in_specs=[
            pl.BlockSpec(memory_space=where.get(i, pltpu.VMEM)) for i in range(len(args))
        ],
        out_specs=[pl.BlockSpec(memory_space=pltpu.VMEM)] * len(outs),
        scratch_shapes=scratch,
        compiler_params=pltpu.CompilerParams(vmem_limit_bytes=grant * 1024 * 1024),
        cost_estimate=pl.CostEstimate(
            flops=weight, bytes_accessed=1, transcendentals=0
        ),
        name=name,
    )(*args)


def body(hidden, expert_ids, gate_fix, grad_out, w_down):
    tokens, top, ff = hidden.shape
    half = grad_out.shape[1]
    local, _, full = w_down.shape
    n = lax.axis_size("ctx")
    experts = n * local
    assigned = tokens * top
    cap = min(tokens, assigned // experts + max(1, assigned // (8 * experts)))
    unit = 8 if local % 2 == 0 else 16
    cap = -(-cap // unit) * unit
    width = local * cap
    dims = (experts, local, cap, width)
    run = functools.partial(call, grant=24 if n <= 4 else 56)
    place = jnp.stack([lax.axis_index("ctx"), lax.axis_index("tp")]).astype(jnp.int32)
    placed = {0: pltpu.SMEM}

    def send(x, s):
        return lax.ppermute(x, "ctx", [(i, i ^ s) for i in range(n)]) if s else x

    def swap(x):
        return lax.ppermute(x, "tp", [(0, 1), (1, 0)])

    meta = jnp.concatenate([expert_ids.T, gate_fix.T], axis=0)
    hid_t = hidden.transpose(1, 2, 0)
    (names,) = run(
        names_kernel, [shaped((8, tokens))], [expert_ids.T], name="names", weight=10**9
    )
    (packed,) = run(
        pack_kernel, [shaped((half // 128 * tokens + 8, 128))], [grad_out, names], name="pack"
    )
    forward = n == 4
    own = [send(packed, s) for s in range(n)]
    hid_sent = run(
        functools.partial(dispatch_kernel, dims), [shaped((packed_rows(width, ff)[0] + 16, 128))] * n,
        [place, meta, hid_t], where=placed, name="dispatch",
    )
    hid = [send(hid_sent[s], s) for s in range(n)]
    slot = shaped((packed_rows(width, ff)[0], 128))

    def swaps(xs):
        return [swap(x) for x in xs]

    def swaps_in_turn(xs):
        first = swap(xs[0])
        second, first = lax.optimization_barrier((xs[1], first))
        return [first, swap(second)]

    if forward:
        always = place[0] < 1000
        last, mine = lax.cond(always, swaps_in_turn, list, [own[3], own[0]])
        *own[1:3], last = lax.optimization_barrier((*own[1:3], last))
        other = [mine] + lax.cond(always, swaps, list, own[1:3]) + [last]
    else:
        other = swaps(own)
    (x,) = run(
        functools.partial(gather_kernel, dims, top, tokens), [shaped((local, n * cap, full))],
        [place, *own, *other], where=placed, name="gather", weight=20 * 10**8,
    )
    grad_sent = run(
        functools.partial(grad_kernel, dims), [slot] * n, [x, w_down], name="grad"
    )
    hid[0], grad_own = lax.optimization_barrier((hid[0], grad_sent[0]))
    grad_back = [grad_own] + [send(grad_sent[s], s) for s in range(1, n)]

    mixing = dict(where=placed)
    (theirs,) = run(
        functools.partial(mix_kernel, dims, True), [shaped((n * tokens, half))],
        [place, *hid, w_down], name="mix_sibling", **mixing,
    )
    arrived = swap(theirs)
    if forward:
        (mine,) = run(
            functools.partial(mix_kernel, dims, False), [shaped((n * tokens, half), F32)],
            [place, *hid, w_down], name="mix_own", weight=BIG, **mixing,
        )
        cut = half // 2
        kept, wide = shaped((tokens, half), F32), shaped((tokens, cut), F32)
        piece = shaped((tokens, cut))
        kept, one_low, one_high, two_low, two_high, low, high = run(
            add_split_kernel, [kept, piece, wide, wide, piece, piece, piece],
            [mine, arrived], name="add",
        )
        low, high = send(low, 1), send(high, 2)
        one_low, two_high, *grad_back[1:3] = lax.optimization_barrier(
            (one_low, two_high, *grad_back[1:3])
        )
        one_low, two_high = send(one_low, 1), send(two_high, 2)
        to_one, to_two = run(
            join_kernel, [piece] * 2, [one_high, two_low, low, high], name="join"
        )
        (mixed,) = run(
            finish_kernel, [shaped((tokens, half))],
            [kept, one_low, send(to_one, 1), send(to_two, 2), two_high], name="finish",
        )
    else:
        sums = run(
            functools.partial(mix_add_kernel, dims), [shaped((tokens, half))] * n,
            [place, *hid, w_down, arrived], name="mix_own", **mixing,
        )
        mixed = sum(send(sums[s], s).astype(F32) for s in range(n)).astype(BF16)

    (grad_t,) = run(
        functools.partial(restore_kernel, dims), [shaped((top, ff, tokens))],
        [place, meta, *grad_back], where=placed, name="restore", weight=BIG,
    )
    return mixed, grad_t.transpose(2, 0, 1)


def solution(mesh):
    placed = (
        P(("ctx", "exp"), None, "tp"),
        P(("ctx", "exp"), None),
        P(("ctx", "exp"), None),
        P(("ctx", "exp"), "tp"),
        P("ctx", "tp", None),
    )
    return jax.shard_map(
        body,
        mesh=mesh,
        in_specs=placed,
        out_specs=(P(("ctx", "exp"), "tp"), P(("ctx", "exp"), None, "tp")),
        check_vma=False,
    )
```

```python
import functools

import jax
import jax.numpy as jnp
from jax import lax
from jax.experimental import pallas as pl
from jax.experimental.pallas import tpu as pltpu
from jax.sharding import PartitionSpec as P

BF16 = jnp.bfloat16
F32 = jnp.float32
NN = (((1,), (0,)), ((), ()))
NT = (((1,), (1,)), ((), ()))
TN = (((0,), (0,)), ((), ()))
BIG = 10**11


def dot(a, b, dims):
    return lax.dot_general(a, b, dims, preferred_element_type=F32)


def iota(shape, axis):
    return lax.broadcasted_iota(jnp.int32, shape, axis)


def ones_where(mask):
    return mask.astype(F32).astype(BF16)


def earlier(tokens):
    return ones_where(iota((tokens, tokens), 0) < iota((tokens, tokens), 1))


def token_slots(ids, me, experts, local, cap, width):
    top, tokens = ids.shape
    row = iota((experts, tokens), 0)
    hits = [ids[k : k + 1, :] == row for k in range(top)]
    named = functools.reduce(jnp.logical_or, hits)
    before = dot(ones_where(named), earlier(tokens), NN)
    base = jnp.bitwise_xor(row // local, me) * width + lax.rem(row, local) * cap
    slot = before + base.astype(F32)
    return [
        jnp.sum(jnp.where(hit, slot, 0.0), axis=0, keepdims=True).astype(jnp.int32)
        for hit in hits
    ]


def named_here(ids, me, local):
    top, tokens = ids.shape
    row = iota((8, tokens), 0) + me * local
    return functools.reduce(
        jnp.logical_or, [ids[k : k + 1, :] == row for k in range(top)]
    )


def slots_by_lane(ids, me, local, cap, width):
    tokens = ids.shape[1]
    named = named_here(ids, me, local)
    before = dot(ones_where(named), earlier(tokens), NN)
    slot = before.astype(jnp.int32) + iota((8, tokens), 0) * cap
    slot = jnp.where(named, slot, -1)
    rows = iota((cap, tokens), 0)
    return [ones_where(rows + l * cap == slot[l : l + 1, :]) for l in range(local)]


def packed_rows(width, ff):
    first = -(-(width // 2) // 16) * 16
    return ff // 128 * width + (first if ff % 128 else 0), first


def pack_slots(rows, out):
    width, ff = rows.shape
    full, rest = ff // 128, ff % 128
    for c in range(full):
        out[c * width : (c + 1) * width, :] = rows[:, c * 128 : (c + 1) * 128].astype(BF16)
    if rest:
        end, first = packed_rows(width, ff)
        tail = rows[:, full * 128 :]
        right = tail[first:]
        if right.shape[0] < first:
            spare = jnp.zeros((first - right.shape[0], rest), F32)
            right = jnp.concatenate([right, spare], axis=0)
        pair = jnp.concatenate([tail[:first], right], axis=1)
        out[full * width : end, :] = pair.astype(BF16)


def unpack_slots(ref, width, ff):
    full, rest = ff // 128, ff % 128
    blocks = [ref[c * width : (c + 1) * width, :].astype(F32) for c in range(full)]
    if rest:
        end, first = packed_rows(width, ff)
        pair = ref[full * width : end, :].astype(F32)
        blocks.append(
            jnp.concatenate([pair[:, :rest], pair[: width - first, rest:]], axis=0)
        )
    return jnp.concatenate(blocks, axis=1)


def picks_of(meta, me, dims):
    experts, local, cap, width = dims
    top = meta.shape[0] // 2
    slots = token_slots(meta[:top], me, experts, local, cap, width)
    rows = iota((experts // local * width, meta.shape[1]), 0)
    picks = jnp.concatenate([ones_where(rows == slot) for slot in slots], axis=1)
    return picks, meta[top:].astype(F32) * (1.0 / 65536.0)


def dispatch_kernel(dims, place, meta_ref, hid_ref, *outs):
    width = dims[3]
    picks, gate = picks_of(meta_ref[...], place[0], dims)
    scaled = [
        (hid_ref[k].astype(F32) * gate[k : k + 1, :]).astype(BF16)
        for k in range(hid_ref.shape[0])
    ]
    sent = dot(picks, jnp.concatenate(scaled, axis=1), NT)
    tokens = hid_ref.shape[2]
    number = jnp.bitwise_and(iota((8, picks.shape[1]), 1), tokens - 1) + 1
    number = number.astype(F32).astype(BF16)
    for s, out in enumerate(outs):
        at = slice(s * width, (s + 1) * width)
        pack_slots(sent[at], out)
        names = dot(number, picks[at], NT)[:1]
        if width % 128:
            spare = jnp.zeros((1, -width % 128), F32)
            names = jnp.concatenate([names, spare], axis=1)
        lines = jnp.zeros((16, 128), F32)
        for i in range(names.shape[1] // 128):
            line = names[:, i * 128 : (i + 1) * 128]
            lines = jnp.where(iota((16, 128), 0) == i, line, lines)
        out[out.shape[0] - 16 :, :] = lines.astype(BF16)


def names_kernel(ids_ref, out):
    top, tokens = ids_ref.shape
    ids = ids_ref[...].astype(F32)
    spare = jnp.zeros((out.shape[0] - top, tokens), F32)
    out[...] = jnp.concatenate([ids, spare], axis=0).astype(BF16)


def pack_kernel(dy_ref, names_ref, out):
    tokens, half = dy_ref.shape
    for c in range(half // 128):
        out[c * tokens : (c + 1) * tokens, :] = dy_ref[:, c * 128 : (c + 1) * 128]
    out[half // 128 * tokens :, :] = names_ref[...]


def by_expert(rows, local, cap):
    return [
        jnp.concatenate([r[l * cap : (l + 1) * cap] for r in rows], axis=0)
        for l in range(local)
    ]


def by_source(rows, count, cap):
    return [
        jnp.concatenate([r[s * cap : (s + 1) * cap] for r in rows], axis=0)
        for s in range(count)
    ]


def routes(dims, top, me, packed, tokens):
    experts, local, cap, width = dims
    ids = packed[tokens:, :tokens].astype(F32).astype(jnp.int32)[:top]
    return jnp.concatenate(slots_by_lane(ids, me, local, cap, width), axis=0)


def gather_rows(dims, held, halves, x_ref):
    experts, local, cap, width = dims
    tokens, half = held[0].shape[1], halves[0].shape[1]
    chunk = min(half, 512)
    for c in range(0, half, chunk):
        rows = [dot(h, ref[:tokens, c : c + chunk], NN) for h, ref in zip(held, halves)]
        for l, x in enumerate(by_expert(rows, local, cap)):
            x_ref[l, :, c : c + chunk] = x.astype(BF16)


def pass_kernel(one, two, low, high):
    rows = high.shape[0]
    low[:rows, :] = one[:rows, :]
    low[rows:, :] = one[2 * rows :, :]
    high[...] = two[rows : 2 * rows, :]


def by_part(refs, n):
    if len(refs) == n:
        return [(ref,) for ref in refs]
    return [(ref,) for ref in refs[: n - 1]] + [tuple(refs[n - 1 :])]


def gather_kernel(dims, top, tokens, place, *refs):
    experts, local, cap, width = dims
    n = experts // local
    count = len(refs) // 2
    own, other, x_ref = by_part(refs[:count], n), by_part(refs[count:-1], n), refs[-1]
    half = x_ref.shape[2] // 2
    chunk = min(half, 512)
    held = []
    for parts in own:
        end = half // 128 // len(parts) * tokens
        ids = parts[0][end:, :].astype(F32).astype(jnp.int32)[:top]
        held.append(
            jnp.concatenate(slots_by_lane(ids, place[0], local, cap, width), axis=0)
        )

    def features(parts, start):
        size = half // len(parts)
        ref, start = parts[start // size], start % size
        blocks = range(start // 128, (start + chunk) // 128)
        return jnp.concatenate([ref[c * tokens : (c + 1) * tokens, :] for c in blocks], axis=1)

    for side, halves in ((place[1], own), (1 - place[1], other)):
        for c in range(0, half, chunk):
            rows = [dot(h, features(parts, c), NN) for h, parts in zip(held, halves)]
            at = pl.ds(pl.multiple_of(side * half + c, chunk), chunk)
            for l, x in enumerate(by_expert(rows, local, cap)):
                x_ref[l, :, at] = x.astype(BF16)


def grad_kernel(dims, x_ref, w_ref, *outs):
    experts, local, cap, width = dims
    grads = [dot(x_ref[l], w_ref[l], NT) for l in range(local)]
    for s, rows in enumerate(by_source(grads, len(outs), cap)):
        pack_slots(rows, outs[s])


def mix_rows(dims, side, hid, w_ref, tokens, half, store):
    experts, local, cap, width = dims
    n = len(hid)
    ff = w_ref.shape[1]
    chunk = min(half, 256)
    held, rows = [], []
    for h in hid:
        lines = h[h.shape[0] - 16 :, :].astype(F32)
        names = jnp.concatenate(
            [lines[i // 128 : i // 128 + 1, : min(128, width - i)] for i in range(0, width, 128)],
            axis=1,
        )
        held.append(ones_where(iota((tokens, width), 0) == names.astype(jnp.int32) - 1))
        rows.append(unpack_slots(h, width, ff))
    x = [r.astype(BF16) for r in by_expert(rows, local, cap)]
    for c in range(0, half, chunk):
        at = pl.ds(pl.multiple_of(side * half + c, chunk), chunk)
        out = [dot(x[l], w_ref[l, :, at], NN) for l in range(local)]
        for s, rows in enumerate(by_source(out, n, cap)):
            store(s, slice(c, c + chunk), dot(held[s], rows.astype(BF16), NN))


def mix_kernel(dims, sibling, place, *refs):
    hid, (w_ref, out) = refs[:-2], refs[-2:]
    tokens = out.shape[0] // len(hid)

    def store(s, columns, part):
        out[pl.ds(s * tokens, tokens), columns] = part.astype(out.dtype)

    side = 1 - place[1] if sibling else place[1]
    mix_rows(dims, side, hid, w_ref, tokens, out.shape[1], store)


def mix_add_kernel(dims, place, *refs):
    n = (len(refs) - 2) // 2
    hid, (w_ref, arrived), outs = refs[:n], refs[n : n + 2], refs[n + 2 :]
    tokens, half = outs[0].shape

    def store(s, columns, part):
        theirs = arrived[pl.ds(s * tokens, tokens), columns].astype(F32)
        outs[s][:, columns] = (part + theirs).astype(BF16)

    mix_rows(dims, place[1], hid, w_ref, tokens, half, store)


def add_split_kernel(own, arrived, mine, one_low, one_high, two_low, two_high, low, high):
    tokens, half = mine.shape
    cut = half // 2
    parts = []
    for s in range(4):
        at = pl.ds(s * tokens, tokens)
        parts.append(own[at, :] + arrived[at, :].astype(F32))
    mine[...] = parts[0]
    one_low[...] = parts[1][:, :cut].astype(BF16)
    one_high[...] = parts[1][:, cut:]
    two_low[...] = parts[2][:, :cut]
    two_high[...] = parts[2][:, cut:].astype(BF16)
    low[...] = parts[3][:, :cut].astype(BF16)
    high[...] = parts[3][:, cut:].astype(BF16)


def join_kernel(one_high, two_low, low, high, to_one, to_two):
    to_one[...] = (one_high[...] + high[...].astype(F32)).astype(BF16)
    to_two[...] = (two_low[...] + low[...].astype(F32)).astype(BF16)


def finish_kernel(mine, one_low, one_high, two_low, two_high, out):
    cut = one_low.shape[1]
    for at, one, two in ((0, one_low, two_low), (cut, one_high, two_high)):
        total = mine[:, at : at + cut] + one[...].astype(F32) + two[...].astype(F32)
        out[:, at : at + cut] = total.astype(BF16)


def restore_kernel(dims, place, meta_ref, *refs):
    back_refs, out = refs[:-1], refs[-1]
    top, _, tokens = out.shape
    picks, gate = picks_of(meta_ref[...], place[0], dims)
    ff = out.shape[1]
    back = [unpack_slots(ref, dims[3], ff).astype(BF16) for ref in back_refs]
    back = jnp.concatenate(back, axis=0)
    grads = dot(back, picks, TN)
    for k in range(top):
        out[k] = (grads[:, k * tokens : (k + 1) * tokens] * gate[k : k + 1, :]).astype(BF16)


def shaped(shape, dtype=BF16):
    return jax.ShapeDtypeStruct(shape, dtype)


def call(kernel, outs, args, where=(), scratch=(), grant=24, weight=1, name=None):
    where = dict(where)
    return pl.pallas_call(
        kernel,
        out_shape=outs,
        in_specs=[
            pl.BlockSpec(memory_space=where.get(i, pltpu.VMEM)) for i in range(len(args))
        ],
        out_specs=[pl.BlockSpec(memory_space=pltpu.VMEM)] * len(outs),
        scratch_shapes=scratch,
        compiler_params=pltpu.CompilerParams(vmem_limit_bytes=grant * 1024 * 1024),
        cost_estimate=pl.CostEstimate(
            flops=weight, bytes_accessed=1, transcendentals=0
        ),
        name=name,
    )(*args)


def body(hidden, expert_ids, gate_fix, grad_out, w_down):
    tokens, top, ff = hidden.shape
    half = grad_out.shape[1]
    local, _, full = w_down.shape
    n = lax.axis_size("ctx")
    experts = n * local
    assigned = tokens * top
    cap = min(tokens, assigned // experts + max(1, assigned // (8 * experts)))
    unit = 8 if local % 2 == 0 else 16
    cap = -(-cap // unit) * unit
    width = local * cap
    dims = (experts, local, cap, width)
    run = functools.partial(call, grant=24 if n <= 4 else 56)
    place = jnp.stack([lax.axis_index("ctx"), lax.axis_index("tp")]).astype(jnp.int32)
    placed = {0: pltpu.SMEM}

    def send(x, s):
        return lax.ppermute(x, "ctx", [(i, i ^ s) for i in range(n)]) if s else x

    def swap(x):
        return lax.ppermute(x, "tp", [(0, 1), (1, 0)])

    meta = jnp.concatenate([expert_ids.T, gate_fix.T], axis=0)
    hid_t = hidden.transpose(1, 2, 0)
    (names,) = run(
        names_kernel, [shaped((8, tokens))], [expert_ids.T], name="names", weight=10**9
    )
    (packed,) = run(
        pack_kernel, [shaped((half // 128 * tokens + 8, 128))], [grad_out, names], name="pack"
    )
    forward = n == 4
    near = 3 if forward else n
    own = [send(packed, s) for s in range(near)]
    hid_sent = run(
        functools.partial(dispatch_kernel, dims),
        [shaped((packed_rows(width, ff)[0] + 16, 128))] * n,
        [place, meta, hid_t], where=placed, name="dispatch",
    )
    slot = shaped((packed_rows(width, ff)[0], 128))

    def swaps(xs):
        return [swap(x) for x in xs]

    def swaps_by_two(xs):
        first = swaps(xs[:2])
        *rest, first[0], first[1] = lax.optimization_barrier((*xs[2:], *first))
        return first + swaps(rest)

    if forward:
        always = place[0] < 1000
        hid_own = hid_sent[0]
        mine = lax.cond(always, swap, lambda x: x, packed)
        *own[1:], mine, hid_own = lax.optimization_barrier((*own[1:], mine, hid_own))
        rows = half // 256 * tokens
        low, high = run(
            pass_kernel, [shaped((rows + 8, 128)), shaped((rows, 128))], own[1:], name="pass"
        )
        own += [send(low, 2), send(high, 1)]
        hid = [hid_own] + [send(hid_sent[s], s) for s in range(1, n)]
        other = [mine] + lax.cond(always, swaps_by_two, list, own[1:])
    else:
        hid = [send(hid_sent[s], s) for s in range(n)]
        other = swaps(own)
    (x,) = run(
        functools.partial(gather_kernel, dims, top, tokens), [shaped((local, n * cap, full))],
        [place, *own, *other], where=placed, name="gather", weight=20 * 10**8,
    )
    grad_sent = run(
        functools.partial(grad_kernel, dims), [slot] * n, [x, w_down], name="grad"
    )
    hid[0], grad_own = lax.optimization_barrier((hid[0], grad_sent[0]))
    grad_back = [grad_own] + [send(grad_sent[s], s) for s in range(1, n)]

    mixing = dict(where=placed)
    (theirs,) = run(
        functools.partial(mix_kernel, dims, True), [shaped((n * tokens, half))],
        [place, *hid, w_down], name="mix_sibling", **mixing,
    )
    arrived = swap(theirs)
    if forward:
        (mine,) = run(
            functools.partial(mix_kernel, dims, False), [shaped((n * tokens, half), F32)],
            [place, *hid, w_down], name="mix_own", weight=BIG, **mixing,
        )
        cut = half // 2
        kept, wide = shaped((tokens, half), F32), shaped((tokens, cut), F32)
        piece = shaped((tokens, cut))
        kept, one_low, one_high, two_low, two_high, low, high = run(
            add_split_kernel, [kept, piece, wide, wide, piece, piece, piece],
            [mine, arrived], name="add",
        )
        low, high = send(low, 1), send(high, 2)
        one_low, two_high, *grad_back[1:3] = lax.optimization_barrier(
            (one_low, two_high, *grad_back[1:3])
        )
        one_low, two_high = send(one_low, 1), send(two_high, 2)
        to_one, to_two = run(
            join_kernel, [piece] * 2, [one_high, two_low, low, high], name="join"
        )
        (mixed,) = run(
            finish_kernel, [shaped((tokens, half))],
            [kept, one_low, send(to_one, 1), send(to_two, 2), two_high], name="finish",
        )
    else:
        sums = run(
            functools.partial(mix_add_kernel, dims), [shaped((tokens, half))] * n,
            [place, *hid, w_down, arrived], name="mix_own", **mixing,
        )
        mixed = sum(send(sums[s], s).astype(F32) for s in range(n)).astype(BF16)

    (grad_t,) = run(
        functools.partial(restore_kernel, dims), [shaped((top, ff, tokens))],
        [place, meta, *grad_back], where=placed, name="restore", weight=BIG,
    )
    return mixed, grad_t.transpose(2, 0, 1)


def solution(mesh):
    placed = (
        P(("ctx", "exp"), None, "tp"),
        P(("ctx", "exp"), None),
        P(("ctx", "exp"), None),
        P(("ctx", "exp"), "tp"),
        P("ctx", "tp", None),
    )
    return jax.shard_map(
        body,
        mesh=mesh,
        in_specs=placed,
        out_specs=(P(("ctx", "exp"), "tp"), P(("ctx", "exp"), None, "tp")),
        check_vma=False,
    )
```

```python
import functools

import jax
import jax.numpy as jnp
from jax import lax
from jax.experimental import pallas as pl
from jax.experimental.pallas import tpu as pltpu
from jax.sharding import PartitionSpec as P

BF16 = jnp.bfloat16
F32 = jnp.float32
NN = (((1,), (0,)), ((), ()))
NT = (((1,), (1,)), ((), ()))
TN = (((0,), (0,)), ((), ()))
BIG = 10**11


def dot(a, b, dims):
    return lax.dot_general(a, b, dims, preferred_element_type=F32)


def iota(shape, axis):
    return lax.broadcasted_iota(jnp.int32, shape, axis)


def ones_where(mask):
    return mask.astype(F32).astype(BF16)


def earlier(tokens):
    return ones_where(iota((tokens, tokens), 0) < iota((tokens, tokens), 1))


def token_slots(ids, me, experts, local, cap, width):
    top, tokens = ids.shape
    row = iota((experts, tokens), 0)
    hits = [ids[k : k + 1, :] == row for k in range(top)]
    named = functools.reduce(jnp.logical_or, hits)
    before = dot(ones_where(named), earlier(tokens), NN)
    base = jnp.bitwise_xor(row // local, me) * width + lax.rem(row, local) * cap
    slot = before + base.astype(F32)
    return [
        jnp.sum(jnp.where(hit, slot, 0.0), axis=0, keepdims=True).astype(jnp.int32)
        for hit in hits
    ]


def named_here(ids, me, local):
    top, tokens = ids.shape
    row = iota((8, tokens), 0) + me * local
    return functools.reduce(
        jnp.logical_or, [ids[k : k + 1, :] == row for k in range(top)]
    )


def slots_by_lane(ids, me, local, cap, width):
    tokens = ids.shape[1]
    named = named_here(ids, me, local)
    before = dot(ones_where(named), earlier(tokens), NN)
    slot = before.astype(jnp.int32) + iota((8, tokens), 0) * cap
    slot = jnp.where(named, slot, -1)
    rows = iota((cap, tokens), 0)
    return [ones_where(rows + l * cap == slot[l : l + 1, :]) for l in range(local)]


def packed_rows(width, ff):
    first = -(-(width // 2) // 16) * 16
    return ff // 128 * width + (first if ff % 128 else 0), first


def pack_slots(rows, out):
    width, ff = rows.shape
    full, rest = ff // 128, ff % 128
    for c in range(full):
        out[c * width : (c + 1) * width, :] = rows[:, c * 128 : (c + 1) * 128].astype(BF16)
    if rest:
        end, first = packed_rows(width, ff)
        tail = rows[:, full * 128 :]
        right = tail[first:]
        if right.shape[0] < first:
            spare = jnp.zeros((first - right.shape[0], rest), F32)
            right = jnp.concatenate([right, spare], axis=0)
        pair = jnp.concatenate([tail[:first], right], axis=1)
        out[full * width : end, :] = pair.astype(BF16)


def unpack_slots(ref, width, ff):
    full, rest = ff // 128, ff % 128
    blocks = [ref[c * width : (c + 1) * width, :].astype(F32) for c in range(full)]
    if rest:
        end, first = packed_rows(width, ff)
        pair = ref[full * width : end, :].astype(F32)
        blocks.append(
            jnp.concatenate([pair[:, :rest], pair[: width - first, rest:]], axis=0)
        )
    return jnp.concatenate(blocks, axis=1)


def picks_of(meta, me, dims):
    experts, local, cap, width = dims
    top = meta.shape[0] // 2
    slots = token_slots(meta[:top], me, experts, local, cap, width)
    rows = iota((experts // local * width, meta.shape[1]), 0)
    picks = jnp.concatenate([ones_where(rows == slot) for slot in slots], axis=1)
    return picks, meta[top:].astype(F32) * (1.0 / 65536.0)


def dispatch_kernel(dims, place, meta_ref, hid_ref, *outs):
    width = dims[3]
    picks, gate = picks_of(meta_ref[...], place[0], dims)
    scaled = [
        (hid_ref[k].astype(F32) * gate[k : k + 1, :]).astype(BF16)
        for k in range(hid_ref.shape[0])
    ]
    sent = dot(picks, jnp.concatenate(scaled, axis=1), NT)
    tokens = hid_ref.shape[2]
    number = jnp.bitwise_and(iota((8, picks.shape[1]), 1), tokens - 1) + 1
    number = number.astype(F32).astype(BF16)
    for s, out in enumerate(outs):
        at = slice(s * width, (s + 1) * width)
        pack_slots(sent[at], out)
        names = dot(number, picks[at], NT)[:1]
        if width % 128:
            spare = jnp.zeros((1, -width % 128), F32)
            names = jnp.concatenate([names, spare], axis=1)
        lines = jnp.zeros((16, 128), F32)
        for i in range(names.shape[1] // 128):
            line = names[:, i * 128 : (i + 1) * 128]
            lines = jnp.where(iota((16, 128), 0) == i, line, lines)
        out[out.shape[0] - 16 :, :] = lines.astype(BF16)


def names_kernel(ids_ref, out):
    top, tokens = ids_ref.shape
    ids = ids_ref[...].astype(F32)
    spare = jnp.zeros((out.shape[0] - top, tokens), F32)
    out[...] = jnp.concatenate([ids, spare], axis=0).astype(BF16)


def pack_kernel(dy_ref, names_ref, out):
    tokens, half = dy_ref.shape
    for c in range(half // 128):
        out[c * tokens : (c + 1) * tokens, :] = dy_ref[:, c * 128 : (c + 1) * 128]
    out[half // 128 * tokens :, :] = names_ref[...]


def by_expert(rows, local, cap):
    return [
        jnp.concatenate([r[l * cap : (l + 1) * cap] for r in rows], axis=0)
        for l in range(local)
    ]


def by_source(rows, count, cap):
    return [
        jnp.concatenate([r[s * cap : (s + 1) * cap] for r in rows], axis=0)
        for s in range(count)
    ]


def routes(dims, top, me, packed, tokens):
    experts, local, cap, width = dims
    ids = packed[tokens:, :tokens].astype(F32).astype(jnp.int32)[:top]
    return jnp.concatenate(slots_by_lane(ids, me, local, cap, width), axis=0)


def gather_rows(dims, held, halves, x_ref):
    experts, local, cap, width = dims
    tokens, half = held[0].shape[1], halves[0].shape[1]
    chunk = min(half, 512)
    for c in range(0, half, chunk):
        rows = [dot(h, ref[:tokens, c : c + chunk], NN) for h, ref in zip(held, halves)]
        for l, x in enumerate(by_expert(rows, local, cap)):
            x_ref[l, :, c : c + chunk] = x.astype(BF16)


def gather_kernel(dims, top, tokens, count, place, *refs):
    experts, local, cap, width = dims
    n = experts // local
    names, own, other, x_ref = refs[:count], refs[count : count + n], refs[count + n : -1], refs[-1]
    half = x_ref.shape[2] // 2
    chunk = min(half, 512)
    held = []
    for s, ref in enumerate(own):
        ids = names[s][...] if s < count else ref[half // 128 * tokens :, :]
        ids = ids.astype(F32).astype(jnp.int32)[:top]
        held.append(
            jnp.concatenate(slots_by_lane(ids, place[0], local, cap, width), axis=0)
        )

    def features(ref, start):
        if ref.shape[1] == half:
            return ref[:, start : start + chunk]
        blocks = range(start // 128, (start + chunk) // 128)
        return jnp.concatenate([ref[c * tokens : (c + 1) * tokens, :] for c in blocks], axis=1)

    for side, halves in ((place[1], own), (1 - place[1], other)):
        for c in range(0, half, chunk):
            rows = [dot(h, features(ref, c), NN) for h, ref in zip(held, halves)]
            at = pl.ds(pl.multiple_of(side * half + c, chunk), chunk)
            for l, x in enumerate(by_expert(rows, local, cap)):
                x_ref[l, :, at] = x.astype(BF16)


def grad_kernel(dims, x_ref, w_ref, *outs):
    experts, local, cap, width = dims
    grads = [dot(x_ref[l], w_ref[l], NT) for l in range(local)]
    for s, rows in enumerate(by_source(grads, len(outs), cap)):
        pack_slots(rows, outs[s])


def mix_rows(dims, side, hid, w_ref, tokens, half, store):
    experts, local, cap, width = dims
    n = len(hid)
    ff = w_ref.shape[1]
    chunk = min(half, 256)
    held, rows = [], []
    for h in hid:
        lines = h[h.shape[0] - 16 :, :].astype(F32)
        names = jnp.concatenate(
            [lines[i // 128 : i // 128 + 1, : min(128, width - i)] for i in range(0, width, 128)],
            axis=1,
        )
        held.append(ones_where(iota((tokens, width), 0) == names.astype(jnp.int32) - 1))
        rows.append(unpack_slots(h, width, ff))
    x = [r.astype(BF16) for r in by_expert(rows, local, cap)]
    for c in range(0, half, chunk):
        at = pl.ds(pl.multiple_of(side * half + c, chunk), chunk)
        out = [dot(x[l], w_ref[l, :, at], NN) for l in range(local)]
        for s, rows in enumerate(by_source(out, n, cap)):
            store(s, slice(c, c + chunk), dot(held[s], rows.astype(BF16), NN))


def mix_kernel(dims, sibling, place, *refs):
    hid, (w_ref, out) = refs[:-2], refs[-2:]
    tokens = out.shape[0] // len(hid)

    def store(s, columns, part):
        out[pl.ds(s * tokens, tokens), columns] = part.astype(out.dtype)

    side = 1 - place[1] if sibling else place[1]
    mix_rows(dims, side, hid, w_ref, tokens, out.shape[1], store)


def mix_add_kernel(dims, place, *refs):
    n = (len(refs) - 2) // 2
    hid, (w_ref, arrived), outs = refs[:n], refs[n : n + 2], refs[n + 2 :]
    tokens, half = outs[0].shape

    def store(s, columns, part):
        theirs = arrived[pl.ds(s * tokens, tokens), columns].astype(F32)
        outs[s][:, columns] = (part + theirs).astype(BF16)

    mix_rows(dims, place[1], hid, w_ref, tokens, half, store)


def add_split_kernel(own, arrived, mine, one_low, one_high, two_low, two_high, low, high):
    tokens, half = mine.shape
    cut = half // 2
    parts = []
    for s in range(4):
        at = pl.ds(s * tokens, tokens)
        parts.append(own[at, :] + arrived[at, :].astype(F32))
    mine[...] = parts[0]
    one_low[...] = parts[1][:, :cut].astype(BF16)
    one_high[...] = parts[1][:, cut:]
    two_low[...] = parts[2][:, :cut]
    two_high[...] = parts[2][:, cut:].astype(BF16)
    low[...] = parts[3][:, :cut].astype(BF16)
    high[...] = parts[3][:, cut:].astype(BF16)


def join_kernel(one_high, two_low, low, high, to_one, to_two):
    to_one[...] = (one_high[...] + high[...].astype(F32)).astype(BF16)
    to_two[...] = (two_low[...] + low[...].astype(F32)).astype(BF16)


def finish_kernel(mine, one_low, one_high, two_low, two_high, out):
    cut = one_low.shape[1]
    for at, one, two in ((0, one_low, two_low), (cut, one_high, two_high)):
        total = mine[:, at : at + cut] + one[...].astype(F32) + two[...].astype(F32)
        out[:, at : at + cut] = total.astype(BF16)


def restore_kernel(dims, place, meta_ref, *refs):
    back_refs, out = refs[:-1], refs[-1]
    top, _, tokens = out.shape
    picks, gate = picks_of(meta_ref[...], place[0], dims)
    ff = out.shape[1]
    back = [unpack_slots(ref, dims[3], ff).astype(BF16) for ref in back_refs]
    back = jnp.concatenate(back, axis=0)
    grads = dot(back, picks, TN)
    for k in range(top):
        out[k] = (grads[:, k * tokens : (k + 1) * tokens] * gate[k : k + 1, :]).astype(BF16)


def shaped(shape, dtype=BF16):
    return jax.ShapeDtypeStruct(shape, dtype)


def call(kernel, outs, args, where=(), scratch=(), grant=24, weight=1, name=None):
    where = dict(where)
    return pl.pallas_call(
        kernel,
        out_shape=outs,
        in_specs=[
            pl.BlockSpec(memory_space=where.get(i, pltpu.VMEM)) for i in range(len(args))
        ],
        out_specs=[pl.BlockSpec(memory_space=pltpu.VMEM)] * len(outs),
        scratch_shapes=scratch,
        compiler_params=pltpu.CompilerParams(vmem_limit_bytes=grant * 1024 * 1024),
        cost_estimate=pl.CostEstimate(
            flops=weight, bytes_accessed=1, transcendentals=0
        ),
        name=name,
    )(*args)


def body(hidden, expert_ids, gate_fix, grad_out, w_down):
    tokens, top, ff = hidden.shape
    half = grad_out.shape[1]
    local, _, full = w_down.shape
    n = lax.axis_size("ctx")
    experts = n * local
    assigned = tokens * top
    cap = min(tokens, assigned // experts + max(1, assigned // (8 * experts)))
    unit = 8 if local % 2 == 0 else 16
    cap = -(-cap // unit) * unit
    width = local * cap
    dims = (experts, local, cap, width)
    run = functools.partial(call, grant=24 if n <= 4 else 56)
    place = jnp.stack([lax.axis_index("ctx"), lax.axis_index("tp")]).astype(jnp.int32)
    placed = {0: pltpu.SMEM}

    def send(x, s):
        return lax.ppermute(x, "ctx", [(i, i ^ s) for i in range(n)]) if s else x

    def swap(x):
        return lax.ppermute(x, "tp", [(0, 1), (1, 0)])

    meta = jnp.concatenate([expert_ids.T, gate_fix.T], axis=0)
    hid_t = hidden.transpose(1, 2, 0)
    (names,) = run(
        names_kernel, [shaped((8, tokens))], [expert_ids.T], name="names", weight=10**9
    )
    (packed,) = run(
        pack_kernel, [shaped((half // 128 * tokens + 8, 128))], [grad_out, names], name="pack"
    )
    forward = n == 4
    count = 3 if forward else n
    own = [send(grad_out if s < count else packed, s) for s in range(n)]
    ids = [send(names, s) for s in range(count)]
    hid_sent = run(
        functools.partial(dispatch_kernel, dims), [shaped((packed_rows(width, ff)[0] + 16, 128))] * n,
        [place, meta, hid_t], where=placed, name="dispatch",
    )
    hid = [send(hid_sent[s], s) for s in range(n)]
    slot = shaped((packed_rows(width, ff)[0], 128))

    def swaps(xs):
        return [swap(x) for x in xs]

    def swaps_by_two(xs):
        first = swaps(xs[:2])
        *rest, first[0], first[1] = lax.optimization_barrier((*xs[2:], *first))
        return first + swaps(rest)

    if forward:
        always = place[0] < 1000
        *own[1:3], ids[1], ids[2], hid[0] = lax.optimization_barrier(
            (*own[1:3], ids[1], ids[2], hid[0])
        )
        one, two, mine = lax.cond(always, swaps_by_two, list, [own[1], own[2], grad_out])
        own[3], mine = lax.optimization_barrier((own[3], mine))
        other = [mine, one, two] + lax.cond(always, swaps, list, own[3:])
    else:
        other = swaps(own)
    (x,) = run(
        functools.partial(gather_kernel, dims, top, tokens, count),
        [shaped((local, n * cap, full))],
        [place, *ids, *own, *other], where=placed, name="gather", weight=20 * 10**8,
    )
    grad_sent = run(
        functools.partial(grad_kernel, dims), [slot] * n, [x, w_down], name="grad"
    )
    hid[0], grad_own = lax.optimization_barrier((hid[0], grad_sent[0]))
    grad_back = [grad_own] + [send(grad_sent[s], s) for s in range(1, n)]

    mixing = dict(where=placed)
    (theirs,) = run(
        functools.partial(mix_kernel, dims, True), [shaped((n * tokens, half))],
        [place, *hid, w_down], name="mix_sibling", **mixing,
    )
    arrived = swap(theirs)
    if forward:
        (mine,) = run(
            functools.partial(mix_kernel, dims, False), [shaped((n * tokens, half), F32)],
            [place, *hid, w_down], name="mix_own", weight=BIG, **mixing,
        )
        cut = half // 2
        kept, wide = shaped((tokens, half), F32), shaped((tokens, cut), F32)
        piece = shaped((tokens, cut))
        kept, one_low, one_high, two_low, two_high, low, high = run(
            add_split_kernel, [kept, piece, wide, wide, piece, piece, piece],
            [mine, arrived], name="add",
        )
        low, high = send(low, 1), send(high, 2)
        one_low, two_high, *grad_back[1:3] = lax.optimization_barrier(
            (one_low, two_high, *grad_back[1:3])
        )
        one_low, two_high = send(one_low, 1), send(two_high, 2)
        to_one, to_two = run(
            join_kernel, [piece] * 2, [one_high, two_low, low, high], name="join"
        )
        (mixed,) = run(
            finish_kernel, [shaped((tokens, half))],
            [kept, one_low, send(to_one, 1), send(to_two, 2), two_high], name="finish",
        )
    else:
        sums = run(
            functools.partial(mix_add_kernel, dims), [shaped((tokens, half))] * n,
            [place, *hid, w_down, arrived], name="mix_own", **mixing,
        )
        mixed = sum(send(sums[s], s).astype(F32) for s in range(n)).astype(BF16)

    (grad_t,) = run(
        functools.partial(restore_kernel, dims), [shaped((top, ff, tokens))],
        [place, meta, *grad_back], where=placed, name="restore", weight=BIG,
    )
    return mixed, grad_t.transpose(2, 0, 1)


def solution(mesh):
    placed = (
        P(("ctx", "exp"), None, "tp"),
        P(("ctx", "exp"), None),
        P(("ctx", "exp"), None),
        P(("ctx", "exp"), "tp"),
        P("ctx", "tp", None),
    )
    return jax.shard_map(
        body,
        mesh=mesh,
        in_specs=placed,
        out_specs=(P(("ctx", "exp"), "tp"), P(("ctx", "exp"), None, "tp")),
        check_vma=False,
    )
```

```python
import functools

import jax
import jax.numpy as jnp
from jax import lax
from jax.experimental import pallas as pl
from jax.experimental.pallas import tpu as pltpu
from jax.sharding import PartitionSpec as P

BF16 = jnp.bfloat16
F32 = jnp.float32
NN = (((1,), (0,)), ((), ()))
NT = (((1,), (1,)), ((), ()))
TN = (((0,), (0,)), ((), ()))
BIG = 10**11


def dot(a, b, dims):
    return lax.dot_general(a, b, dims, preferred_element_type=F32)


def iota(shape, axis):
    return lax.broadcasted_iota(jnp.int32, shape, axis)


def ones_where(mask):
    return mask.astype(F32).astype(BF16)


def earlier(tokens):
    return ones_where(iota((tokens, tokens), 0) < iota((tokens, tokens), 1))


def token_slots(ids, me, experts, local, cap, width):
    top, tokens = ids.shape
    row = iota((experts, tokens), 0)
    hits = [ids[k : k + 1, :] == row for k in range(top)]
    named = functools.reduce(jnp.logical_or, hits)
    before = dot(ones_where(named), earlier(tokens), NN)
    base = jnp.bitwise_xor(row // local, me) * width + lax.rem(row, local) * cap
    slot = before + base.astype(F32)
    return [
        jnp.sum(jnp.where(hit, slot, 0.0), axis=0, keepdims=True).astype(jnp.int32)
        for hit in hits
    ]


def named_here(ids, me, local):
    top, tokens = ids.shape
    row = iota((8, tokens), 0) + me * local
    return functools.reduce(
        jnp.logical_or, [ids[k : k + 1, :] == row for k in range(top)]
    )


def slots_by_lane(ids, me, local, cap, width):
    tokens = ids.shape[1]
    named = named_here(ids, me, local)
    before = dot(ones_where(named), earlier(tokens), NN)
    slot = before.astype(jnp.int32) + iota((8, tokens), 0) * cap
    slot = jnp.where(named, slot, -1)
    rows = iota((cap, tokens), 0)
    return [ones_where(rows + l * cap == slot[l : l + 1, :]) for l in range(local)]


def packed_rows(width, ff):
    first = -(-(width // 2) // 16) * 16
    return ff // 128 * width + (first if ff % 128 else 0), first


def pack_slots(rows, out):
    width, ff = rows.shape
    full, rest = ff // 128, ff % 128
    for c in range(full):
        out[c * width : (c + 1) * width, :] = rows[:, c * 128 : (c + 1) * 128].astype(BF16)
    if rest:
        end, first = packed_rows(width, ff)
        tail = rows[:, full * 128 :]
        right = tail[first:]
        if right.shape[0] < first:
            spare = jnp.zeros((first - right.shape[0], rest), F32)
            right = jnp.concatenate([right, spare], axis=0)
        pair = jnp.concatenate([tail[:first], right], axis=1)
        out[full * width : end, :] = pair.astype(BF16)


def unpack_slots(ref, width, ff):
    full, rest = ff // 128, ff % 128
    blocks = [ref[c * width : (c + 1) * width, :].astype(F32) for c in range(full)]
    if rest:
        end, first = packed_rows(width, ff)
        pair = ref[full * width : end, :].astype(F32)
        blocks.append(
            jnp.concatenate([pair[:, :rest], pair[: width - first, rest:]], axis=0)
        )
    return jnp.concatenate(blocks, axis=1)


def picks_of(meta, me, dims):
    experts, local, cap, width = dims
    top = meta.shape[0] // 2
    slots = token_slots(meta[:top], me, experts, local, cap, width)
    rows = iota((experts // local * width, meta.shape[1]), 0)
    picks = jnp.concatenate([ones_where(rows == slot) for slot in slots], axis=1)
    return picks, meta[top:].astype(F32) * (1.0 / 65536.0)


def dispatch_kernel(dims, place, meta_ref, hid_ref, *outs):
    width = dims[3]
    picks, gate = picks_of(meta_ref[...], place[0], dims)
    scaled = [
        (hid_ref[k].astype(F32) * gate[k : k + 1, :]).astype(BF16)
        for k in range(hid_ref.shape[0])
    ]
    sent = dot(picks, jnp.concatenate(scaled, axis=1), NT)
    tokens = hid_ref.shape[2]
    number = jnp.bitwise_and(iota((8, picks.shape[1]), 1), tokens - 1) + 1
    number = number.astype(F32).astype(BF16)
    for s, out in enumerate(outs):
        at = slice(s * width, (s + 1) * width)
        pack_slots(sent[at], out)
        names = dot(number, picks[at], NT)[:1]
        if width % 128:
            spare = jnp.zeros((1, -width % 128), F32)
            names = jnp.concatenate([names, spare], axis=1)
        lines = jnp.zeros((16, 128), F32)
        for i in range(names.shape[1] // 128):
            line = names[:, i * 128 : (i + 1) * 128]
            lines = jnp.where(iota((16, 128), 0) == i, line, lines)
        out[out.shape[0] - 16 :, :] = lines.astype(BF16)


def names_kernel(ids_ref, out):
    top, tokens = ids_ref.shape
    ids = ids_ref[...].astype(F32)
    spare = jnp.zeros((out.shape[0] - top, tokens), F32)
    out[...] = jnp.concatenate([ids, spare], axis=0).astype(BF16)


def pack_kernel(dy_ref, names_ref, out):
    tokens, half = dy_ref.shape
    for c in range(half // 128):
        out[c * tokens : (c + 1) * tokens, :] = dy_ref[:, c * 128 : (c + 1) * 128]
    out[half // 128 * tokens :, :] = names_ref[...]


def by_expert(rows, local, cap):
    return [
        jnp.concatenate([r[l * cap : (l + 1) * cap] for r in rows], axis=0)
        for l in range(local)
    ]


def by_source(rows, count, cap):
    return [
        jnp.concatenate([r[s * cap : (s + 1) * cap] for r in rows], axis=0)
        for s in range(count)
    ]


def routes(dims, top, me, packed, tokens):
    experts, local, cap, width = dims
    ids = packed[tokens:, :tokens].astype(F32).astype(jnp.int32)[:top]
    return jnp.concatenate(slots_by_lane(ids, me, local, cap, width), axis=0)


def gather_rows(dims, held, halves, x_ref):
    experts, local, cap, width = dims
    tokens, half = held[0].shape[1], halves[0].shape[1]
    chunk = min(half, 512)
    for c in range(0, half, chunk):
        rows = [dot(h, ref[:tokens, c : c + chunk], NN) for h, ref in zip(held, halves)]
        for l, x in enumerate(by_expert(rows, local, cap)):
            x_ref[l, :, c : c + chunk] = x.astype(BF16)


def gather_kernel(dims, top, tokens, place, *refs):
    experts, local, cap, width = dims
    n = experts // local
    own, other, x_ref = refs[:n], refs[n:-1], refs[-1]
    half = x_ref.shape[2] // 2
    chunk = min(half, 512)
    held = []
    for ref in own:
        ids = ref[half // 128 * tokens :, :].astype(F32).astype(jnp.int32)[:top]
        held.append(
            jnp.concatenate(slots_by_lane(ids, place[0], local, cap, width), axis=0)
        )

    def features(ref, start):
        blocks = range(start // 128, (start + chunk) // 128)
        return jnp.concatenate([ref[c * tokens : (c + 1) * tokens, :] for c in blocks], axis=1)

    for side, halves in ((place[1], own), (1 - place[1], other)):
        for c in range(0, half, chunk):
            rows = [dot(h, features(ref, c), NN) for h, ref in zip(held, halves)]
            at = pl.ds(pl.multiple_of(side * half + c, chunk), chunk)
            for l, x in enumerate(by_expert(rows, local, cap)):
                x_ref[l, :, at] = x.astype(BF16)


def grad_kernel(dims, x_ref, w_ref, *outs):
    experts, local, cap, width = dims
    grads = [dot(x_ref[l], w_ref[l], NT) for l in range(local)]
    for s, rows in enumerate(by_source(grads, len(outs), cap)):
        pack_slots(rows, outs[s])


def mix_rows(dims, side, hid, w_ref, tokens, half, store):
    experts, local, cap, width = dims
    n = len(hid)
    ff = w_ref.shape[1]
    chunk = min(half, 256)
    held, rows = [], []
    for h in hid:
        lines = h[h.shape[0] - 16 :, :].astype(F32)
        names = jnp.concatenate(
            [lines[i // 128 : i // 128 + 1, : min(128, width - i)] for i in range(0, width, 128)],
            axis=1,
        )
        held.append(ones_where(iota((tokens, width), 0) == names.astype(jnp.int32) - 1))
        rows.append(unpack_slots(h, width, ff))
    x = [r.astype(BF16) for r in by_expert(rows, local, cap)]
    for c in range(0, half, chunk):
        at = pl.ds(pl.multiple_of(side * half + c, chunk), chunk)
        out = [dot(x[l], w_ref[l, :, at], NN) for l in range(local)]
        for s, rows in enumerate(by_source(out, n, cap)):
            store(s, slice(c, c + chunk), dot(held[s], rows.astype(BF16), NN))


def mix_kernel(dims, sibling, place, *refs):
    hid, (w_ref, out) = refs[:-2], refs[-2:]
    tokens = out.shape[0] // len(hid)

    def store(s, columns, part):
        out[pl.ds(s * tokens, tokens), columns] = part.astype(out.dtype)

    side = 1 - place[1] if sibling else place[1]
    mix_rows(dims, side, hid, w_ref, tokens, out.shape[1], store)


def mix_add_kernel(dims, place, *refs):
    n = (len(refs) - 2) // 2
    hid, (w_ref, arrived), outs = refs[:n], refs[n : n + 2], refs[n + 2 :]
    tokens, half = outs[0].shape

    def store(s, columns, part):
        theirs = arrived[pl.ds(s * tokens, tokens), columns].astype(F32)
        outs[s][:, columns] = (part + theirs).astype(BF16)

    mix_rows(dims, place[1], hid, w_ref, tokens, half, store)


def add_split_kernel(own, arrived, mine, one_low, one_high, two_low, two_high, low, high):
    tokens, half = mine.shape
    cut = half // 2
    parts = []
    for s in range(4):
        at = pl.ds(s * tokens, tokens)
        parts.append(own[at, :] + arrived[at, :].astype(F32))
    mine[...] = parts[0]
    one_low[...] = parts[1][:, :cut].astype(BF16)
    one_high[...] = parts[1][:, cut:]
    two_low[...] = parts[2][:, :cut]
    two_high[...] = parts[2][:, cut:].astype(BF16)
    low[...] = parts[3][:, :cut].astype(BF16)
    high[...] = parts[3][:, cut:].astype(BF16)


def join_kernel(one_high, two_low, low, high, to_one, to_two):
    to_one[...] = (one_high[...] + high[...].astype(F32)).astype(BF16)
    to_two[...] = (two_low[...] + low[...].astype(F32)).astype(BF16)


def finish_kernel(mine, one_low, one_high, two_low, two_high, out):
    cut = one_low.shape[1]
    for at, one, two in ((0, one_low, two_low), (cut, one_high, two_high)):
        total = mine[:, at : at + cut] + one[...].astype(F32) + two[...].astype(F32)
        out[:, at : at + cut] = total.astype(BF16)


def restore_kernel(dims, place, meta_ref, *refs):
    back_refs, out = refs[:-1], refs[-1]
    top, _, tokens = out.shape
    picks, gate = picks_of(meta_ref[...], place[0], dims)
    ff = out.shape[1]
    back = [unpack_slots(ref, dims[3], ff).astype(BF16) for ref in back_refs]
    back = jnp.concatenate(back, axis=0)
    grads = dot(back, picks, TN)
    for k in range(top):
        out[k] = (grads[:, k * tokens : (k + 1) * tokens] * gate[k : k + 1, :]).astype(BF16)


def shaped(shape, dtype=BF16):
    return jax.ShapeDtypeStruct(shape, dtype)


def call(kernel, outs, args, where=(), scratch=(), grant=24, weight=1, name=None):
    where = dict(where)
    return pl.pallas_call(
        kernel,
        out_shape=outs,
        in_specs=[
            pl.BlockSpec(memory_space=where.get(i, pltpu.VMEM)) for i in range(len(args))
        ],
        out_specs=[pl.BlockSpec(memory_space=pltpu.VMEM)] * len(outs),
        scratch_shapes=scratch,
        compiler_params=pltpu.CompilerParams(vmem_limit_bytes=grant * 1024 * 1024),
        cost_estimate=pl.CostEstimate(
            flops=weight, bytes_accessed=1, transcendentals=0
        ),
        name=name,
    )(*args)


def body(hidden, expert_ids, gate_fix, grad_out, w_down):
    tokens, top, ff = hidden.shape
    half = grad_out.shape[1]
    local, _, full = w_down.shape
    n = lax.axis_size("ctx")
    experts = n * local
    assigned = tokens * top
    cap = min(tokens, assigned // experts + max(1, assigned // (8 * experts)))
    unit = 8 if local % 2 == 0 else 16
    cap = -(-cap // unit) * unit
    width = local * cap
    dims = (experts, local, cap, width)
    run = functools.partial(call, grant=24 if n <= 4 else 56)
    place = jnp.stack([lax.axis_index("ctx"), lax.axis_index("tp")]).astype(jnp.int32)
    placed = {0: pltpu.SMEM}

    def send(x, s):
        return lax.ppermute(x, "ctx", [(i, i ^ s) for i in range(n)]) if s else x

    def swap(x):
        return lax.ppermute(x, "tp", [(0, 1), (1, 0)])

    meta = jnp.concatenate([expert_ids.T, gate_fix.T], axis=0)
    hid_t = hidden.transpose(1, 2, 0)
    (names,) = run(
        names_kernel, [shaped((8, tokens))], [expert_ids.T], name="names", weight=10**9
    )
    (packed,) = run(
        pack_kernel, [shaped((half // 128 * tokens + 8, 128))], [grad_out, names], name="pack"
    )
    forward = n == 4
    own = [send(packed, s) for s in range(n)]
    hid_sent = run(
        functools.partial(dispatch_kernel, dims), [shaped((packed_rows(width, ff)[0] + 16, 128))] * n,
        [place, meta, hid_t], where=placed, name="dispatch",
    )
    hid = [send(hid_sent[s], s) for s in range(n)]
    slot = shaped((packed_rows(width, ff)[0], 128))

    def swaps(xs):
        return [swap(x) for x in xs]

    def swaps_by_two(xs):
        first = swaps(xs[:2])
        *rest, first[0], first[1] = lax.optimization_barrier((*xs[2:], *first))
        return first + swaps(rest)

    if forward:
        always = place[0] < 1000
        one, two, mine = lax.cond(always, swaps_by_two, list, [own[1], own[2], own[0]])
        own[3], mine = lax.optimization_barrier((own[3], mine))
        other = [mine, one, two] + lax.cond(always, swaps, list, own[3:])
    else:
        other = swaps(own)
    (x,) = run(
        functools.partial(gather_kernel, dims, top, tokens), [shaped((local, n * cap, full))],
        [place, *own, *other], where=placed, name="gather", weight=20 * 10**8,
    )
    grad_sent = run(
        functools.partial(grad_kernel, dims), [slot] * n, [x, w_down], name="grad"
    )
    hid[0], grad_own = lax.optimization_barrier((hid[0], grad_sent[0]))
    grad_back = [grad_own] + [send(grad_sent[s], s) for s in range(1, n)]

    mixing = dict(where=placed)
    (theirs,) = run(
        functools.partial(mix_kernel, dims, True), [shaped((n * tokens, half))],
        [place, *hid, w_down], name="mix_sibling", **mixing,
    )
    arrived = swap(theirs)
    if forward:
        (mine,) = run(
            functools.partial(mix_kernel, dims, False), [shaped((n * tokens, half), F32)],
            [place, *hid, w_down], name="mix_own", weight=BIG, **mixing,
        )
        cut = half // 2
        kept, wide = shaped((tokens, half), F32), shaped((tokens, cut), F32)
        piece = shaped((tokens, cut))
        kept, one_low, one_high, two_low, two_high, low, high = run(
            add_split_kernel, [kept, piece, wide, wide, piece, piece, piece],
            [mine, arrived], name="add",
        )
        low, high = send(low, 1), send(high, 2)
        one_low, two_high, *grad_back[1:3] = lax.optimization_barrier(
            (one_low, two_high, *grad_back[1:3])
        )
        one_low, two_high = send(one_low, 1), send(two_high, 2)
        to_one, to_two = run(
            join_kernel, [piece] * 2, [one_high, two_low, low, high], name="join"
        )
        (mixed,) = run(
            finish_kernel, [shaped((tokens, half))],
            [kept, one_low, send(to_one, 1), send(to_two, 2), two_high], name="finish",
        )
    else:
        sums = run(
            functools.partial(mix_add_kernel, dims), [shaped((tokens, half))] * n,
            [place, *hid, w_down, arrived], name="mix_own", **mixing,
        )
        mixed = sum(send(sums[s], s).astype(F32) for s in range(n)).astype(BF16)

    (grad_t,) = run(
        functools.partial(restore_kernel, dims), [shaped((top, ff, tokens))],
        [place, meta, *grad_back], where=placed, name="restore", weight=BIG,
    )
    return mixed, grad_t.transpose(2, 0, 1)


def solution(mesh):
    placed = (
        P(("ctx", "exp"), None, "tp"),
        P(("ctx", "exp"), None),
        P(("ctx", "exp"), None),
        P(("ctx", "exp"), "tp"),
        P("ctx", "tp", None),
    )
    return jax.shard_map(
        body,
        mesh=mesh,
        in_specs=placed,
        out_specs=(P(("ctx", "exp"), "tp"), P(("ctx", "exp"), None, "tp")),
        check_vma=False,
    )
```

```python
import functools

import jax
import jax.numpy as jnp
from jax import lax
from jax.experimental import pallas as pl
from jax.experimental.pallas import tpu as pltpu
from jax.sharding import PartitionSpec as P

BF16 = jnp.bfloat16
F32 = jnp.float32
NN = (((1,), (0,)), ((), ()))
NT = (((1,), (1,)), ((), ()))
TN = (((0,), (0,)), ((), ()))
BIG = 10**11


def dot(a, b, dims):
    return lax.dot_general(a, b, dims, preferred_element_type=F32)


def iota(shape, axis):
    return lax.broadcasted_iota(jnp.int32, shape, axis)


def ones_where(mask):
    return mask.astype(F32).astype(BF16)


def earlier(tokens):
    return ones_where(iota((tokens, tokens), 0) < iota((tokens, tokens), 1))


def token_slots(ids, me, experts, local, cap, width):
    top, tokens = ids.shape
    row = iota((experts, tokens), 0)
    hits = [ids[k : k + 1, :] == row for k in range(top)]
    named = functools.reduce(jnp.logical_or, hits)
    before = dot(ones_where(named), earlier(tokens), NN)
    base = jnp.bitwise_xor(row // local, me) * width + lax.rem(row, local) * cap
    slot = before + base.astype(F32)
    return [
        jnp.sum(jnp.where(hit, slot, 0.0), axis=0, keepdims=True).astype(jnp.int32)
        for hit in hits
    ]


def named_here(ids, me, local):
    top, tokens = ids.shape
    row = iota((8, tokens), 0) + me * local
    return functools.reduce(
        jnp.logical_or, [ids[k : k + 1, :] == row for k in range(top)]
    )


def slots_by_lane(ids, me, local, cap, width):
    tokens = ids.shape[1]
    named = named_here(ids, me, local)
    before = dot(ones_where(named), earlier(tokens), NN)
    slot = before.astype(jnp.int32) + iota((8, tokens), 0) * cap
    slot = jnp.where(named, slot, -1)
    rows = iota((cap, tokens), 0)
    return [ones_where(rows + l * cap == slot[l : l + 1, :]) for l in range(local)]


def packed_rows(width, ff):
    first = -(-(width // 2) // 16) * 16
    return ff // 128 * width + (first if ff % 128 else 0), first


def pack_slots(rows, out):
    width, ff = rows.shape
    full, rest = ff // 128, ff % 128
    for c in range(full):
        out[c * width : (c + 1) * width, :] = rows[:, c * 128 : (c + 1) * 128].astype(BF16)
    if rest:
        end, first = packed_rows(width, ff)
        tail = rows[:, full * 128 :]
        right = tail[first:]
        if right.shape[0] < first:
            spare = jnp.zeros((first - right.shape[0], rest), F32)
            right = jnp.concatenate([right, spare], axis=0)
        pair = jnp.concatenate([tail[:first], right], axis=1)
        out[full * width : end, :] = pair.astype(BF16)


def unpack_slots(ref, width, ff):
    full, rest = ff // 128, ff % 128
    blocks = [ref[c * width : (c + 1) * width, :].astype(F32) for c in range(full)]
    if rest:
        end, first = packed_rows(width, ff)
        pair = ref[full * width : end, :].astype(F32)
        blocks.append(
            jnp.concatenate([pair[:, :rest], pair[: width - first, rest:]], axis=0)
        )
    return jnp.concatenate(blocks, axis=1)


def picks_of(meta, me, dims):
    experts, local, cap, width = dims
    top = meta.shape[0] // 2
    slots = token_slots(meta[:top], me, experts, local, cap, width)
    rows = iota((experts // local * width, meta.shape[1]), 0)
    picks = jnp.concatenate([ones_where(rows == slot) for slot in slots], axis=1)
    return picks, meta[top:].astype(F32) * (1.0 / 65536.0)


def dispatch_kernel(dims, place, meta_ref, hid_ref, *outs):
    width = dims[3]
    picks, gate = picks_of(meta_ref[...], place[0], dims)
    scaled = [
        (hid_ref[k].astype(F32) * gate[k : k + 1, :]).astype(BF16)
        for k in range(hid_ref.shape[0])
    ]
    sent = dot(picks, jnp.concatenate(scaled, axis=1), NT)
    tokens = hid_ref.shape[2]
    number = lax.rem(iota((8, picks.shape[1]), 1), tokens) + 1
    number = number.astype(F32).astype(BF16)
    for s, out in enumerate(outs):
        at = slice(s * width, (s + 1) * width)
        pack_slots(sent[at], out)
        names = dot(number, picks[at], NT)[:1]
        if width % 128:
            spare = jnp.zeros((1, -width % 128), F32)
            names = jnp.concatenate([names, spare], axis=1)
        lines = jnp.zeros((16, 128), F32)
        for i in range(names.shape[1] // 128):
            line = names[:, i * 128 : (i + 1) * 128]
            lines = jnp.where(iota((16, 128), 0) == i, line, lines)
        out[out.shape[0] - 16 :, :] = lines.astype(BF16)


def names_kernel(ids_ref, out):
    top, tokens = ids_ref.shape
    ids = ids_ref[...].astype(F32)
    spare = jnp.zeros((out.shape[0] - top, tokens), F32)
    out[...] = jnp.concatenate([ids, spare], axis=0).astype(BF16)


def pack_kernel(dy_ref, names_ref, out):
    tokens, half = dy_ref.shape
    for c in range(half // 128):
        out[c * tokens : (c + 1) * tokens, :] = dy_ref[:, c * 128 : (c + 1) * 128]
    out[half // 128 * tokens :, :] = names_ref[...]


def by_expert(rows, local, cap):
    return [
        jnp.concatenate([r[l * cap : (l + 1) * cap] for r in rows], axis=0)
        for l in range(local)
    ]


def by_source(rows, count, cap):
    return [
        jnp.concatenate([r[s * cap : (s + 1) * cap] for r in rows], axis=0)
        for s in range(count)
    ]


def gather_kernel(dims, top, tokens, place, *refs):
    experts, local, cap, width = dims
    n = experts // local
    own, other, x_ref = refs[:n], refs[n:-1], refs[-1]
    half = x_ref.shape[2] // 2
    chunk = min(half, 512)
    held = []
    for ref in own:
        ids = ref[half // 128 * tokens :, :].astype(F32).astype(jnp.int32)[:top]
        held.append(
            jnp.concatenate(slots_by_lane(ids, place[0], local, cap, width), axis=0)
        )

    def features(ref, start):
        blocks = range(start // 128, (start + chunk) // 128)
        return jnp.concatenate([ref[c * tokens : (c + 1) * tokens, :] for c in blocks], axis=1)

    for side, halves in ((place[1], own), (1 - place[1], other)):
        for c in range(0, half, chunk):
            rows = [dot(h, features(ref, c), NN) for h, ref in zip(held, halves)]
            at = pl.ds(pl.multiple_of(side * half + c, chunk), chunk)
            for l, x in enumerate(by_expert(rows, local, cap)):
                x_ref[l, :, at] = x.astype(BF16)


def grad_kernel(dims, x_ref, w_ref, *outs):
    experts, local, cap, width = dims
    grads = [dot(x_ref[l], w_ref[l], NT) for l in range(local)]
    for s, rows in enumerate(by_source(grads, len(outs), cap)):
        pack_slots(rows, outs[s])


def mix_rows(dims, side, hid, w_ref, tokens, half, store):
    experts, local, cap, width = dims
    n = len(hid)
    ff = w_ref.shape[1]
    chunk = min(half, 256)
    held, rows = [], []
    for h in hid:
        lines = h[h.shape[0] - 16 :, :].astype(F32)
        names = jnp.concatenate(
            [lines[i // 128 : i // 128 + 1, : min(128, width - i)] for i in range(0, width, 128)],
            axis=1,
        )
        held.append(ones_where(iota((tokens, width), 0) == names.astype(jnp.int32) - 1))
        rows.append(unpack_slots(h, width, ff))
    x = [r.astype(BF16) for r in by_expert(rows, local, cap)]
    for c in range(0, half, chunk):
        at = pl.ds(pl.multiple_of(side * half + c, chunk), chunk)
        out = [dot(x[l], w_ref[l, :, at], NN) for l in range(local)]
        for s, rows in enumerate(by_source(out, n, cap)):
            store(s, slice(c, c + chunk), dot(held[s], rows.astype(BF16), NN))


def mix_kernel(dims, sibling, place, *refs):
    hid, (w_ref, out) = refs[:-2], refs[-2:]
    tokens = out.shape[0] // len(hid)

    def store(s, columns, part):
        out[pl.ds(s * tokens, tokens), columns] = part.astype(out.dtype)

    side = 1 - place[1] if sibling else place[1]
    mix_rows(dims, side, hid, w_ref, tokens, out.shape[1], store)


def mix_add_kernel(dims, place, *refs):
    n = (len(refs) - 2) // 2
    hid, (w_ref, arrived), outs = refs[:n], refs[n : n + 2], refs[n + 2 :]
    tokens, half = outs[0].shape

    def store(s, columns, part):
        theirs = arrived[pl.ds(s * tokens, tokens), columns].astype(F32)
        outs[s][:, columns] = (part + theirs).astype(BF16)

    mix_rows(dims, place[1], hid, w_ref, tokens, half, store)


def add_split_kernel(own, arrived, mine, one_low, one_high, two_low, two_high, low, high):
    tokens, half = mine.shape
    cut = half // 2
    parts = []
    for s in range(4):
        at = pl.ds(s * tokens, tokens)
        parts.append(own[at, :] + arrived[at, :].astype(F32))
    mine[...] = parts[0]
    one_low[...] = parts[1][:, :cut].astype(BF16)
    one_high[...] = parts[1][:, cut:]
    two_low[...] = parts[2][:, :cut]
    two_high[...] = parts[2][:, cut:].astype(BF16)
    low[...] = parts[3][:, :cut].astype(BF16)
    high[...] = parts[3][:, cut:].astype(BF16)


def join_kernel(one_high, two_low, low, high, to_one, to_two):
    to_one[...] = (one_high[...] + high[...].astype(F32)).astype(BF16)
    to_two[...] = (two_low[...] + low[...].astype(F32)).astype(BF16)


def finish_kernel(mine, one_low, one_high, two_low, two_high, out):
    cut = one_low.shape[1]
    for at, one, two in ((0, one_low, two_low), (cut, one_high, two_high)):
        total = mine[:, at : at + cut] + one[...].astype(F32) + two[...].astype(F32)
        out[:, at : at + cut] = total.astype(BF16)


def restore_kernel(dims, place, meta_ref, *refs):
    back_refs, out = refs[:-1], refs[-1]
    top, _, tokens = out.shape
    picks, gate = picks_of(meta_ref[...], place[0], dims)
    ff = out.shape[1]
    back = [unpack_slots(ref, dims[3], ff).astype(BF16) for ref in back_refs]
    back = jnp.concatenate(back, axis=0)
    grads = dot(back, picks, TN)
    for k in range(top):
        out[k] = (grads[:, k * tokens : (k + 1) * tokens] * gate[k : k + 1, :]).astype(BF16)


def shaped(shape, dtype=BF16):
    return jax.ShapeDtypeStruct(shape, dtype)


def call(kernel, outs, args, where=(), scratch=(), grant=24, weight=1, name=None):
    where = dict(where)
    return pl.pallas_call(
        kernel,
        out_shape=outs,
        in_specs=[
            pl.BlockSpec(memory_space=where.get(i, pltpu.VMEM)) for i in range(len(args))
        ],
        out_specs=[pl.BlockSpec(memory_space=pltpu.VMEM)] * len(outs),
        scratch_shapes=scratch,
        compiler_params=pltpu.CompilerParams(vmem_limit_bytes=grant * 1024 * 1024),
        cost_estimate=pl.CostEstimate(
            flops=weight, bytes_accessed=1, transcendentals=0
        ),
        name=name,
    )(*args)


def body(hidden, expert_ids, gate_fix, grad_out, w_down):
    tokens, top, ff = hidden.shape
    half = grad_out.shape[1]
    local, _, full = w_down.shape
    n = lax.axis_size("ctx")
    experts = n * local
    assigned = tokens * top
    cap = min(tokens, assigned // experts + max(1, assigned // (8 * experts)))
    unit = 8 if local % 2 == 0 else 16
    cap = -(-cap // unit) * unit
    width = local * cap
    dims = (experts, local, cap, width)
    run = functools.partial(call, grant=24 if n <= 4 else 56)
    place = jnp.stack([lax.axis_index("ctx"), lax.axis_index("tp")]).astype(jnp.int32)
    placed = {0: pltpu.SMEM}

    def send(x, s):
        return lax.ppermute(x, "ctx", [(i, i ^ s) for i in range(n)]) if s else x

    def swap(x):
        return lax.ppermute(x, "tp", [(0, 1), (1, 0)])

    meta = jnp.concatenate([expert_ids.T, gate_fix.T], axis=0)
    hid_t = hidden.transpose(1, 2, 0)
    (names,) = run(
        names_kernel, [shaped((16, tokens))], [expert_ids.T], name="names", weight=10**9
    )
    (packed,) = run(
        pack_kernel, [shaped((half // 128 * tokens + 16, 128))], [grad_out, names], name="pack"
    )
    forward = n == 4
    own = [send(packed, s) for s in range(n)]
    hid_sent = run(
        functools.partial(dispatch_kernel, dims), [shaped((packed_rows(width, ff)[0] + 16, 128))] * n,
        [place, meta, hid_t], where=placed, name="dispatch",
    )
    hid = [send(hid_sent[s], s) for s in range(n)]
    slot = shaped((packed_rows(width, ff)[0], 128))

    def swaps(xs):
        return [swap(x) for x in xs]

    def swaps_in_turn(xs):
        first = swap(xs[0])
        second, first = lax.optimization_barrier((xs[1], first))
        return [first, swap(second)]

    if forward:
        always = place[0] < 1000
        last, mine = lax.cond(always, swaps_in_turn, list, [own[3], own[0]])
        *own[1:3], last = lax.optimization_barrier((*own[1:3], last))
        other = [mine] + lax.cond(always, swaps, list, own[1:3]) + [last]
    else:
        other = swaps(own)
    (x,) = run(
        functools.partial(gather_kernel, dims, top, tokens), [shaped((local, n * cap, full))],
        [place, *own, *other], where=placed, name="gather", weight=20 * 10**8,
    )
    grad_sent = run(
        functools.partial(grad_kernel, dims), [slot] * n, [x, w_down], name="grad"
    )
    hid[0], grad_own = lax.optimization_barrier((hid[0], grad_sent[0]))
    grad_back = [grad_own] + [send(grad_sent[s], s) for s in range(1, n)]

    mixing = dict(where=placed)
    (theirs,) = run(
        functools.partial(mix_kernel, dims, True), [shaped((n * tokens, half))],
        [place, *hid, w_down], name="mix_sibling", **mixing,
    )
    arrived = swap(theirs)
    if forward:
        (mine,) = run(
            functools.partial(mix_kernel, dims, False), [shaped((n * tokens, half), F32)],
            [place, *hid, w_down], name="mix_own", weight=BIG, **mixing,
        )
        cut = half // 2
        kept, wide = shaped((tokens, half), F32), shaped((tokens, cut), F32)
        piece = shaped((tokens, cut))
        kept, one_low, one_high, two_low, two_high, low, high = run(
            add_split_kernel, [kept, piece, wide, wide, piece, piece, piece],
            [mine, arrived], name="add",
        )
        low, high = send(low, 1), send(high, 2)
        one_low, two_high, *grad_back[1:3] = lax.optimization_barrier(
            (one_low, two_high, *grad_back[1:3])
        )
        one_low, two_high = send(one_low, 1), send(two_high, 2)
        to_one, to_two = run(
            join_kernel, [piece] * 2, [one_high, two_low, low, high], name="join"
        )
        (mixed,) = run(
            finish_kernel, [shaped((tokens, half))],
            [kept, one_low, send(to_one, 1), send(to_two, 2), two_high], name="finish",
        )
    else:
        sums = run(
            functools.partial(mix_add_kernel, dims), [shaped((tokens, half))] * n,
            [place, *hid, w_down, arrived], name="mix_own", **mixing,
        )
        mixed = sum(send(sums[s], s).astype(F32) for s in range(n)).astype(BF16)

    (grad_t,) = run(
        functools.partial(restore_kernel, dims), [shaped((top, ff, tokens))],
        [place, meta, *grad_back], where=placed, name="restore", weight=BIG,
    )
    return mixed, grad_t.transpose(2, 0, 1)


def solution(mesh):
    placed = (
        P(("ctx", "exp"), None, "tp"),
        P(("ctx", "exp"), None),
        P(("ctx", "exp"), None),
        P(("ctx", "exp"), "tp"),
        P("ctx", "tp", None),
    )
    return jax.shard_map(
        body,
        mesh=mesh,
        in_specs=placed,
        out_specs=(P(("ctx", "exp"), "tp"), P(("ctx", "exp"), None, "tp")),
        check_vma=False,
    )
```

```python
import functools

import jax
import jax.numpy as jnp
from jax import lax
from jax.experimental import pallas as pl
from jax.experimental.pallas import tpu as pltpu
from jax.sharding import PartitionSpec as P

BF16 = jnp.bfloat16
F32 = jnp.float32
NN = (((1,), (0,)), ((), ()))
NT = (((1,), (1,)), ((), ()))
TN = (((0,), (0,)), ((), ()))
BIG = 10**11


def dot(a, b, dims):
    return lax.dot_general(a, b, dims, preferred_element_type=F32)


def iota(shape, axis):
    return lax.broadcasted_iota(jnp.int32, shape, axis)


def ones_where(mask):
    return mask.astype(F32).astype(BF16)


def earlier(tokens):
    return ones_where(iota((tokens, tokens), 0) < iota((tokens, tokens), 1))


def token_slots(ids, me, experts, local, cap, width):
    top, tokens = ids.shape
    row = iota((experts, tokens), 0)
    hits = [ids[k : k + 1, :] == row for k in range(top)]
    named = functools.reduce(jnp.logical_or, hits)
    before = dot(ones_where(named), earlier(tokens), NN)
    base = jnp.bitwise_xor(row // local, me) * width + lax.rem(row, local) * cap
    slot = before + base.astype(F32)
    return [
        jnp.sum(jnp.where(hit, slot, 0.0), axis=0, keepdims=True).astype(jnp.int32)
        for hit in hits
    ]


def named_here(ids, me, local):
    top, tokens = ids.shape
    row = iota((8, tokens), 0) + me * local
    return functools.reduce(
        jnp.logical_or, [ids[k : k + 1, :] == row for k in range(top)]
    )


def slots_by_lane(ids, me, local, cap, width):
    tokens = ids.shape[1]
    named = named_here(ids, me, local)
    before = dot(ones_where(named), earlier(tokens), NN)
    slot = before.astype(jnp.int32) + iota((8, tokens), 0) * cap
    slot = jnp.where(named, slot, -1)
    rows = iota((cap, tokens), 0)
    return [ones_where(rows + l * cap == slot[l : l + 1, :]) for l in range(local)]


def packed_rows(width, ff):
    first = -(-(width // 2) // 16) * 16
    return ff // 128 * width + (first if ff % 128 else 0), first


def pack_slots(rows, out):
    width, ff = rows.shape
    full, rest = ff // 128, ff % 128
    for c in range(full):
        out[c * width : (c + 1) * width, :] = rows[:, c * 128 : (c + 1) * 128].astype(BF16)
    if rest:
        end, first = packed_rows(width, ff)
        tail = rows[:, full * 128 :]
        right = tail[first:]
        if right.shape[0] < first:
            spare = jnp.zeros((first - right.shape[0], rest), F32)
            right = jnp.concatenate([right, spare], axis=0)
        pair = jnp.concatenate([tail[:first], right], axis=1)
        out[full * width : end, :] = pair.astype(BF16)


def unpack_slots(ref, width, ff):
    full, rest = ff // 128, ff % 128
    blocks = [ref[c * width : (c + 1) * width, :].astype(F32) for c in range(full)]
    if rest:
        end, first = packed_rows(width, ff)
        pair = ref[full * width : end, :].astype(F32)
        blocks.append(
            jnp.concatenate([pair[:, :rest], pair[: width - first, rest:]], axis=0)
        )
    return jnp.concatenate(blocks, axis=1)


def picks_of(meta, me, dims):
    experts, local, cap, width = dims
    top = meta.shape[0] // 2
    slots = token_slots(meta[:top], me, experts, local, cap, width)
    rows = iota((experts // local * width, meta.shape[1]), 0)
    picks = jnp.concatenate([ones_where(rows == slot) for slot in slots], axis=1)
    return picks, meta[top:].astype(F32) * (1.0 / 65536.0)


def dispatch_kernel(dims, place, meta_ref, hid_ref, *outs):
    width = dims[3]
    picks, gate = picks_of(meta_ref[...], place[0], dims)
    scaled = [
        (hid_ref[k].astype(F32) * gate[k : k + 1, :]).astype(BF16)
        for k in range(hid_ref.shape[0])
    ]
    sent = dot(picks, jnp.concatenate(scaled, axis=1), NT)
    tokens = hid_ref.shape[2]
    number = lax.rem(iota((8, picks.shape[1]), 1), tokens) + 1
    number = number.astype(F32).astype(BF16)
    for s, out in enumerate(outs):
        at = slice(s * width, (s + 1) * width)
        pack_slots(sent[at], out)
        names = dot(number, picks[at], NT)[:1]
        if width % 128:
            spare = jnp.zeros((1, -width % 128), F32)
            names = jnp.concatenate([names, spare], axis=1)
        lines = jnp.zeros((16, 128), F32)
        for i in range(names.shape[1] // 128):
            line = names[:, i * 128 : (i + 1) * 128]
            lines = jnp.where(iota((16, 128), 0) == i, line, lines)
        out[out.shape[0] - 16 :, :] = lines.astype(BF16)


def names_kernel(ids_ref, out):
    top, tokens = ids_ref.shape
    ids = ids_ref[...].astype(F32)
    spare = jnp.zeros((out.shape[0] - top, tokens), F32)
    out[...] = jnp.concatenate([ids, spare], axis=0).astype(BF16)


def pack_kernel(dy_ref, names_ref, out):
    tokens, half = dy_ref.shape
    for c in range(half // 128):
        out[c * tokens : (c + 1) * tokens, :] = dy_ref[:, c * 128 : (c + 1) * 128]
    out[half // 128 * tokens :, :] = names_ref[...]


def by_expert(rows, local, cap):
    return [
        jnp.concatenate([r[l * cap : (l + 1) * cap] for r in rows], axis=0)
        for l in range(local)
    ]


def by_source(rows, count, cap):
    return [
        jnp.concatenate([r[s * cap : (s + 1) * cap] for r in rows], axis=0)
        for s in range(count)
    ]


def gather_kernel(dims, top, tokens, place, *refs):
    experts, local, cap, width = dims
    n = experts // local
    own, other, x_ref = refs[:n], refs[n:-1], refs[-1]
    half = x_ref.shape[2] // 2
    chunk = min(half, 512)
    held = []
    for ref in own:
        ids = ref[half // 128 * tokens :, :].astype(F32).astype(jnp.int32)[:top]
        held.append(
            jnp.concatenate(slots_by_lane(ids, place[0], local, cap, width), axis=0)
        )

    def features(ref, start):
        blocks = range(start // 128, (start + chunk) // 128)
        return jnp.concatenate([ref[c * tokens : (c + 1) * tokens, :] for c in blocks], axis=1)

    for side, halves in ((place[1], own), (1 - place[1], other)):
        for c in range(0, half, chunk):
            rows = [dot(h, features(ref, c), NN) for h, ref in zip(held, halves)]
            at = pl.ds(pl.multiple_of(side * half + c, chunk), chunk)
            for l, x in enumerate(by_expert(rows, local, cap)):
                x_ref[l, :, at] = x.astype(BF16)


def grad_kernel(dims, x_ref, w_ref, *outs):
    experts, local, cap, width = dims
    grads = [dot(x_ref[l], w_ref[l], NT) for l in range(local)]
    for s, rows in enumerate(by_source(grads, len(outs), cap)):
        pack_slots(rows, outs[s])


def mix_rows(dims, side, hid, w_ref, tokens, half, store):
    experts, local, cap, width = dims
    n = len(hid)
    ff = w_ref.shape[1]
    chunk = min(half, 256)
    held, rows = [], []
    for h in hid:
        lines = h[h.shape[0] - 16 :, :].astype(F32)
        names = jnp.concatenate(
            [lines[i // 128 : i // 128 + 1, : min(128, width - i)] for i in range(0, width, 128)],
            axis=1,
        )
        held.append(ones_where(iota((tokens, width), 0) == names.astype(jnp.int32) - 1))
        rows.append(unpack_slots(h, width, ff))
    x = [r.astype(BF16) for r in by_expert(rows, local, cap)]
    for c in range(0, half, chunk):
        at = pl.ds(pl.multiple_of(side * half + c, chunk), chunk)
        out = [dot(x[l], w_ref[l, :, at], NN) for l in range(local)]
        for s, rows in enumerate(by_source(out, n, cap)):
            store(s, slice(c, c + chunk), dot(held[s], rows.astype(BF16), NN))


def mix_kernel(dims, sibling, place, *refs):
    hid, (w_ref, out) = refs[:-2], refs[-2:]
    tokens = out.shape[0] // len(hid)

    def store(s, columns, part):
        out[pl.ds(s * tokens, tokens), columns] = part.astype(out.dtype)

    side = 1 - place[1] if sibling else place[1]
    mix_rows(dims, side, hid, w_ref, tokens, out.shape[1], store)


def mix_add_kernel(dims, place, *refs):
    n = (len(refs) - 2) // 2
    hid, (w_ref, arrived), outs = refs[:n], refs[n : n + 2], refs[n + 2 :]
    tokens, half = outs[0].shape

    def store(s, columns, part):
        theirs = arrived[pl.ds(s * tokens, tokens), columns].astype(F32)
        outs[s][:, columns] = (part + theirs).astype(BF16)

    mix_rows(dims, place[1], hid, w_ref, tokens, half, store)


def add_split_kernel(own, arrived, mine, one_low, one_high, two_low, two_high, low, high):
    tokens, half = mine.shape
    cut = half // 2
    parts = []
    for s in range(4):
        at = pl.ds(s * tokens, tokens)
        parts.append(own[at, :] + arrived[at, :].astype(F32))
    mine[...] = parts[0]
    one_low[...] = parts[1][:, :cut].astype(BF16)
    one_high[...] = parts[1][:, cut:]
    two_low[...] = parts[2][:, :cut]
    two_high[...] = parts[2][:, cut:].astype(BF16)
    low[...] = parts[3][:, :cut].astype(BF16)
    high[...] = parts[3][:, cut:].astype(BF16)


def join_kernel(one_high, two_low, low, high, to_one, to_two):
    to_one[...] = (one_high[...] + high[...].astype(F32)).astype(BF16)
    to_two[...] = (two_low[...] + low[...].astype(F32)).astype(BF16)


def finish_kernel(mine, one_low, one_high, two_low, two_high, out):
    cut = one_low.shape[1]
    for at, one, two in ((0, one_low, two_low), (cut, one_high, two_high)):
        total = mine[:, at : at + cut] + one[...].astype(F32) + two[...].astype(F32)
        out[:, at : at + cut] = total.astype(BF16)


def restore_kernel(dims, place, meta_ref, *refs):
    back_refs, out = refs[:-1], refs[-1]
    top, _, tokens = out.shape
    picks, gate = picks_of(meta_ref[...], place[0], dims)
    ff = out.shape[1]
    back = [unpack_slots(ref, dims[3], ff).astype(BF16) for ref in back_refs]
    back = jnp.concatenate(back, axis=0)
    grads = dot(back, picks, TN)
    for k in range(top):
        out[k] = (grads[:, k * tokens : (k + 1) * tokens] * gate[k : k + 1, :]).astype(BF16)


def shaped(shape, dtype=BF16):
    return jax.ShapeDtypeStruct(shape, dtype)


def call(kernel, outs, args, where=(), scratch=(), grant=24, weight=1, name=None):
    where = dict(where)
    return pl.pallas_call(
        kernel,
        out_shape=outs,
        in_specs=[
            pl.BlockSpec(memory_space=where.get(i, pltpu.VMEM)) for i in range(len(args))
        ],
        out_specs=[pl.BlockSpec(memory_space=pltpu.VMEM)] * len(outs),
        scratch_shapes=scratch,
        compiler_params=pltpu.CompilerParams(vmem_limit_bytes=grant * 1024 * 1024),
        cost_estimate=pl.CostEstimate(
            flops=weight, bytes_accessed=1, transcendentals=0
        ),
        name=name,
    )(*args)


def body(hidden, expert_ids, gate_fix, grad_out, w_down):
    tokens, top, ff = hidden.shape
    half = grad_out.shape[1]
    local, _, full = w_down.shape
    n = lax.axis_size("ctx")
    experts = n * local
    assigned = tokens * top
    cap = min(tokens, assigned // experts + max(1, assigned // (8 * experts)))
    unit = 8 if local % 2 == 0 else 16
    cap = -(-cap // unit) * unit
    width = local * cap
    dims = (experts, local, cap, width)
    run = functools.partial(call, grant=24 if n <= 4 else 56)
    place = jnp.stack([lax.axis_index("ctx"), lax.axis_index("tp")]).astype(jnp.int32)
    placed = {0: pltpu.SMEM}

    def send(x, s):
        return lax.ppermute(x, "ctx", [(i, i ^ s) for i in range(n)]) if s else x

    def swap(x):
        return lax.ppermute(x, "tp", [(0, 1), (1, 0)])

    meta = jnp.concatenate([expert_ids.T, gate_fix.T], axis=0)
    hid_t = hidden.transpose(1, 2, 0)
    (names,) = run(
        names_kernel, [shaped((16, tokens))], [expert_ids.T], name="names", weight=10**9
    )
    (packed,) = run(
        pack_kernel, [shaped((half // 128 * tokens + 16, 128))], [grad_out, names], name="pack"
    )
    forward = n == 4
    own = [send(packed, s) for s in range(n)]
    hid_sent = run(
        functools.partial(dispatch_kernel, dims), [shaped((packed_rows(width, ff)[0] + 16, 128))] * n,
        [place, meta, hid_t], where=placed, name="dispatch",
    )
    hid = [send(hid_sent[s], s) for s in range(n)]
    slot = shaped((packed_rows(width, ff)[0], 128))

    def swaps(xs):
        return [swap(x) for x in xs]

    def swaps_in_turn(xs):
        first = swap(xs[0])
        second, first = lax.optimization_barrier((xs[1], first))
        return [first, swap(second)]

    if forward:
        always = place[0] < 1000
        last, mine = lax.cond(always, swaps_in_turn, list, [own[3], own[0]])
        *own[1:3], last = lax.optimization_barrier((*own[1:3], last))
        other = [mine] + lax.cond(always, swaps, list, own[1:3]) + [last]
    else:
        other = swaps(own)
    (x,) = run(
        functools.partial(gather_kernel, dims, top, tokens), [shaped((local, n * cap, full))],
        [place, *own, *other], where=placed, name="gather", weight=20 * 10**8,
    )
    grad_sent = run(
        functools.partial(grad_kernel, dims), [slot] * n, [x, w_down], name="grad"
    )
    hid[0], grad_own = lax.optimization_barrier((hid[0], grad_sent[0]))
    grad_back = [grad_own] + [send(grad_sent[s], s) for s in range(1, n)]

    mixing = dict(where=placed)
    (theirs,) = run(
        functools.partial(mix_kernel, dims, True), [shaped((n * tokens, half))],
        [place, *hid, w_down], name="mix_sibling", **mixing,
    )
    arrived = swap(theirs)
    if forward:
        (mine,) = run(
            functools.partial(mix_kernel, dims, False), [shaped((n * tokens, half), F32)],
            [place, *hid, w_down], name="mix_own", weight=BIG, **mixing,
        )
        cut = half // 2
        kept, wide = shaped((tokens, half), F32), shaped((tokens, cut), F32)
        piece = shaped((tokens, cut))
        kept, one_low, one_high, two_low, two_high, low, high = run(
            add_split_kernel, [kept, piece, wide, wide, piece, piece, piece],
            [mine, arrived], name="add",
        )
        low, high = send(low, 1), send(high, 2)
        one_low, two_high, *grad_back[2:] = lax.optimization_barrier(
            (one_low, two_high, *grad_back[2:])
        )
        one_low, two_high = send(one_low, 1), send(two_high, 2)
        to_one, to_two = run(
            join_kernel, [piece] * 2, [one_high, two_low, low, high], name="join"
        )
        (mixed,) = run(
            finish_kernel, [shaped((tokens, half))],
            [kept, one_low, send(to_one, 1), send(to_two, 2), two_high], name="finish",
        )
    else:
        sums = run(
            functools.partial(mix_add_kernel, dims), [shaped((tokens, half))] * n,
            [place, *hid, w_down, arrived], name="mix_own", **mixing,
        )
        mixed = sum(send(sums[s], s).astype(F32) for s in range(n)).astype(BF16)

    (grad_t,) = run(
        functools.partial(restore_kernel, dims), [shaped((top, ff, tokens))],
        [place, meta, *grad_back], where=placed, name="restore", weight=BIG,
    )
    return mixed, grad_t.transpose(2, 0, 1)


def solution(mesh):
    placed = (
        P(("ctx", "exp"), None, "tp"),
        P(("ctx", "exp"), None),
        P(("ctx", "exp"), None),
        P(("ctx", "exp"), "tp"),
        P("ctx", "tp", None),
    )
    return jax.shard_map(
        body,
        mesh=mesh,
        in_specs=placed,
        out_specs=(P(("ctx", "exp"), "tp"), P(("ctx", "exp"), None, "tp")),
        check_vma=False,
    )
```

```python
import functools

import jax
import jax.numpy as jnp
from jax import lax
from jax.experimental import pallas as pl
from jax.experimental.pallas import tpu as pltpu
from jax.sharding import PartitionSpec as P

BF16 = jnp.bfloat16
F32 = jnp.float32
NN = (((1,), (0,)), ((), ()))
NT = (((1,), (1,)), ((), ()))
TN = (((0,), (0,)), ((), ()))
BIG = 10**11


def dot(a, b, dims):
    return lax.dot_general(a, b, dims, preferred_element_type=F32)


def iota(shape, axis):
    return lax.broadcasted_iota(jnp.int32, shape, axis)


def ones_where(mask):
    return mask.astype(F32).astype(BF16)


def earlier(tokens):
    return ones_where(iota((tokens, tokens), 0) < iota((tokens, tokens), 1))


def token_slots(ids, me, experts, local, cap, width):
    top, tokens = ids.shape
    row = iota((experts, tokens), 0)
    hits = [ids[k : k + 1, :] == row for k in range(top)]
    named = functools.reduce(jnp.logical_or, hits)
    before = dot(ones_where(named), earlier(tokens), NN)
    base = jnp.bitwise_xor(row // local, me) * width + lax.rem(row, local) * cap
    slot = before + base.astype(F32)
    return [
        jnp.sum(jnp.where(hit, slot, 0.0), axis=0, keepdims=True).astype(jnp.int32)
        for hit in hits
    ]


def named_here(ids, me, local):
    top, tokens = ids.shape
    row = iota((8, tokens), 0) + me * local
    return functools.reduce(
        jnp.logical_or, [ids[k : k + 1, :] == row for k in range(top)]
    )


def slots_by_lane(ids, me, local, cap, width):
    tokens = ids.shape[1]
    named = named_here(ids, me, local)
    before = dot(ones_where(named), earlier(tokens), NN)
    slot = before.astype(jnp.int32) + iota((8, tokens), 0) * cap
    slot = jnp.where(named, slot, -1)
    rows = iota((cap, tokens), 0)
    return [ones_where(rows + l * cap == slot[l : l + 1, :]) for l in range(local)]


def packed_rows(width, ff):
    first = -(-(width // 2) // 16) * 16
    return ff // 128 * width + (first if ff % 128 else 0), first


def lines_of(names, lines):
    width, lanes = names.shape[1], lines.shape[1]
    if width % lanes:
        names = jnp.concatenate([names, jnp.zeros((1, -width % lanes), F32)], axis=1)
    for i in range(names.shape[1] // lanes):
        line = names[:, i * lanes : (i + 1) * lanes]
        lines = jnp.where(iota(lines.shape, 0) == i, line, lines)
    return lines


def spare_fits(width, ff):
    rest, first = ff % 128, packed_rows(width, ff)[1]
    return bool(rest) and (2 * first - width) * rest >= -(-width // rest) * rest


def pack_slots(rows, out, names=None):
    width, ff = rows.shape
    full, rest = ff // 128, ff % 128
    for c in range(full):
        out[c * width : (c + 1) * width, :] = rows[:, c * 128 : (c + 1) * 128].astype(BF16)
    if rest:
        end, first = packed_rows(width, ff)
        tail = rows[:, full * 128 :]
        right = tail[first:]
        if right.shape[0] < first:
            spare = jnp.zeros((first - right.shape[0], rest), F32)
            if names is not None:
                spare = lines_of(names, spare)
            right = jnp.concatenate([right, spare], axis=0)
        pair = jnp.concatenate([tail[:first], right], axis=1)
        out[full * width : end, :] = pair.astype(BF16)


def unpack_slots(ref, width, ff):
    full, rest = ff // 128, ff % 128
    blocks = [ref[c * width : (c + 1) * width, :].astype(F32) for c in range(full)]
    if rest:
        end, first = packed_rows(width, ff)
        pair = ref[full * width : end, :].astype(F32)
        blocks.append(
            jnp.concatenate([pair[:, :rest], pair[: width - first, rest:]], axis=0)
        )
    return jnp.concatenate(blocks, axis=1)


def picks_of(meta, me, dims):
    experts, local, cap, width = dims
    top = meta.shape[0] // 2
    slots = token_slots(meta[:top], me, experts, local, cap, width)
    rows = iota((experts // local * width, meta.shape[1]), 0)
    picks = jnp.concatenate([ones_where(rows == slot) for slot in slots], axis=1)
    return picks, meta[top:].astype(F32) * (1.0 / 65536.0)


def dispatch_kernel(dims, place, meta_ref, hid_ref, *outs):
    width = dims[3]
    picks, gate = picks_of(meta_ref[...], place[0], dims)
    scaled = [
        (hid_ref[k].astype(F32) * gate[k : k + 1, :]).astype(BF16)
        for k in range(hid_ref.shape[0])
    ]
    sent = dot(picks, jnp.concatenate(scaled, axis=1), NT)
    tokens = hid_ref.shape[2]
    number = lax.rem(iota((8, picks.shape[1]), 1), tokens) + 1
    number = number.astype(F32).astype(BF16)
    for s, out in enumerate(outs):
        at = slice(s * width, (s + 1) * width)
        names = dot(number, picks[at], NT)[:1]
        if spare_fits(width, sent.shape[1]):
            pack_slots(sent[at], out, names)
        else:
            pack_slots(sent[at], out)
            lines = lines_of(names, jnp.zeros((16, 128), F32))
            out[out.shape[0] - 16 :, :] = lines.astype(BF16)


def names_kernel(ids_ref, out):
    top, tokens = ids_ref.shape
    ids = ids_ref[...].astype(F32)
    spare = jnp.zeros((out.shape[0] - top, tokens), F32)
    out[...] = jnp.concatenate([ids, spare], axis=0).astype(BF16)


def pack_kernel(dy_ref, names_ref, out):
    tokens, half = dy_ref.shape
    for c in range(half // 128):
        out[c * tokens : (c + 1) * tokens, :] = dy_ref[:, c * 128 : (c + 1) * 128]
    out[half // 128 * tokens :, :] = names_ref[...]


def by_expert(rows, local, cap):
    return [
        jnp.concatenate([r[l * cap : (l + 1) * cap] for r in rows], axis=0)
        for l in range(local)
    ]


def by_source(rows, count, cap):
    return [
        jnp.concatenate([r[s * cap : (s + 1) * cap] for r in rows], axis=0)
        for s in range(count)
    ]


def gather_kernel(dims, top, tokens, place, *refs):
    experts, local, cap, width = dims
    n = experts // local
    own, other, x_ref = refs[:n], refs[n:-1], refs[-1]
    half = x_ref.shape[2] // 2
    chunk = min(half, 512)
    held = []
    for ref in own:
        ids = ref[half // 128 * tokens :, :].astype(F32).astype(jnp.int32)[:top]
        held.append(
            jnp.concatenate(slots_by_lane(ids, place[0], local, cap, width), axis=0)
        )

    def features(ref, start):
        blocks = range(start // 128, (start + chunk) // 128)
        return jnp.concatenate([ref[c * tokens : (c + 1) * tokens, :] for c in blocks], axis=1)

    for side, halves in ((place[1], own), (1 - place[1], other)):
        for c in range(0, half, chunk):
            rows = [dot(h, features(ref, c), NN) for h, ref in zip(held, halves)]
            at = pl.ds(pl.multiple_of(side * half + c, chunk), chunk)
            for l, x in enumerate(by_expert(rows, local, cap)):
                x_ref[l, :, at] = x.astype(BF16)


def grad_kernel(dims, x_ref, w_ref, *outs):
    experts, local, cap, width = dims
    grads = [dot(x_ref[l], w_ref[l], NT) for l in range(local)]
    for s, rows in enumerate(by_source(grads, len(outs), cap)):
        pack_slots(rows, outs[s])


def mix_rows(dims, side, hid, w_ref, tokens, half, store):
    experts, local, cap, width = dims
    n = len(hid)
    ff = w_ref.shape[1]
    chunk = min(half, 256)
    held, rows = [], []
    for h in hid:
        if spare_fits(width, ff):
            end, first = packed_rows(width, ff)
            lines = h[end - first : end, :].astype(F32)[width - first :, ff % 128 :]
        else:
            lines = h[h.shape[0] - 16 :, :].astype(F32)
        lanes = lines.shape[1]
        names = [
            lines[i // lanes : i // lanes + 1, : min(lanes, width - i)]
            for i in range(0, width, lanes)
        ]
        names = jnp.concatenate(names, axis=1)
        held.append(ones_where(iota((tokens, width), 0) == names.astype(jnp.int32) - 1))
        rows.append(unpack_slots(h, width, ff))
    x = [r.astype(BF16) for r in by_expert(rows, local, cap)]
    for c in range(0, half, chunk):
        at = pl.ds(pl.multiple_of(side * half + c, chunk), chunk)
        out = [dot(x[l], w_ref[l, :, at], NN) for l in range(local)]
        for s, rows in enumerate(by_source(out, n, cap)):
            store(s, slice(c, c + chunk), dot(held[s], rows.astype(BF16), NN))


def mix_kernel(dims, sibling, place, *refs):
    hid, (w_ref, out) = refs[:-2], refs[-2:]
    tokens = out.shape[0] // len(hid)

    def store(s, columns, part):
        out[pl.ds(s * tokens, tokens), columns] = part.astype(out.dtype)

    side = 1 - place[1] if sibling else place[1]
    mix_rows(dims, side, hid, w_ref, tokens, out.shape[1], store)


def mix_add_kernel(dims, place, *refs):
    n = (len(refs) - 2) // 2
    hid, (w_ref, arrived), outs = refs[:n], refs[n : n + 2], refs[n + 2 :]
    tokens, half = outs[0].shape

    def store(s, columns, part):
        theirs = arrived[pl.ds(s * tokens, tokens), columns].astype(F32)
        outs[s][:, columns] = (part + theirs).astype(BF16)

    mix_rows(dims, place[1], hid, w_ref, tokens, half, store)


def add_split_kernel(own, arrived, mine, one_low, one_high, two_low, two_high, low, high):
    tokens, half = mine.shape
    cut = half // 2
    parts = []
    for s in range(4):
        at = pl.ds(s * tokens, tokens)
        parts.append(own[at, :] + arrived[at, :].astype(F32))
    mine[...] = parts[0]
    one_low[...] = parts[1][:, :cut].astype(BF16)
    one_high[...] = parts[1][:, cut:]
    two_low[...] = parts[2][:, :cut]
    two_high[...] = parts[2][:, cut:].astype(BF16)
    low[...] = parts[3][:, :cut].astype(BF16)
    high[...] = parts[3][:, cut:].astype(BF16)


def join_kernel(one_high, two_low, low, high, to_one, to_two):
    to_one[...] = (one_high[...] + high[...].astype(F32)).astype(BF16)
    to_two[...] = (two_low[...] + low[...].astype(F32)).astype(BF16)


def finish_kernel(mine, one_low, one_high, two_low, two_high, out):
    cut = one_low.shape[1]
    for at, one, two in ((0, one_low, two_low), (cut, one_high, two_high)):
        total = mine[:, at : at + cut] + one[...].astype(F32) + two[...].astype(F32)
        out[:, at : at + cut] = total.astype(BF16)


def restore_kernel(dims, place, meta_ref, *refs):
    back_refs, out = refs[:-1], refs[-1]
    top, _, tokens = out.shape
    picks, gate = picks_of(meta_ref[...], place[0], dims)
    ff = out.shape[1]
    back = [unpack_slots(ref, dims[3], ff).astype(BF16) for ref in back_refs]
    back = jnp.concatenate(back, axis=0)
    grads = dot(back, picks, TN)
    for k in range(top):
        out[k] = (grads[:, k * tokens : (k + 1) * tokens] * gate[k : k + 1, :]).astype(BF16)


def shaped(shape, dtype=BF16):
    return jax.ShapeDtypeStruct(shape, dtype)


def call(kernel, outs, args, where=(), scratch=(), grant=24, weight=1, name=None):
    where = dict(where)
    return pl.pallas_call(
        kernel,
        out_shape=outs,
        in_specs=[
            pl.BlockSpec(memory_space=where.get(i, pltpu.VMEM)) for i in range(len(args))
        ],
        out_specs=[pl.BlockSpec(memory_space=pltpu.VMEM)] * len(outs),
        scratch_shapes=scratch,
        compiler_params=pltpu.CompilerParams(vmem_limit_bytes=grant * 1024 * 1024),
        cost_estimate=pl.CostEstimate(
            flops=weight, bytes_accessed=1, transcendentals=0
        ),
        name=name,
    )(*args)


def body(hidden, expert_ids, gate_fix, grad_out, w_down):
    tokens, top, ff = hidden.shape
    half = grad_out.shape[1]
    local, _, full = w_down.shape
    n = lax.axis_size("ctx")
    experts = n * local
    assigned = tokens * top
    cap = min(tokens, assigned // experts + max(1, assigned // (8 * experts)))
    unit = 8 if local % 2 == 0 else 16
    cap = -(-cap // unit) * unit
    width = local * cap
    dims = (experts, local, cap, width)
    run = functools.partial(call, grant=24 if n <= 4 else 56)
    place = jnp.stack([lax.axis_index("ctx"), lax.axis_index("tp")]).astype(jnp.int32)
    placed = {0: pltpu.SMEM}

    def send(x, s):
        return lax.ppermute(x, "ctx", [(i, i ^ s) for i in range(n)]) if s else x

    def swap(x):
        return lax.ppermute(x, "tp", [(0, 1), (1, 0)])

    meta = jnp.concatenate([expert_ids.T, gate_fix.T], axis=0)
    hid_t = hidden.transpose(1, 2, 0)
    (names,) = run(
        names_kernel, [shaped((16, tokens))], [expert_ids.T], name="names", weight=10**9
    )
    (packed,) = run(
        pack_kernel, [shaped((half // 128 * tokens + 16, 128))], [grad_out, names], name="pack"
    )
    forward = n == 4
    own = [send(packed, s) for s in range(n)]
    tail = 0 if spare_fits(width, ff) else 16
    hid_sent = run(
        functools.partial(dispatch_kernel, dims), [shaped((packed_rows(width, ff)[0] + tail, 128))] * n,
        [place, meta, hid_t], where=placed, name="dispatch",
    )
    hid = [send(hid_sent[s], s) for s in range(n)]
    slot = shaped((packed_rows(width, ff)[0], 128))

    def swaps(xs):
        return [swap(x) for x in xs]

    def swaps_in_turn(xs):
        first = swap(xs[0])
        second, first = lax.optimization_barrier((xs[1], first))
        return [first, swap(second)]

    if forward:
        always = place[0] < 1000
        last, mine = lax.cond(always, swaps_in_turn, list, [own[3], own[0]])
        *own[1:3], last = lax.optimization_barrier((*own[1:3], last))
        other = [mine] + lax.cond(always, swaps, list, own[1:3]) + [last]
    else:
        other = swaps(own)
    (x,) = run(
        functools.partial(gather_kernel, dims, top, tokens), [shaped((local, n * cap, full))],
        [place, *own, *other], where=placed, name="gather", weight=20 * 10**8,
    )
    grad_sent = run(
        functools.partial(grad_kernel, dims), [slot] * n, [x, w_down], name="grad"
    )
    hid[0], grad_own = lax.optimization_barrier((hid[0], grad_sent[0]))
    grad_back = [grad_own] + [send(grad_sent[s], s) for s in range(1, n)]

    mixing = dict(where=placed)
    (theirs,) = run(
        functools.partial(mix_kernel, dims, True), [shaped((n * tokens, half))],
        [place, *hid, w_down], name="mix_sibling", **mixing,
    )
    arrived = swap(theirs)
    if forward:
        (mine,) = run(
            functools.partial(mix_kernel, dims, False), [shaped((n * tokens, half), F32)],
            [place, *hid, w_down], name="mix_own", weight=BIG, **mixing,
        )
        cut = half // 2
        kept, wide = shaped((tokens, half), F32), shaped((tokens, cut), F32)
        piece = shaped((tokens, cut))
        kept, one_low, one_high, two_low, two_high, low, high = run(
            add_split_kernel, [kept, piece, wide, wide, piece, piece, piece],
            [mine, arrived], name="add",
        )
        low, high = send(low, 1), send(high, 2)
        one_low, two_high, *grad_back[1:3] = lax.optimization_barrier(
            (one_low, two_high, *grad_back[1:3])
        )
        one_low, two_high = send(one_low, 1), send(two_high, 2)
        to_one, to_two = run(
            join_kernel, [piece] * 2, [one_high, two_low, low, high], name="join"
        )
        (mixed,) = run(
            finish_kernel, [shaped((tokens, half))],
            [kept, one_low, send(to_one, 1), send(to_two, 2), two_high], name="finish",
        )
    else:
        sums = run(
            functools.partial(mix_add_kernel, dims), [shaped((tokens, half))] * n,
            [place, *hid, w_down, arrived], name="mix_own", **mixing,
        )
        mixed = sum(send(sums[s], s).astype(F32) for s in range(n)).astype(BF16)

    (grad_t,) = run(
        functools.partial(restore_kernel, dims), [shaped((top, ff, tokens))],
        [place, meta, *grad_back], where=placed, name="restore", weight=BIG,
    )
    return mixed, grad_t.transpose(2, 0, 1)


def solution(mesh):
    placed = (
        P(("ctx", "exp"), None, "tp"),
        P(("ctx", "exp"), None),
        P(("ctx", "exp"), None),
        P(("ctx", "exp"), "tp"),
        P("ctx", "tp", None),
    )
    return jax.shard_map(
        body,
        mesh=mesh,
        in_specs=placed,
        out_specs=(P(("ctx", "exp"), "tp"), P(("ctx", "exp"), None, "tp")),
        check_vma=False,
    )
```

```python
import functools

import jax
import jax.numpy as jnp
from jax import lax
from jax.experimental import pallas as pl
from jax.experimental.pallas import tpu as pltpu
from jax.sharding import PartitionSpec as P

BF16 = jnp.bfloat16
F32 = jnp.float32
NN = (((1,), (0,)), ((), ()))
NT = (((1,), (1,)), ((), ()))
TN = (((0,), (0,)), ((), ()))
BIG = 10**11


def dot(a, b, dims):
    return lax.dot_general(a, b, dims, preferred_element_type=F32)


def iota(shape, axis):
    return lax.broadcasted_iota(jnp.int32, shape, axis)


def ones_where(mask):
    return mask.astype(F32).astype(BF16)


def earlier(tokens):
    return ones_where(iota((tokens, tokens), 0) < iota((tokens, tokens), 1))


def token_slots(ids, me, experts, local, cap, width):
    top, tokens = ids.shape
    row = iota((experts, tokens), 0)
    hits = [ids[k : k + 1, :] == row for k in range(top)]
    named = functools.reduce(jnp.logical_or, hits)
    before = dot(ones_where(named), earlier(tokens), NN)
    base = jnp.bitwise_xor(row // local, me) * width + lax.rem(row, local) * cap
    slot = before + base.astype(F32)
    return [
        jnp.sum(jnp.where(hit, slot, 0.0), axis=0, keepdims=True).astype(jnp.int32)
        for hit in hits
    ]


def named_here(ids, me, local):
    top, tokens = ids.shape
    row = iota((8, tokens), 0) + me * local
    return functools.reduce(
        jnp.logical_or, [ids[k : k + 1, :] == row for k in range(top)]
    )


def slots_by_lane(ids, me, local, cap, width):
    tokens = ids.shape[1]
    named = named_here(ids, me, local)
    before = dot(ones_where(named), earlier(tokens), NN)
    slot = before.astype(jnp.int32) + iota((8, tokens), 0) * cap
    slot = jnp.where(named, slot, -1)
    rows = iota((cap, tokens), 0)
    return [ones_where(rows + l * cap == slot[l : l + 1, :]) for l in range(local)]


def packed_rows(width, ff):
    first = -(-(width // 2) // 16) * 16
    return ff // 128 * width + (first if ff % 128 else 0), first


def lines_of(names, lines):
    width, lanes = names.shape[1], lines.shape[1]
    if width % lanes:
        names = jnp.concatenate([names, jnp.zeros((1, -width % lanes), F32)], axis=1)
    for i in range(names.shape[1] // lanes):
        line = names[:, i * lanes : (i + 1) * lanes]
        lines = jnp.where(iota(lines.shape, 0) == i, line, lines)
    return lines


def spare_fits(width, ff):
    rest, first = ff % 128, packed_rows(width, ff)[1]
    return bool(rest) and (2 * first - width) * rest >= -(-width // rest) * rest


def pack_slots(rows, out, names=None):
    width, ff = rows.shape
    full, rest = ff // 128, ff % 128
    for c in range(full):
        out[c * width : (c + 1) * width, :] = rows[:, c * 128 : (c + 1) * 128].astype(BF16)
    if rest:
        end, first = packed_rows(width, ff)
        tail = rows[:, full * 128 :]
        right = tail[first:]
        if right.shape[0] < first:
            spare = jnp.zeros((first - right.shape[0], rest), F32)
            if names is not None:
                spare = lines_of(names, spare)
            right = jnp.concatenate([right, spare], axis=0)
        pair = jnp.concatenate([tail[:first], right], axis=1)
        out[full * width : end, :] = pair.astype(BF16)


def unpack_slots(ref, width, ff):
    full, rest = ff // 128, ff % 128
    blocks = [ref[c * width : (c + 1) * width, :].astype(F32) for c in range(full)]
    if rest:
        end, first = packed_rows(width, ff)
        pair = ref[full * width : end, :].astype(F32)
        blocks.append(
            jnp.concatenate([pair[:, :rest], pair[: width - first, rest:]], axis=0)
        )
    return jnp.concatenate(blocks, axis=1)


def picks_of(meta, me, dims):
    experts, local, cap, width = dims
    top = meta.shape[0] // 2
    slots = token_slots(meta[:top], me, experts, local, cap, width)
    rows = iota((experts // local * width, meta.shape[1]), 0)
    picks = jnp.concatenate([ones_where(rows == slot) for slot in slots], axis=1)
    return picks, meta[top:].astype(F32) * (1.0 / 65536.0)


def dispatch_kernel(dims, place, meta_ref, hid_ref, *outs):
    width = dims[3]
    picks, gate = picks_of(meta_ref[...], place[0], dims)
    scaled = [
        (hid_ref[k].astype(F32) * gate[k : k + 1, :]).astype(BF16)
        for k in range(hid_ref.shape[0])
    ]
    sent = dot(picks, jnp.concatenate(scaled, axis=1), NT)
    tokens = hid_ref.shape[2]
    number = lax.rem(iota((8, picks.shape[1]), 1), tokens) + 1
    number = number.astype(F32).astype(BF16)
    for s, out in enumerate(outs):
        at = slice(s * width, (s + 1) * width)
        names = dot(number, picks[at], NT)[:1]
        if spare_fits(width, sent.shape[1]):
            pack_slots(sent[at], out, names)
        else:
            pack_slots(sent[at], out)
            lines = lines_of(names, jnp.zeros((16, 128), F32))
            out[out.shape[0] - 16 :, :] = lines.astype(BF16)


def names_kernel(ids_ref, out):
    top, tokens = ids_ref.shape
    ids = ids_ref[...].astype(F32)
    spare = jnp.zeros((out.shape[0] - top, tokens), F32)
    out[...] = jnp.concatenate([ids, spare], axis=0).astype(BF16)


def pack_kernel(dy_ref, names_ref, out):
    tokens, half = dy_ref.shape
    for c in range(half // 128):
        out[c * tokens : (c + 1) * tokens, :] = dy_ref[:, c * 128 : (c + 1) * 128]
    out[half // 128 * tokens :, :] = names_ref[...]


def by_expert(rows, local, cap):
    return [
        jnp.concatenate([r[l * cap : (l + 1) * cap] for r in rows], axis=0)
        for l in range(local)
    ]


def by_source(rows, count, cap):
    return [
        jnp.concatenate([r[s * cap : (s + 1) * cap] for r in rows], axis=0)
        for s in range(count)
    ]


def gather_kernel(dims, top, tokens, place, *refs):
    experts, local, cap, width = dims
    n = experts // local
    own, other, x_ref = refs[:n], refs[n:-1], refs[-1]
    half = x_ref.shape[2] // 2
    chunk = min(half, 512)
    held = []
    for ref in own:
        ids = ref[half // 128 * tokens :, :].astype(F32).astype(jnp.int32)[:top]
        held.append(
            jnp.concatenate(slots_by_lane(ids, place[0], local, cap, width), axis=0)
        )

    def features(ref, start):
        blocks = range(start // 128, (start + chunk) // 128)
        return jnp.concatenate([ref[c * tokens : (c + 1) * tokens, :] for c in blocks], axis=1)

    for side, halves in ((place[1], own), (1 - place[1], other)):
        for c in range(0, half, chunk):
            rows = [dot(h, features(ref, c), NN) for h, ref in zip(held, halves)]
            at = pl.ds(pl.multiple_of(side * half + c, chunk), chunk)
            for l, x in enumerate(by_expert(rows, local, cap)):
                x_ref[l, :, at] = x.astype(BF16)


def grad_kernel(dims, x_ref, w_ref, *outs):
    experts, local, cap, width = dims
    grads = [dot(x_ref[l], w_ref[l], NT) for l in range(local)]
    for s, rows in enumerate(by_source(grads, len(outs), cap)):
        pack_slots(rows, outs[s])


def mix_rows(dims, side, hid, w_ref, tokens, half, store):
    experts, local, cap, width = dims
    n = len(hid)
    ff = w_ref.shape[1]
    chunk = min(half, 256)
    held, rows = [], []
    for h in hid:
        if spare_fits(width, ff):
            end, first = packed_rows(width, ff)
            lines = h[end - first : end, :].astype(F32)[width - first :, ff % 128 :]
        else:
            lines = h[h.shape[0] - 16 :, :].astype(F32)
        lanes = lines.shape[1]
        names = [
            lines[i // lanes : i // lanes + 1, : min(lanes, width - i)]
            for i in range(0, width, lanes)
        ]
        names = jnp.concatenate(names, axis=1)
        held.append(ones_where(iota((tokens, width), 0) == names.astype(jnp.int32) - 1))
        rows.append(unpack_slots(h, width, ff))
    x = [r.astype(BF16) for r in by_expert(rows, local, cap)]
    for c in range(0, half, chunk):
        at = pl.ds(pl.multiple_of(side * half + c, chunk), chunk)
        out = [dot(x[l], w_ref[l, :, at], NN) for l in range(local)]
        for s, rows in enumerate(by_source(out, n, cap)):
            store(s, slice(c, c + chunk), dot(held[s], rows.astype(BF16), NN))


def mix_kernel(dims, sibling, place, *refs):
    hid, (w_ref, out) = refs[:-2], refs[-2:]
    tokens = out.shape[0] // len(hid)

    def store(s, columns, part):
        out[pl.ds(s * tokens, tokens), columns] = part.astype(out.dtype)

    side = 1 - place[1] if sibling else place[1]
    mix_rows(dims, side, hid, w_ref, tokens, out.shape[1], store)


def mix_add_kernel(dims, place, *refs):
    n = (len(refs) - 2) // 2
    hid, (w_ref, arrived), outs = refs[:n], refs[n : n + 2], refs[n + 2 :]
    tokens, half = outs[0].shape

    def store(s, columns, part):
        theirs = arrived[pl.ds(s * tokens, tokens), columns].astype(F32)
        outs[s][:, columns] = (part + theirs).astype(BF16)

    mix_rows(dims, place[1], hid, w_ref, tokens, half, store)


def add_split_kernel(own, arrived, mine, one_low, one_high, two_low, two_high, low, high):
    tokens, half = mine.shape
    cut = half // 2
    parts = []
    for s in range(4):
        at = pl.ds(s * tokens, tokens)
        parts.append(own[at, :] + arrived[at, :].astype(F32))
    mine[...] = parts[0]
    one_low[...] = parts[1][:, :cut].astype(BF16)
    one_high[...] = parts[1][:, cut:]
    two_low[...] = parts[2][:, :cut]
    two_high[...] = parts[2][:, cut:].astype(BF16)
    low[...] = parts[3][:, :cut].astype(BF16)
    high[...] = parts[3][:, cut:].astype(BF16)


def join_kernel(high, low, one_high, two_low, to_one, to_two):
    to_one[...] = (one_high[...] + high[...].astype(F32)).astype(BF16)
    to_two[...] = (two_low[...] + low[...].astype(F32)).astype(BF16)


def finish_kernel(two_high, two_low, one_low, one_high, mine, out):
    cut = one_low.shape[1]
    for at, one, two in ((0, one_low, two_low), (cut, one_high, two_high)):
        total = mine[:, at : at + cut] + one[...].astype(F32) + two[...].astype(F32)
        out[:, at : at + cut] = total.astype(BF16)


def restore_kernel(dims, place, meta_ref, *refs):
    back_refs, out = refs[:-1], refs[-1]
    top, _, tokens = out.shape
    picks, gate = picks_of(meta_ref[...], place[0], dims)
    ff = out.shape[1]
    back = [unpack_slots(ref, dims[3], ff).astype(BF16) for ref in back_refs]
    back = jnp.concatenate(back, axis=0)
    grads = dot(back, picks, TN)
    for k in range(top):
        out[k] = (grads[:, k * tokens : (k + 1) * tokens] * gate[k : k + 1, :]).astype(BF16)


def shaped(shape, dtype=BF16):
    return jax.ShapeDtypeStruct(shape, dtype)


def call(kernel, outs, args, where=(), scratch=(), grant=24, weight=1, name=None):
    where = dict(where)
    return pl.pallas_call(
        kernel,
        out_shape=outs,
        in_specs=[
            pl.BlockSpec(memory_space=where.get(i, pltpu.VMEM)) for i in range(len(args))
        ],
        out_specs=[pl.BlockSpec(memory_space=pltpu.VMEM)] * len(outs),
        scratch_shapes=scratch,
        compiler_params=pltpu.CompilerParams(vmem_limit_bytes=grant * 1024 * 1024),
        cost_estimate=pl.CostEstimate(
            flops=weight, bytes_accessed=1, transcendentals=0
        ),
        name=name,
    )(*args)


def body(hidden, expert_ids, gate_fix, grad_out, w_down):
    tokens, top, ff = hidden.shape
    half = grad_out.shape[1]
    local, _, full = w_down.shape
    n = lax.axis_size("ctx")
    experts = n * local
    assigned = tokens * top
    cap = min(tokens, assigned // experts + max(1, assigned // (8 * experts)))
    unit = 8 if local % 2 == 0 else 16
    cap = -(-cap // unit) * unit
    width = local * cap
    dims = (experts, local, cap, width)
    run = functools.partial(call, grant=24 if n <= 4 else 56)
    place = jnp.stack([lax.axis_index("ctx"), lax.axis_index("tp")]).astype(jnp.int32)
    placed = {0: pltpu.SMEM}

    def send(x, s):
        return lax.ppermute(x, "ctx", [(i, i ^ s) for i in range(n)]) if s else x

    def swap(x):
        return lax.ppermute(x, "tp", [(0, 1), (1, 0)])

    meta = jnp.concatenate([expert_ids.T, gate_fix.T], axis=0)
    hid_t = hidden.transpose(1, 2, 0)
    (names,) = run(
        names_kernel, [shaped((16, tokens))], [expert_ids.T], name="names", weight=10**9
    )
    (packed,) = run(
        pack_kernel, [shaped((half // 128 * tokens + 16, 128))], [grad_out, names], name="pack"
    )
    forward = n == 4
    own = [send(packed, s) for s in range(n)]
    tail = 0 if spare_fits(width, ff) else 16
    hid_sent = run(
        functools.partial(dispatch_kernel, dims), [shaped((packed_rows(width, ff)[0] + tail, 128))] * n,
        [place, meta, hid_t], where=placed, name="dispatch",
    )
    hid = [send(hid_sent[s], s) for s in range(n)]
    slot = shaped((packed_rows(width, ff)[0], 128))

    def swaps(xs):
        return [swap(x) for x in xs]

    def swaps_in_turn(xs):
        first = swap(xs[0])
        second, first = lax.optimization_barrier((xs[1], first))
        return [first, swap(second)]

    if forward:
        always = place[0] < 1000
        last, mine = lax.cond(always, swaps_in_turn, list, [own[3], own[0]])
        *own[1:3], last = lax.optimization_barrier((*own[1:3], last))
        other = [mine] + lax.cond(always, swaps, list, own[1:3]) + [last]
    else:
        other = swaps(own)
    (x,) = run(
        functools.partial(gather_kernel, dims, top, tokens), [shaped((local, n * cap, full))],
        [place, *own, *other], where=placed, name="gather", weight=20 * 10**8,
    )
    grad_sent = run(
        functools.partial(grad_kernel, dims), [slot] * n, [x, w_down], name="grad"
    )
    hid[0], grad_own = lax.optimization_barrier((hid[0], grad_sent[0]))
    grad_back = [grad_own] + [send(grad_sent[s], s) for s in range(1, n)]

    mixing = dict(where=placed)
    (theirs,) = run(
        functools.partial(mix_kernel, dims, True), [shaped((n * tokens, half))],
        [place, *hid, w_down], name="mix_sibling", **mixing,
    )
    arrived = swap(theirs)
    if forward:
        (mine,) = run(
            functools.partial(mix_kernel, dims, False), [shaped((n * tokens, half), F32)],
            [place, *hid, w_down], name="mix_own", weight=BIG, **mixing,
        )
        cut = half // 2
        kept, wide = shaped((tokens, half), F32), shaped((tokens, cut), F32)
        piece = shaped((tokens, cut))
        kept, one_low, one_high, two_low, two_high, low, high = run(
            add_split_kernel, [kept, piece, wide, wide, piece, piece, piece],
            [mine, arrived], name="add",
        )
        high, low = send(high, 2), send(low, 1)
        one_low, two_high, *grad_back[1:3] = lax.optimization_barrier(
            (one_low, two_high, *grad_back[1:3])
        )
        two_high, one_low = send(two_high, 2), send(one_low, 1)
        to_one, to_two = run(
            join_kernel, [piece] * 2, [high, low, one_high, two_low], name="join"
        )
        to_two, to_one = send(to_two, 2), send(to_one, 1)
        (mixed,) = run(
            finish_kernel, [shaped((tokens, half))],
            [two_high, to_two, one_low, to_one, kept], name="finish",
        )
    else:
        sums = run(
            functools.partial(mix_add_kernel, dims), [shaped((tokens, half))] * n,
            [place, *hid, w_down, arrived], name="mix_own", **mixing,
        )
        mixed = sum(send(sums[s], s).astype(F32) for s in range(n)).astype(BF16)

    (grad_t,) = run(
        functools.partial(restore_kernel, dims), [shaped((top, ff, tokens))],
        [place, meta, *grad_back], where=placed, name="restore", weight=BIG,
    )
    return mixed, grad_t.transpose(2, 0, 1)


def solution(mesh):
    placed = (
        P(("ctx", "exp"), None, "tp"),
        P(("ctx", "exp"), None),
        P(("ctx", "exp"), None),
        P(("ctx", "exp"), "tp"),
        P("ctx", "tp", None),
    )
    return jax.shard_map(
        body,
        mesh=mesh,
        in_specs=placed,
        out_specs=(P(("ctx", "exp"), "tp"), P(("ctx", "exp"), None, "tp")),
        check_vma=False,
    )
```
